32 devices in a mesh: clip: 8 (over z, y), win: 4 (over x, core).
Axes of the slice: x: 2, y: 2, z: 4, core: 2. Of those that a mesh axis runs over, the one named last changes fastest.
Arguments:
- tokens: bfloat16 [8, 10, 2, 8, 16, 1024], P('clip', None, None, 'win'), may hold values from -6 to 6
- condition: float32 [8, 1024], P('clip'), may hold values from -6 to 6
- frame_count: int32 [8], P('clip'), may hold values from 2 to 9, as said below
- triple_weight: bfloat16 [1024, 3072], P('clip'), may hold values from -0.1875 to 0.1875
- triple_bias: bfloat16 [2048], P('clip'), may hold values from -3 to 3
- project_weight: bfloat16 [1024, 1024], P('clip'), may hold values from -0.75 to 0.75
- project_bias: bfloat16 [1024], P('clip'), may hold values from -3 to 3
- up_weight: bfloat16 [1024, 4096], P('clip'), may hold values from -0.1875 to 0.1875
- up_bias: bfloat16 [4096], P('clip'), may hold values from -3 to 3
- down_weight: bfloat16 [4096, 1024], P('clip'), may hold values from -0.09375 to 0.09375
- down_bias: bfloat16 [1024], P('clip'), may hold values from -3 to 3
- modulate_weight: bfloat16 [1024, 6144], P('clip'), may hold values from -0.1875 to 0.1875
- modulate_bias: bfloat16 [6144], P('clip'), may hold values from -3 to 3
- position_table: float32 [16, 2025], replicated, may hold values from -3 to 3
- cotangent: bfloat16 [8, 10, 2, 8, 16, 1024], P('clip', None, None, 'win'), may hold values from -6 to 6
Outputs:
- output: bfloat16 [8, 10, 2, 8, 16, 1024], P('clip', None, None, 'win')
- input_grad: bfloat16 [8, 10, 2, 8, 16, 1024], P('clip', None, None, 'win')
- condition_grad: float32 [8, 1024], P('clip')
- triple_weight_grad: float32 [1024, 3072], P('clip')
- triple_bias_grad: float32 [2048], P('clip')
- project_weight_grad: float32 [1024, 1024], P('clip')
- project_bias_grad: float32 [1024], P('clip')
- up_weight_grad: float32 [1024, 4096], P('clip')
- up_bias_grad: float32 [4096], P('clip')
- down_weight_grad: float32 [4096, 1024], P('clip')
- down_bias_grad: float32 [1024], P('clip')
- modulate_weight_grad: float32 [1024, 6144], P('clip')
- modulate_bias_grad: float32 [6144], P('clip')
- position_table_grad: float32 [16, 2025], replicated
The draws below stay inside these ranges and needn't reach their ends.
Inputs may be any that keep to these rules, and one draw needn't show every extreme that they name: Frames of clip c from frame_count[c] on are padding; a clip with at most 5 given frames has only padding in its later windows.
All inputs are finite; a program needn't handle non-finite values.
Results may differ from the reference program's by a relative error of at most 0.018.
The reference program's roundings to bfloat16 on the way count: a program that leaves them out, or rounds other values in their place, can miss the bound.
Values may be sent and summed in bfloat16 or wider, within the bound.
No kernel may reach another device: no remote copies, remote signals or barrier semaphores. Data moves between devices by JAX's collectives and lax.ppermute only.
A program may use at most 320 MiB of HBM per device.

```python
from functools import partial
import jax
import jax.numpy as jnp
from jax import lax

D = 1024
HEADS = 16
FF = 4096
SIDE = 16
FRAMES = 10
WIN_T = 5
WIN_S = 8
CLIPS = 8
RELS = 2025


def draw_frame_count(key, part):
    draws = jax.random.randint(key, (CLIPS,), 0, 128)
    marks = jnp.array([96, 64, 48, 32, 16, 8, 2], jnp.int32)
    counts = 2 + jnp.sum((draws[:, None] < marks[None, :]).astype(jnp.int32), axis=1)
    longest = jax.random.randint(jax.random.fold_in(key, 1), (), 0, CLIPS)
    shortest = (longest + 1 + jax.random.randint(jax.random.fold_in(key, 2), (), 0, CLIPS - 1)) % CLIPS
    place = jnp.arange(CLIPS)
    counts = jnp.where(place == longest, FRAMES - 1, counts)
    counts = jnp.where(place == shortest, 2, counts)
    return counts.astype(jnp.int32)


def block_levels(rng, shape, split, least, largest):
    gain = 1.0
    for dim, parts in split:
        heights = jax.random.uniform(jax.random.fold_in(jax.random.fold_in(rng, 6), dim), (parts,), jnp.float32, least / len(split), largest / len(split))
        gain = gain * jnp.repeat(jnp.exp(heights), shape[dim] // parts).reshape((-1,) + (1,) * (len(shape) - 1 - dim))
    return gain


def bell_draw(own_key, extent, spread, limit, cuts=(), dtype=jnp.bfloat16):
    values = jax.random.normal(own_key, extent, jnp.float32) * spread
    if len(cuts) > 0:
        values = block_levels(own_key, extent, cuts, -0.22, 0.18) * values
    return jnp.clip(values, min=-limit, max=limit).astype(dtype)


def setup_inputs(seed: int = 0) -> dict:
    keys = jax.random.split(jax.random.key(seed), 16)
    tokens = bell_draw(keys[0], (CLIPS, FRAMES, SIDE // WIN_S, WIN_S, SIDE, D), 1.0, 6.0, ((0, 8), (3, 4)))
    condition = bell_draw(keys[1], (CLIPS, D), 1.0, 6.0, ((0, 8),), jnp.float32)
    frame_count = draw_frame_count(jax.random.fold_in(keys[15], 71), 0)
    triple_weight = bell_draw(keys[3], (D, 3 * D), D ** -0.5, 0.1875, ((0, 8),))
    triple_bias = bell_draw(keys[4], (2 * D,), 0.5, 3.0, ((0, 8),))
    project_weight = bell_draw(keys[5], (D, D), (D // 16) ** -0.5, 0.75, ((0, 8),))
    project_bias = bell_draw(keys[6], (D,), 0.5, 3.0, ((0, 8),))
    up_weight = bell_draw(keys[7], (D, FF), D ** -0.5, 0.1875, ((0, 8),))
    up_bias = bell_draw(keys[8], (FF,), 0.5, 3.0, ((0, 8),))
    down_weight = bell_draw(keys[9], (FF, D), FF ** -0.5, 0.09375, ((0, 8),))
    down_bias = bell_draw(keys[10], (D,), 0.5, 3.0, ((0, 8),))
    modulate_weight = bell_draw(keys[11], (D, 6 * D), D ** -0.5, 0.1875, ((0, 8),))
    modulate_bias = bell_draw(keys[12], (6 * D,), 0.5, 3.0, ((0, 8),))
    position_table = bell_draw(keys[13], (HEADS, RELS), 0.5, 3.0, (), jnp.float32)
    cotangent = bell_draw(keys[14], (CLIPS, FRAMES, SIDE // WIN_S, WIN_S, SIDE, D), 1.0, 6.0, ((0, 8), (3, 4)))
    return {"tokens": tokens, "condition": condition, "frame_count": frame_count, "triple_weight": triple_weight, "triple_bias": triple_bias, "project_weight": project_weight, "project_bias": project_bias, "up_weight": up_weight, "up_bias": up_bias, "down_weight": down_weight, "down_bias": down_bias, "modulate_weight": modulate_weight, "modulate_bias": modulate_bias, "position_table": position_table, "cotangent": cotangent}


@jax.custom_vjp
def low(v):
    return lax.optimization_barrier(v.astype(jnp.bfloat16)).astype(jnp.float32)

@jax.custom_vjp
def low_back(v):
    return v

def low_keep(v):
    return (low(v), None)

def low_pass(kept, grad):
    return (grad,)

def back_keep(v):
    return (v, None)

def back_low(kept, grad):
    return (low(grad),)
low.defvjp(low_keep, low_pass)
low_back.defvjp(back_keep, back_low)
highest = lax.Precision.HIGHEST
eps_norm = 1e-06
neg_fill = -30000.0

def layer_norm(values):
    center = values - lax.optimization_barrier(jnp.mean(values, axis=-1, keepdims=True))
    return center * lax.rsqrt(lax.optimization_barrier(jnp.mean(center * center, axis=-1, keepdims=True)) + eps_norm)

def offset_index():
    window_size = WIN_T * WIN_S * WIN_S
    place = jnp.arange(window_size)
    frame = place // (WIN_S * WIN_S)
    row = place // WIN_S % WIN_S
    column = place % WIN_S
    span = 2 * WIN_S - 1
    first = (frame[:, None] - frame[None, :] + WIN_T - 1) * span + row[:, None] - row[None, :] + WIN_S - 1
    return (first * span + column[:, None] - column[None, :] + WIN_S - 1).astype(jnp.int32)

def clip_block(grid, modulation, count, triple_weight, triple_bias, project_weight, project_bias, up_weight, up_bias, down_weight, down_bias, position_table):
    width = grid.shape[-1]
    heads = position_table.shape[0]
    head_dim = width // heads
    halves = SIDE // WIN_S
    periods = FRAMES // WIN_T
    windows = periods * halves * halves
    window_size = WIN_T * WIN_S * WIN_S
    cells = grid.reshape(periods, WIN_T, halves, WIN_S, halves, WIN_S, width)
    values = cells.transpose(0, 2, 4, 1, 3, 5, 6).reshape(windows, window_size, width)
    frame_of = (jnp.arange(windows) // (halves * halves))[:, None] * WIN_T + (jnp.arange(window_size) // (WIN_S * WIN_S))[None, :]
    keep = (frame_of < count).astype(jnp.float32)
    pieces = modulation.reshape(6, width)
    shift_one, scale_one, gate_one = (pieces[0], pieces[1], pieces[2])
    shift_two, scale_two, gate_two = (pieces[3], pieces[4], pieces[5])
    norm_in = low(layer_norm(values) * (1.0 + scale_one) + shift_one)
    bias_all = jnp.concatenate([triple_bias[:width], jnp.zeros((width,), jnp.float32), triple_bias[width:]])
    triple = low(low_back(jnp.dot(norm_in.reshape(-1, width), triple_weight, precision=highest) + bias_all))
    triple = triple.reshape(windows, window_size, 3, heads, head_dim)
    query, key, value = (triple[:, :, 0], triple[:, :, 1], triple[:, :, 2])
    raw = jnp.einsum('wqhd,wkhd->whqk', query, key, precision=highest) * head_dim ** (-0.5) + position_table[:, offset_index()][None]
    score = jnp.where(keep[:, None, None, :] > 0, low_back(raw), neg_fill)
    peak = lax.optimization_barrier(jnp.max(score, axis=-1, keepdims=True))
    exponent = jnp.exp(score - peak)
    prob = low(exponent / lax.optimization_barrier(jnp.sum(exponent, axis=-1, keepdims=True)))
    mixed = low(low_back(jnp.einsum('whqk,wkhd->wqhd', prob, value, precision=highest))).reshape(-1, width)
    attention = low_back(jnp.dot(mixed, project_weight, precision=highest) + project_bias).reshape(windows, window_size, width)
    middle = values + keep[..., None] * gate_one * attention
    norm_mid = low(layer_norm(middle) * (1.0 + scale_two) + shift_two)
    hidden = low_back(jnp.dot(norm_mid.reshape(-1, width), up_weight, precision=highest) + up_bias)
    activated = low(jax.nn.gelu(hidden, approximate=True))
    feedforward = low_back(jnp.dot(activated, down_weight, precision=highest) + down_bias).reshape(windows, window_size, width)
    result = middle + keep[..., None] * gate_two * feedforward
    result = result.reshape(periods, halves, halves, WIN_T, WIN_S, WIN_S, width).transpose(0, 3, 1, 4, 2, 5, 6)
    return result.reshape(grid.shape)

def forward(frame_count, tokens, condition, triple_weight, triple_bias, project_weight, project_bias, up_weight, up_bias, down_weight, down_bias, modulate_weight, modulate_bias, position_table):
    cond_in = low(condition * jax.nn.sigmoid(condition))
    modulation = low_back(jnp.dot(cond_in, modulate_weight, precision=highest) + modulate_bias)

    def one_clip(item):
        return clip_block(item[0], item[1], item[2], triple_weight, triple_bias, project_weight, project_bias, up_weight, up_bias, down_weight, down_bias, position_table)
    return lax.map(jax.checkpoint(one_clip), (tokens, modulation, frame_count))

def reference(tokens, condition, frame_count, triple_weight, triple_bias, project_weight, project_bias, up_weight, up_bias, down_weight, down_bias, modulate_weight, modulate_bias, position_table, cotangent):
    floats = (tokens, condition, triple_weight, triple_bias, project_weight, project_bias, up_weight, up_bias, down_weight, down_bias, modulate_weight, modulate_bias, position_table)
    floats = tuple((item.astype(jnp.float32) for item in floats))
    result, pullback = jax.vjp(partial(forward, frame_count), *floats)
    grads = pullback(cotangent.astype(jnp.float32))
    return (result.astype(jnp.bfloat16), grads[0].astype(jnp.bfloat16), grads[1], grads[2], grads[3], grads[4], grads[5], grads[6], grads[7], grads[8], grads[9], grads[10], grads[11], grads[12])
```

```python
import math
import jax
import jax.numpy as jnp
import numpy as np
from jax import lax
from jax.experimental import pallas as pl
from jax.experimental.pallas import tpu as pltpu
from jax.sharding import PartitionSpec as P

WIN_T = 5
WIN_S = 8
WINDOW = WIN_T * WIN_S * WIN_S
CELL = WIN_S * WIN_S
SPAN = 2 * WIN_S - 1
TSPAN = 2 * WIN_T - 1
HEAD = 64
CORES = 2
EPS = 1e-06
NEG = -30000.0
GELU_C = math.sqrt(2.0 / math.pi)
GELU_A = 0.044715
F32 = jnp.float32
BF16 = jnp.bfloat16
VMEM_LIMIT = 56 * 1024 * 1024

NN = (((1,), (0,)), ((), ()))
NT = (((1,), (1,)), ((), ()))
TN = (((0,), (0,)), ((), ()))


def mm(a, b, dims=NN):
    return lax.dot_general(a, b, dims, preferred_element_type=F32)


def any_spec():
    return pl.BlockSpec(memory_space=pl.ANY)


def params(grid_rank):
    return pltpu.CompilerParams(
        dimension_semantics=("arbitrary",) * grid_rank, vmem_limit_bytes=VMEM_LIMIT
    )


def ring_order(n):
    ny = 1 << (int(math.log2(n)) // 2)
    nz = n // ny
    if ny < 2 or nz % 2:
        return list(range(n))
    walk = []
    for z in range(nz):
        ys = list(range(1, ny))
        walk += [z * ny + y for y in (ys if z % 2 == 0 else ys[::-1])]
    return walk + [z * ny for z in reversed(range(nz))]


class Ring:
    def __init__(self, n):
        self.n = n
        order = ring_order(n)
        place = [order.index(r) for r in range(n)]
        self.order = jnp.asarray(np.array(order, np.int32))
        self.place = jnp.asarray(np.array(place, np.int32))
        self.rank = lax.axis_index("clip")
        self.pos = self.place[self.rank]
        self.up = [(order[i], order[(i + 1) % n]) for i in range(n)]
        self.down = [(b, a) for a, b in self.up]
        self.core = lax.axis_index("win") % CORES
        wins = lax.axis_size("win")
        self.swap = [(w, w ^ 1) for w in range(wins)]
        self.across = [
            [(w, w ^ k) for w in range(wins)] for k in (2 << i for i in range(8)) if k < wins
        ]
        self.pairs = [[(w, w ^ k) for w in range(wins)] for k in (1 << i for i in range(8)) if k < wins]
        self.clip_pairs = [
            (k, [(r, r ^ k) for r in range(n)]) for k in (1 << i for i in range(8)) if k < n
        ]

    def at(self, offset):
        return self.order[(self.pos + offset) % self.n]

    def steps(self, flip):
        far, near = self.n // 2, (self.n - 1) // 2
        return (near, far) if flip else (far, near)

    def index(self):
        ranks = [self.at(p) for p in range(self.n)]
        return jnp.stack(ranks + [self.core]).astype(jnp.int32)

    def gather(self, piece, flip):
        far, near = self.steps(flip)
        ahead, back = [], []
        a = b = piece
        for s in range(max(far, near)):
            if s < far:
                a = lax.ppermute(a, "clip", self.up)
                ahead.append(a)
            if s < near:
                b = lax.ppermute(b, "clip", self.down)
                back.append(b)
        own = back + ahead[::-1]
        return own, [lax.ppermute(o, "win", self.swap) for o in own]

    def scatter(self, keep, send, flip):
        far, near = self.steps(flip)
        got = lax.ppermute(send, "win", self.swap)

        def part(offset):
            r = self.at(offset)
            one = lambda arr: lax.dynamic_index_in_dim(arr, r, 0, keepdims=False).astype(F32)
            return one(keep) + one(got)

        a, b = part(far).astype(BF16), part(-near).astype(BF16)
        for s in range(max(far, near)):
            if s < far:
                a = lax.ppermute(a, "clip", self.up)
                if s < far - 1:
                    a = (a.astype(F32) + part(far - 1 - s)).astype(BF16)
            if s < near:
                b = lax.ppermute(b, "clip", self.down)
                if s < near - 1:
                    b = (b.astype(F32) + part(1 + s - near)).astype(BF16)
        total = (part(0) + a.astype(F32) + b.astype(F32)).astype(BF16)
        for perm in self.across:
            other = lax.ppermute(total, "win", perm)
            total = (total.astype(F32) + other.astype(F32)).astype(BF16)
        other = lax.ppermute(total, "win", self.swap)
        first = jnp.where(self.core == 0, total, other)
        second = jnp.where(self.core == 0, other, total)
        return first, second

    def gather_small(self, block):
        for k, perm in self.clip_pairs:
            other = lax.ppermute(block, "clip", perm)
            high = (self.rank & k) > 0
            block = jnp.where(
                high, jnp.concatenate([other, block]), jnp.concatenate([block, other])
            )
        return block

    def scatter_small(self, block):
        for k, perm in reversed(self.clip_pairs):
            high = (self.rank & k) > 0
            low_part, high_part = block[:k], block[k:]
            other = lax.ppermute(jnp.where(high, low_part, high_part), "clip", perm)
            block = jnp.where(high, high_part, low_part) + other
        return block[0]

    def sum_win(self, block):
        for perm in self.pairs:
            block = block + lax.ppermute(block, "win", perm)
        return block

    def sum_all(self, block):
        block = self.sum_win(block)
        for _, perm in self.clip_pairs:
            block = block + lax.ppermute(block, "clip", perm)
        return block


class Weight:
    def __init__(self, local, own, sib, col=0):
        self.local, self.own, self.sib, self.col = local, own, sib, col
        self.rows, self.cols = local.shape
        self.count = len(own)

    def operands(self):
        return [self.local, *self.own, *self.sib]

    def specs(self):
        return [any_spec()] * (1 + 2 * self.count)

    def shape(self):
        return (self.rows * (self.count + 1), self.cols)

    def n_sems(self):
        return 2 * self.count + 1

    def piece(self, idx, refs, dst, sems, i, base, start, width):
        half = self.rows // 2
        cols = pl.ds(start, width)
        into = pl.ds(start, width)
        if i == 0:
            rows = pl.ds(pl.multiple_of(base, self.rows), self.rows)
            return [
                pltpu.make_async_copy(refs[0].at[:, cols], dst.at[rows, into], sems.at[0])
            ]
        from_cols = pl.ds(self.col + start, width)
        core = idx[self.count + 1]
        copies = []
        for which, place in ((0, core), (1, 1 - core)):
            slot = which * self.count + i
            rows = pl.ds(pl.multiple_of(base + place * half, half), half)
            copies.append(
                pltpu.make_async_copy(
                    refs[slot].at[:, from_cols], dst.at[rows, into], sems.at[slot]
                )
            )
        return copies

    def whole(self, idx, refs, dst, sems, start=0, width=None):
        copies = []
        for i in range(self.count + 1):
            copies += self.piece(
                idx, refs, dst, sems, i, idx[i] * self.rows, start, width or self.cols
            )
        return copies


def kernel_call(body, idx, grid, in_specs, out_specs, out_shape, scratch, operands, flops, nbytes):
    return pl.pallas_call(
        body,
        grid_spec=pltpu.PrefetchScalarGridSpec(
            num_scalar_prefetch=1,
            grid=grid,
            in_specs=in_specs,
            out_specs=out_specs,
            scratch_shapes=scratch,
        ),
        out_shape=out_shape,
        compiler_params=params(len(grid)),
        cost_estimate=pl.CostEstimate(
            flops=int(flops), bytes_accessed=int(nbytes), transcendentals=0
        ),
    )(idx, *operands)


def norm_rows(v):
    center = v - jnp.mean(v, axis=-1, keepdims=True)
    inverse = lax.rsqrt(jnp.mean(center * center, axis=-1, keepdims=True) + EPS)
    return center * inverse, inverse


def norm_back(grad, normed, inverse):
    mean_grad = jnp.mean(grad, axis=-1, keepdims=True)
    mean_cross = jnp.mean(grad * normed, axis=-1, keepdims=True)
    return inverse * (grad - mean_grad - normed * mean_cross)


CHUNK = 64


def qkv_project(idx, x, mod, weight, bias):
    tokens, width = x.shape
    cols = weight.cols
    block = 512
    steps = cols // block
    rows = WINDOW
    nw = tokens // rows
    nref = weight.n_sems()

    def body(idx, x_ref, mod_ref, bias_ref, *rest):
        w_refs, rest = rest[:nref], rest[nref:]
        norm_ref, out_ref, w_buf, sems = rest
        j, w = pl.program_id(0), pl.program_id(1)

        @pl.when((j == 0) & (w == 0))
        def _():
            for s in range(steps):
                for c in weight.whole(idx, w_refs, w_buf, sems.at[s], s * block, block):
                    c.start()

            def chunk(i, _):
                r = pl.ds(pl.multiple_of(i * CHUNK, CHUNK), CHUNK)
                normed, _inv = norm_rows(x_ref[r, :].astype(F32))
                norm_ref[r, :] = (normed * (1.0 + mod_ref[1:2, :]) + mod_ref[0:1, :]).astype(BF16)
                return 0

            lax.fori_loop(0, tokens // CHUNK, chunk, 0)

        for s in range(steps):

            @pl.when((j == s) & (w == 0))
            def _():
                for c in weight.whole(idx, w_refs, w_buf, sems.at[s], s * block, block):
                    c.wait()

        a = norm_ref[pl.ds(pl.multiple_of(w * rows, rows), rows), :]
        b = w_buf[:, pl.ds(pl.multiple_of(j * block, block), block)]
        out_ref[...] = (mm(a, b) + bias_ref[...]).astype(BF16)

    return kernel_call(
        body,
        idx,
        (steps, nw),
        [
            pl.BlockSpec((tokens, width), lambda j, w, idx: (0, 0)),
            pl.BlockSpec((6, width), lambda j, w, idx: (0, 0)),
            pl.BlockSpec((1, block), lambda j, w, idx: (0, j)),
            *weight.specs(),
        ],
        [
            pl.BlockSpec((tokens, width), lambda j, w, idx: (0, 0)),
            pl.BlockSpec((rows, block), lambda j, w, idx: (w, j)),
        ],
        [
            jax.ShapeDtypeStruct((tokens, width), BF16),
            jax.ShapeDtypeStruct((tokens, cols), BF16),
        ],
        [pltpu.VMEM((width, cols), BF16), pltpu.SemaphoreType.DMA((steps, nref))],
        [x, mod, bias, *weight.operands()],
        2 * tokens * width * cols,
        2 * (tokens * (2 * width + cols) + width * cols),
    )


def bias_rows(table):
    return jnp.concatenate(
        [table[:, (WIN_T - 1 - f) * CELL : (WIN_T - 1 - f) * CELL + WINDOW] for f in range(WIN_T)],
        axis=0,
    )


def attention_specs(pairs):
    q = pl.BlockSpec((WINDOW, 2 * HEAD), lambda h, w, nv: (w, h))
    k = pl.BlockSpec((WINDOW, 2 * HEAD), lambda h, w, nv: (w, pairs + h))
    v = pl.BlockSpec((WINDOW, 2 * HEAD), lambda h, w, nv: (w, 2 * pairs + h))
    t = pl.BlockSpec((2, CELL, TSPAN * CELL), lambda h, w, nv: (h, 0, 0))
    return q, k, v, t


def attend(valid, triple, table):
    tokens = triple.shape[0]
    width = triple.shape[1] // 3
    nw = tokens // WINDOW
    pairs = width // (2 * HEAD)

    def body(nv, q_ref, k_ref, v_ref, t_ref, o_ref, l_ref):
        w = pl.program_id(1)
        keep = lax.broadcasted_iota(jnp.int32, (WINDOW, 1), 0) < nv[w] * CELL
        outs = []
        for a in range(2):
            cols = slice(a * HEAD, (a + 1) * HEAD)
            q = q_ref[:, cols] * jnp.asarray(HEAD**-0.5, BF16)
            s = mm(k_ref[:, cols], q, NT)
            s = jnp.where(keep, s + bias_rows(t_ref[a]), NEG)
            peak = jnp.max(s, axis=0, keepdims=True)
            e = jnp.exp(s - peak)
            total = jnp.sum(e, axis=0, keepdims=True)
            p = (e * (1.0 / total)).astype(BF16)
            l_ref[0, 0, a : a + 1, :] = peak + jnp.log(total)
            outs.append(mm(v_ref[:, cols], p, TN))
        o_ref[...] = jnp.concatenate(outs, axis=0).T.astype(BF16)

    q, k, v, t = attention_specs(pairs)
    return kernel_call(
        body,
        valid,
        (pairs, nw),
        [q, k, v, t],
        [
            pl.BlockSpec((WINDOW, 2 * HEAD), lambda h, w, nv: (w, h)),
            pl.BlockSpec((1, 1, 2, WINDOW), lambda h, w, nv: (w, h, 0, 0)),
        ],
        [
            jax.ShapeDtypeStruct((tokens, width), BF16),
            jax.ShapeDtypeStruct((nw, pairs, 2, WINDOW), F32),
        ],
        [],
        [triple, triple, triple, table],
        4 * tokens * WINDOW * width * 4,
        2 * tokens * 4 * width,
    )


def attend_back(valid, triple, table, grad, logs):
    tokens = triple.shape[0]
    width = triple.shape[1] // 3
    nw = tokens // WINDOW
    pairs = width // (2 * HEAD)

    def body(nv, q_ref, k_ref, v_ref, t_ref, g_ref, l_ref, dq_ref, dk_ref, dv_ref, dt_ref):
        w = pl.program_id(1)
        keep = lax.broadcasted_iota(jnp.int32, (WINDOW, 1), 0) < nv[w] * CELL
        dqs, dks, dvs = [], [], []

        @pl.when(w == 0)
        def _():
            dt_ref[...] = jnp.zeros_like(dt_ref)

        for a in range(2):
            cols = slice(a * HEAD, (a + 1) * HEAD)
            q = q_ref[:, cols] * jnp.asarray(HEAD**-0.5, BF16)
            k, g = k_ref[:, cols], g_ref[:, cols]
            s = mm(k, q, NT)
            s = jnp.where(keep, s + bias_rows(t_ref[a]), NEG)
            p = jnp.exp(s - l_ref[0, 0, a : a + 1, :])
            gp = mm(v_ref[:, cols], g, NT)
            delta = jnp.sum(gp * p, axis=0, keepdims=True)
            ds = jnp.where(keep, p * (gp - delta), 0.0).astype(BF16)
            dvs.append(mm(p.astype(BF16), g))
            dks.append(mm(ds, q))
            dqs.append(mm(k, ds, TN))
            wide = ds.astype(F32)
            for f in range(WIN_T):
                at = (WIN_T - 1 - f) * CELL
                dt_ref[a, :, at : at + WINDOW] += wide[f * CELL : (f + 1) * CELL, :]
        scale = HEAD**-0.5
        dq_ref[...] = (jnp.concatenate(dqs, axis=0) * scale).T.astype(BF16)
        dk_ref[...] = jnp.concatenate(dks, axis=1).astype(BF16)
        dv_ref[...] = jnp.concatenate(dvs, axis=1).astype(BF16)

    q, k, v, t = attention_specs(pairs)
    one = pl.BlockSpec((WINDOW, 2 * HEAD), lambda h, w, nv: (w, h))
    return kernel_call(
        body,
        valid,
        (pairs, nw),
        [q, k, v, t, one, pl.BlockSpec((1, 1, 2, WINDOW), lambda h, w, nv: (w, h, 0, 0))],
        [one, one, one, t],
        [jax.ShapeDtypeStruct((tokens, width), BF16)] * 3
        + [jax.ShapeDtypeStruct((2 * pairs, CELL, TSPAN * CELL), F32)],
        [],
        [triple, triple, triple, table, grad, logs],
        10 * tokens * WINDOW * width * 4,
        2 * tokens * 8 * width,
    )


def attention_out(idx, mixed, x, mod, keep, weight, bias):
    tokens, width = x.shape
    rows = WINDOW
    nref = weight.n_sems()

    def body(idx, mixed_ref, x_ref, mod_ref, keep_ref, bias_ref, *rest):
        w_refs, rest = rest[:nref], rest[nref:]
        att_ref, mid_ref, norm_ref, w_buf, acc, sems = rest

        @pl.when(pl.program_id(0) == 0)
        def _():
            copies = weight.whole(idx, w_refs, w_buf, sems)
            for c in copies:
                c.start()
            for c in copies:
                c.wait()

        acc[...] = mm(mixed_ref[...], w_buf[...])

        def chunk(i, _):
            r = pl.ds(pl.multiple_of(i * CHUNK, CHUNK), CHUNK)
            att = acc[r, :] + bias_ref[...]
            mid = x_ref[r, :].astype(F32) + keep_ref[r, :] * mod_ref[2:3, :] * att
            normed, _inv = norm_rows(mid)
            att_ref[r, :] = att.astype(BF16)
            mid_ref[r, :] = mid
            norm_ref[r, :] = (normed * (1.0 + mod_ref[4:5, :]) + mod_ref[3:4, :]).astype(BF16)
            return 0

        lax.fori_loop(0, rows // CHUNK, chunk, 0)

    block = pl.BlockSpec((rows, width), lambda w, idx: (w, 0))
    return kernel_call(
        body,
        idx,
        (tokens // rows,),
        [
            block,
            block,
            pl.BlockSpec((6, width), lambda w, idx: (0, 0)),
            pl.BlockSpec((rows, 1), lambda w, idx: (w, 0)),
            pl.BlockSpec((1, width), lambda w, idx: (0, 0)),
            *weight.specs(),
        ],
        [block, block, block],
        [
            jax.ShapeDtypeStruct((tokens, width), BF16),
            jax.ShapeDtypeStruct((tokens, width), F32),
            jax.ShapeDtypeStruct((tokens, width), BF16),
        ],
        [
            pltpu.VMEM((width, width), BF16),
            pltpu.VMEM((rows, width), F32),
            pltpu.SemaphoreType.DMA((nref,)),
        ],
        [mixed, x, mod, keep, bias, *weight.operands()],
        2 * tokens * width * width,
        tokens * width * 12 + 2 * width * width,
    )


def gelu_up(idx, norm_mid, weight, bias):
    tokens, width = norm_mid.shape
    cols = weight.cols
    block = 512
    steps = cols // block
    rows = WINDOW
    nw = tokens // rows
    nref = weight.n_sems()

    def body(idx, x_ref, bias_ref, *rest):
        w_refs, rest = rest[:nref], rest[nref:]
        act_ref, slope_ref, w_buf, sems = rest
        j, w = pl.program_id(0), pl.program_id(1)

        @pl.when((j == 0) & (w == 0))
        def _():
            for s in range(steps):
                for c in weight.whole(idx, w_refs, w_buf, sems.at[s], s * block, block):
                    c.start()

        for s in range(steps):

            @pl.when((j == s) & (w == 0))
            def _():
                for c in weight.whole(idx, w_refs, w_buf, sems.at[s], s * block, block):
                    c.wait()

        a = x_ref[pl.ds(pl.multiple_of(w * rows, rows), rows), :]
        b = w_buf[:, pl.ds(pl.multiple_of(j * block, block), block)]
        h = mm(a, b) + bias_ref[...]
        square = h * h
        inner = GELU_C * h * (1.0 + GELU_A * square)
        th = jnp.tanh(inner)
        left = 0.5 * (1.0 + th)
        act_ref[...] = (h * left).astype(BF16)
        slope = left + 0.5 * h * (1.0 - th * th) * (GELU_C * (1.0 + 3.0 * GELU_A * square))
        slope_ref[...] = slope.astype(BF16)

    return kernel_call(
        body,
        idx,
        (steps, nw),
        [
            pl.BlockSpec((tokens, width), lambda j, w, idx: (0, 0)),
            pl.BlockSpec((1, block), lambda j, w, idx: (0, j)),
            *weight.specs(),
        ],
        [pl.BlockSpec((rows, block), lambda j, w, idx: (w, j))] * 2,
        [jax.ShapeDtypeStruct((tokens, cols), BF16)] * 2,
        [pltpu.VMEM((width, cols), BF16), pltpu.SemaphoreType.DMA((steps, nref))],
        [norm_mid, bias, *weight.operands()],
        2 * tokens * width * cols,
        2 * (tokens * (width + 2 * cols) + width * cols),
    )


def ffn_down(idx, activated, middle, cot, keep, gate, weight, bias):
    tokens, inner = activated.shape
    width = weight.cols
    block = 256
    steps = width // block
    rows = WINDOW
    nw = tokens // rows
    nref = weight.n_sems()

    def body(idx, act_ref, mid_ref, cot_ref, keep_ref, gate_ref, bias_ref, *rest):
        w_refs, rest = rest[:nref], rest[nref:]
        out_ref, gg_ref, w_buf, sems = rest
        j, w = pl.program_id(0), pl.program_id(1)

        @pl.when((j == 0) & (w == 0))
        def _():
            for s in range(steps):
                for c in weight.whole(idx, w_refs, w_buf, sems.at[s], s * block, block):
                    c.start()

        for s in range(steps):

            @pl.when((j == s) & (w == 0))
            def _():
                for c in weight.whole(idx, w_refs, w_buf, sems.at[s], s * block, block):
                    c.wait()

        a = act_ref[pl.ds(pl.multiple_of(w * rows, rows), rows), :]
        b = w_buf[:, pl.ds(pl.multiple_of(j * block, block), block)]
        ff = (mm(a, b) + bias_ref[...]) * keep_ref[...]
        out_ref[...] = (mid_ref[...] + ff * gate_ref[...]).astype(BF16)
        part = jnp.sum(ff * cot_ref[...].astype(F32), axis=0, keepdims=True)

        @pl.when(w == 0)
        def _():
            gg_ref[...] = part

        @pl.when(w > 0)
        def _():
            gg_ref[...] += part

    cell = pl.BlockSpec((rows, block), lambda j, w, idx: (w, j))
    line = pl.BlockSpec((1, block), lambda j, w, idx: (0, j))
    return kernel_call(
        body,
        idx,
        (steps, nw),
        [
            pl.BlockSpec((tokens, inner), lambda j, w, idx: (0, 0)),
            cell,
            cell,
            pl.BlockSpec((rows, 1), lambda j, w, idx: (w, 0)),
            line,
            line,
            *weight.specs(),
        ],
        [cell, line],
        [jax.ShapeDtypeStruct((tokens, width), BF16), jax.ShapeDtypeStruct((1, width), F32)],
        [pltpu.VMEM((inner, width), BF16), pltpu.SemaphoreType.DMA((steps, nref))],
        [activated, middle, cot, keep, gate, bias, *weight.operands()],
        2 * tokens * inner * width,
        2 * (tokens * (inner + 4 * width) + width * inner),
    )


def outer_product(idx, left, right, block, sums=False):
    _, half, tokens = left.shape
    cols = right.shape[1]

    def body(idx, mine_ref, other_ref, right_ref, keep_ref, send_ref, *sum_ref):
        b = right_ref[...]
        send_ref[...] = mm(other_ref[...], b).astype(BF16)
        keep_ref[...] = mm(mine_ref[...], b).astype(BF16)
        if sums:
            sum_ref[0][...] = jnp.sum(b.astype(F32), axis=0, keepdims=True)

    n = idx.shape[0] - 1
    out = pl.BlockSpec((half, block), lambda j, idx: (0, j))
    shape = jax.ShapeDtypeStruct((half, cols), BF16)
    extra = [pl.BlockSpec((1, block), lambda j, idx: (0, j))] if sums else []
    extra_shape = [jax.ShapeDtypeStruct((1, cols), F32)] if sums else []
    return kernel_call(
        body,
        idx,
        (cols // block,),
        [
            pl.BlockSpec((None, half, tokens), lambda j, idx: (idx[n], 0, 0)),
            pl.BlockSpec((None, half, tokens), lambda j, idx: (1 - idx[n], 0, 0)),
            pl.BlockSpec((tokens, block), lambda j, idx: (0, j)),
        ],
        [out, out, *extra],
        [shape, shape, *extra_shape],
        [],
        [left, left, right],
        4 * tokens * half * cols,
        2 * (2 * half * tokens + tokens * cols + 2 * half * cols),
    )


def hidden_back(idx, grad_ffn, slope, norm_t, weight):
    tokens, width = grad_ffn.shape
    inner = slope.shape[1]
    block = weight.rows
    steps = weight.count + 1
    half = norm_t.shape[1]
    nref = weight.n_sems()

    def body(idx, g_ref, slope_ref, mine_ref, other_ref, *rest):
        w_refs, rest = rest[:nref], rest[nref:]
        gh_ref, keep_ref, send_ref, sum_ref, w_buf, sems = rest
        j = pl.program_id(0)

        def copies(s):
            return weight.piece(idx, w_refs, w_buf, sems, s, s * block, 0, width)

        @pl.when(j == 0)
        def _():
            for s in range(steps):
                for c in copies(s):
                    c.start()

        for s in range(steps):

            @pl.when(j == s)
            def _():
                for c in copies(s):
                    c.wait()

        b = w_buf[pl.ds(pl.multiple_of(j * block, block), block), :]
        gh = (mm(g_ref[...], b, NT) * slope_ref[...].astype(F32)).astype(BF16)
        gh_ref[...] = gh
        sum_ref[...] = jnp.sum(gh.astype(F32), axis=0, keepdims=True)
        send_ref[...] = mm(other_ref[...], gh).astype(BF16)
        keep_ref[...] = mm(mine_ref[...], gh).astype(BF16)

    n = weight.count + 1
    out = pl.BlockSpec((half, block), lambda j, idx: (0, idx[j]))
    return kernel_call(
        body,
        idx,
        (steps,),
        [
            pl.BlockSpec((tokens, width), lambda j, idx: (0, 0)),
            pl.BlockSpec((tokens, block), lambda j, idx: (0, idx[j])),
            pl.BlockSpec((None, half, tokens), lambda j, idx: (idx[n], 0, 0)),
            pl.BlockSpec((None, half, tokens), lambda j, idx: (1 - idx[n], 0, 0)),
            *weight.specs(),
        ],
        [
            pl.BlockSpec((tokens, block), lambda j, idx: (0, idx[j])),
            out,
            out,
            pl.BlockSpec((1, block), lambda j, idx: (0, idx[j])),
        ],
        [
            jax.ShapeDtypeStruct((tokens, inner), BF16),
            jax.ShapeDtypeStruct((half, inner), BF16),
            jax.ShapeDtypeStruct((half, inner), BF16),
            jax.ShapeDtypeStruct((1, inner), F32),
        ],
        [pltpu.VMEM((inner, width), BF16), pltpu.SemaphoreType.DMA((nref,))],
        [grad_ffn, slope, norm_t, norm_t, *weight.operands()],
        8 * tokens * width * inner,
        2 * (tokens * (width + 2 * inner) + 2 * width * inner),
    )


def middle_back(idx, grad_hidden, middle, cot, attention, keep, mod, up, project):
    tokens, inner = grad_hidden.shape
    width = middle.shape[1]
    rows = WINDOW
    n_up, n_pr = up.n_sems(), project.n_sems()

    def body(idx, gh_ref, mid_ref, cot_ref, att_ref, keep_ref, mod_ref, *rest):
        up_refs, rest = rest[:n_up], rest[n_up:]
        pr_refs, rest = rest[:n_pr], rest[n_pr:]
        gm_ref, ga_ref, gx_ref, sum_ref, up_buf, pr_buf, acc, up_sems, pr_sems = rest

        @pl.when(pl.program_id(0) == 0)
        def _():
            first = up.whole(idx, up_refs, up_buf, up_sems)
            second = project.whole(idx, pr_refs, pr_buf, pr_sems)
            for c in first + second:
                c.start()
            sum_ref[...] = jnp.zeros_like(sum_ref)
            for c in first + second:
                c.wait()

        acc[...] = mm(gh_ref[...], up_buf[...], NT)

        def chunk(i, sums):
            r = pl.ds(pl.multiple_of(i * CHUNK, CHUNK), CHUNK)
            grad = acc[r, :]
            normed, inverse = norm_rows(mid_ref[r, :])
            whole = cot_ref[r, :].astype(F32) + norm_back(
                grad * (1.0 + mod_ref[4:5, :]), normed, inverse
            )
            gm_ref[r, :] = whole
            gated = keep_ref[r, :] * whole
            ga = (gated * mod_ref[2:3, :]).astype(BF16)
            ga_ref[r, :] = ga
            terms = (grad, grad * normed, gated * att_ref[r, :].astype(F32), ga.astype(F32))
            return tuple(
                s + jnp.sum(t.reshape(CHUNK // 8, 8, width), axis=0)
                for s, t in zip(sums, terms)
            )

        zero = jnp.zeros((8, width), F32)
        sums = lax.fori_loop(0, rows // CHUNK, chunk, (zero,) * 4)
        for i, s in enumerate(sums):
            sum_ref[i : i + 1, :] += jnp.sum(s, axis=0, keepdims=True)
        gx_ref[...] = mm(ga_ref[...], pr_buf[...], NT).astype(BF16)

    block = pl.BlockSpec((rows, width), lambda w, idx: (w, 0))
    return kernel_call(
        body,
        idx,
        (tokens // rows,),
        [
            pl.BlockSpec((rows, inner), lambda w, idx: (w, 0)),
            block,
            block,
            block,
            pl.BlockSpec((rows, 1), lambda w, idx: (w, 0)),
            pl.BlockSpec((6, width), lambda w, idx: (0, 0)),
            *up.specs(),
            *project.specs(),
        ],
        [block, block, block, pl.BlockSpec((4, width), lambda w, idx: (0, 0))],
        [
            jax.ShapeDtypeStruct((tokens, width), F32),
            jax.ShapeDtypeStruct((tokens, width), BF16),
            jax.ShapeDtypeStruct((tokens, width), BF16),
            jax.ShapeDtypeStruct((4, width), F32),
        ],
        [
            pltpu.VMEM((width, inner), BF16),
            pltpu.VMEM((width, width), BF16),
            pltpu.VMEM((rows, width), F32),
            pltpu.SemaphoreType.DMA((n_up,)),
            pltpu.SemaphoreType.DMA((n_pr,)),
        ],
        [grad_hidden, middle, cot, attention, keep, mod, *up.operands(), *project.operands()],
        2 * tokens * width * (inner + width),
        2 * (tokens * (inner + 8 * width) + width * (inner + width)),
    )


def input_back(idx, grads, x, grad_middle, mod, weight):
    tokens, width = x.shape
    rows = WINDOW
    nref = weight.n_sems()

    def body(idx, dq_ref, dk_ref, dv_ref, x_ref, gm_ref, mod_ref, *rest):
        w_refs, rest = rest[:nref], rest[nref:]
        out_ref, sum_ref, w_buf, acc, sems = rest

        @pl.when(pl.program_id(0) == 0)
        def _():
            copies = weight.whole(idx, w_refs, w_buf, sems)
            for c in copies:
                c.start()
            sum_ref[...] = jnp.zeros_like(sum_ref)
            for c in copies:
                c.wait()

        acc[...] = (
            mm(dq_ref[...], w_buf[:, 0:width], NT)
            + mm(dk_ref[...], w_buf[:, width : 2 * width], NT)
            + mm(dv_ref[...], w_buf[:, 2 * width : 3 * width], NT)
        )

        def chunk(i, sums):
            r = pl.ds(pl.multiple_of(i * CHUNK, CHUNK), CHUNK)
            grad = acc[r, :]
            normed, inverse = norm_rows(x_ref[r, :].astype(F32))
            back = norm_back(grad * (1.0 + mod_ref[1:2, :]), normed, inverse)
            out_ref[r, :] = (gm_ref[r, :] + back).astype(BF16)
            return tuple(
                s + jnp.sum(t.reshape(CHUNK // 8, 8, width), axis=0)
                for s, t in zip(sums, (grad, grad * normed))
            )

        zero = jnp.zeros((8, width), F32)
        sums = lax.fori_loop(0, rows // CHUNK, chunk, (zero,) * 2)
        for i, s in enumerate(sums):
            sum_ref[i : i + 1, :] += jnp.sum(s, axis=0, keepdims=True)

    block = pl.BlockSpec((rows, width), lambda w, idx: (w, 0))
    return kernel_call(
        body,
        idx,
        (tokens // rows,),
        [
            *([block] * 5),
            pl.BlockSpec((6, width), lambda w, idx: (0, 0)),
            *weight.specs(),
        ],
        [block, pl.BlockSpec((2, width), lambda w, idx: (0, 0))],
        [jax.ShapeDtypeStruct((tokens, width), BF16), jax.ShapeDtypeStruct((2, width), F32)],
        [
            pltpu.VMEM((width, 3 * width), BF16),
            pltpu.VMEM((rows, width), F32),
            pltpu.SemaphoreType.DMA((nref,)),
        ],
        [*grads, x, grad_middle, mod, *weight.operands()],
        6 * tokens * width * width,
        2 * (tokens * 9 * width + 3 * width * width),
    )


def triple_outer(idx, left, grads, block):
    _, half, tokens = left.shape
    width = grads[0].shape[1]
    per = width // block

    def body(idx, mine_ref, other_ref, q_ref, k_ref, v_ref, keep_ref, send_ref, sum_ref):
        for part, ref in enumerate((q_ref, k_ref, v_ref)):

            @pl.when(pl.program_id(0) // per == part)
            def _():
                b = ref[...]
                send_ref[...] = mm(other_ref[...], b).astype(BF16)
                keep_ref[...] = mm(mine_ref[...], b).astype(BF16)
                sum_ref[...] = jnp.sum(b.astype(F32), axis=0, keepdims=True)

    n = idx.shape[0] - 1
    out = pl.BlockSpec((half, block), lambda j, idx: (0, j))
    shape = jax.ShapeDtypeStruct((half, 3 * width), BF16)

    def part_spec(part):
        return pl.BlockSpec(
            (tokens, block), lambda j, idx: (0, jnp.clip(j - part * per, 0, per - 1))
        )

    return kernel_call(
        body,
        idx,
        (3 * per,),
        [
            pl.BlockSpec((None, half, tokens), lambda j, idx: (idx[n], 0, 0)),
            pl.BlockSpec((None, half, tokens), lambda j, idx: (1 - idx[n], 0, 0)),
            part_spec(0),
            part_spec(1),
            part_spec(2),
        ],
        [out, out, pl.BlockSpec((1, block), lambda j, idx: (0, j))],
        [shape, shape, jax.ShapeDtypeStruct((1, 3 * width), F32)],
        [],
        [left, left, *grads],
        12 * tokens * half * width,
        2 * (2 * half * tokens + 3 * tokens * width + 6 * half * width),
    )


def spread_table(table):
    heads = table.shape[0]
    grid = table.reshape(heads, TSPAN, SPAN, SPAN)
    cols = jnp.stack([grid[..., WIN_S - 1 - x : SPAN - x] for x in range(WIN_S)], axis=1)
    cols = cols.reshape(heads, WIN_S, TSPAN, SPAN * WIN_S)
    rows = jnp.stack(
        [cols[..., (WIN_S - 1 - y) * WIN_S : (SPAN - y) * WIN_S] for y in range(WIN_S)], axis=1
    )
    return rows.reshape(heads, CELL, TSPAN * CELL)


def window_rows(grid, groups):
    clips_here, frames, halves, rows, side, width = grid.shape
    periods = frames // WIN_T
    cells = grid.reshape(clips_here, periods, WIN_T, halves, rows, halves, WIN_S, width)
    cells = cells.transpose(0, 1, 3, 5, 2, 4, 6, 7)
    return cells.reshape(groups, -1, WIN_T, rows, WIN_S, width)


def window_back(pieces, shape):
    clips_here, frames, halves, rows, side, width = shape
    periods = frames // WIN_T
    cells = pieces.reshape(clips_here, periods, halves, halves, WIN_T, rows, WIN_S, width)
    return cells.transpose(0, 1, 4, 2, 5, 3, 6, 7).reshape(shape)


def to_windows(grid, groups):
    got = lax.all_to_all(
        window_rows(grid, groups), "win", split_axis=0, concat_axis=3, tiled=True
    )
    return got.reshape(-1, grid.shape[-1])


def from_windows(rows, per_dev, shape):
    out = lax.all_to_all(
        rows.reshape(1, per_dev, WIN_T, WIN_S, WIN_S, shape[-1]),
        "win",
        split_axis=3,
        concat_axis=0,
        tiled=True,
    )
    return window_back(out, shape)


def body(
    tokens,
    condition,
    frame_count,
    triple_weight,
    triple_bias,
    project_weight,
    project_bias,
    up_weight,
    up_bias,
    down_weight,
    down_bias,
    modulate_weight,
    modulate_bias,
    position_table,
    cotangent,
):
    width = tokens.shape[-1]
    n = lax.axis_size("clip")
    groups = lax.axis_size("win")
    halves = tokens.shape[2]
    per_time = tokens.shape[1] // WIN_T
    per_dev = per_time * halves * halves // groups
    count = per_dev * WINDOW
    ring = Ring(n)
    core = ring.core
    rows = width // n

    def half_of(shard):
        size = shard.shape[0] // CORES
        return lax.dynamic_slice_in_dim(shard, core * size, size, 0)

    x = to_windows(tokens, groups)
    sigma = jax.nn.sigmoid(condition)
    cond_in = (condition * sigma).astype(BF16)
    vectors = [cond_in[0], triple_bias, project_bias, up_bias, down_bias, modulate_bias]
    sizes = np.cumsum([0] + [v.shape[0] for v in vectors])
    small = ring.gather_small(jnp.concatenate(vectors)[None])
    cond_all, triple_b, project_b, up_b, down_b, modulate_b = (
        small[:, sizes[i] : sizes[i + 1]] for i in range(len(vectors))
    )
    flat = lambda v: v.reshape(1, -1).astype(F32)
    triple_b, project_b, up_b, down_b = map(flat, (triple_b, project_b, up_b, down_b))
    bias_all = jnp.concatenate(
        [triple_b[:, :width], jnp.zeros((1, width), F32), triple_b[:, width:]], axis=1
    )
    cond_rows = lax.dynamic_slice_in_dim(cond_all, ring.rank * rows, rows, 1)
    mod = ring.scatter_small(mm(cond_rows, modulate_weight)) + modulate_b.reshape(-1).astype(F32)
    mod = mod.reshape(6, width)

    first = jnp.concatenate([half_of(triple_weight), half_of(project_weight)], axis=1)
    own_a, sib_a = ring.gather(first, False)
    own_b, sib_b = ring.gather(half_of(up_weight), True)
    own_c, sib_c = ring.gather(half_of(down_weight), False)
    idx = ring.index()
    triple_w = Weight(triple_weight, own_a, sib_a)
    project_w = Weight(project_weight, own_a, sib_a, 3 * width)
    up_w = Weight(up_weight, own_b, sib_b)
    down_w = Weight(down_weight, own_c, sib_c)

    window_id = lax.axis_index("win") * per_dev + jnp.arange(per_dev)
    start = window_id // (halves * halves) * WIN_T
    valid = jnp.clip(frame_count[0] - start, 0, WIN_T).astype(jnp.int32)
    keep = (jnp.arange(WINDOW)[None] // CELL < valid[:, None]).astype(F32).reshape(count, 1)
    table, table_back = jax.vjp(spread_table, position_table)
    cot = to_windows(cotangent, groups)
    gate_two = mod[5:6]
    grad_ffn = (keep * cot.astype(F32) * gate_two).astype(BF16)
    down_bias_grad = jnp.sum(grad_ffn.astype(F32), axis=0)

    def turned(v):
        v = v.reshape(count, n, CORES, rows // CORES).transpose(2, 1, 3, 0)
        return v.reshape(CORES, width // CORES, count)

    norm_in, triple = qkv_project(idx, x, mod, triple_w, bias_all)
    mixed, logs = attend(valid, triple, table)
    attention, middle, norm_mid = attention_out(
        idx, mixed, x, mod, keep, project_w, project_b
    )
    activated, slope = gelu_up(idx, norm_mid, up_w, up_b)
    result, grad_gate_two = ffn_down(
        idx, activated, middle, cot, keep, gate_two, down_w, down_b
    )
    output = from_windows(result, per_dev, tokens.shape)

    turned_ffn = grad_ffn.T.reshape(CORES, width // CORES, count)
    inner = activated.shape[1]
    down_keep, down_send = outer_product(idx, turned_ffn, activated, 512)
    split_cols = lambda g: g.reshape(width // CORES, n, inner // n).transpose(1, 0, 2)
    down_parts = ring.scatter(split_cols(down_keep), split_cols(down_send), False)
    down_weight_grad = jnp.concatenate([p.T for p in down_parts], axis=1).astype(F32)

    grad_hidden, up_keep, up_send, up_bias_grad = hidden_back(
        idx, grad_ffn, slope, turned(norm_mid), down_w
    )
    split_rows = lambda g: g.reshape(n, rows // CORES, -1)
    up_parts = ring.scatter(split_rows(up_keep), split_rows(up_send), True)
    up_weight_grad = jnp.concatenate(up_parts, axis=0).astype(F32)

    grad_middle, grad_attention, grad_mixed, mid_sums = middle_back(
        idx, grad_hidden, middle, cot, attention, keep, mod, up_w, project_w
    )
    grad_shift_two, grad_scale_two, grad_gate_one, project_bias_grad = mid_sums
    project_keep, project_send = outer_product(idx, turned(mixed), grad_attention, 512)
    *grads, grad_table = attend_back(valid, triple, table, grad_mixed, logs)
    triple_keep, triple_send, triple_sums = triple_outer(idx, turned(norm_in), grads, 512)
    last_parts = ring.scatter(
        split_rows(jnp.concatenate([triple_keep, project_keep], axis=1)),
        split_rows(jnp.concatenate([triple_send, project_send], axis=1)),
        False,
    )
    last = jnp.concatenate(last_parts, axis=0).astype(F32)
    triple_weight_grad, project_weight_grad = last[:, : 3 * width], last[:, 3 * width :]
    grad_rows, in_sums = input_back(idx, grads, x, grad_middle, mod, triple_w)
    input_grad = from_windows(grad_rows, per_dev, tokens.shape)

    table_grad = table_back(grad_table)[0]
    triple_bias_grad = jnp.concatenate([triple_sums[0, :width], triple_sums[0, 2 * width :]])
    pieces = [
        table_grad.reshape(-1),
        triple_bias_grad,
        project_bias_grad,
        up_bias_grad[0],
        down_bias_grad,
    ]
    ends = np.cumsum([0] + [p.shape[0] for p in pieces])
    pad = -int(ends[-1]) % 1024
    packed = jnp.concatenate(pieces + [jnp.zeros((pad,), F32)]).reshape(-1, 128)
    packed = ring.sum_all(packed).reshape(-1)
    table_grad, *bias_grads = (packed[ends[i] : ends[i + 1]] for i in range(len(pieces)))
    table_grad = table_grad.reshape(position_table.shape)
    bias_grads = [
        lax.dynamic_slice_in_dim(g, ring.rank * (g.shape[0] // n), g.shape[0] // n)
        for g in bias_grads
    ]
    grad_mod = jnp.concatenate(
        [
            in_sums[0],
            in_sums[1],
            grad_gate_one,
            grad_shift_two,
            grad_scale_two,
            grad_gate_two[0],
        ]
    )
    grad_mod = ring.sum_win(grad_mod[None]).astype(BF16)
    grad_mod = ring.gather_small(grad_mod)
    modulate_weight_grad = mm(cond_rows, grad_mod, TN)
    modulate_bias_grad = lax.dynamic_slice_in_dim(
        jnp.sum(grad_mod.astype(F32), axis=0), ring.rank * (6 * rows), 6 * rows
    )
    back = ring.gather_small(mm(grad_mod, modulate_weight, NT)[None])
    back = lax.dynamic_index_in_dim(back, ring.rank, 1, keepdims=False).reshape(1, width)
    condition_grad = back * (sigma * (1.0 + condition * (1.0 - sigma)))
    triple_bias_grad, project_bias_grad, up_bias_grad, down_bias_grad = bias_grads
    return (
        output,
        input_grad,
        condition_grad,
        triple_weight_grad,
        triple_bias_grad,
        project_weight_grad,
        project_bias_grad,
        up_weight_grad,
        up_bias_grad,
        down_weight_grad,
        down_bias_grad,
        modulate_weight_grad,
        modulate_bias_grad,
        table_grad,
    )


def solution(mesh):
    grid = P("clip", None, None, "win", None, None)
    matrix, vector = P("clip", None), P("clip")
    placed = (
        grid,
        matrix,
        vector,
        matrix,
        vector,
        matrix,
        vector,
        matrix,
        vector,
        matrix,
        vector,
        matrix,
        vector,
        P(),
        grid,
    )
    return jax.shard_map(
        body,
        mesh=mesh,
        in_specs=placed,
        out_specs=(grid, grid, *placed[1:2], *placed[3:14]),
        check_vma=False,
    )
```

```python
import math
import jax
import jax.numpy as jnp
import numpy as np
from jax import lax
from jax.experimental import pallas as pl
from jax.experimental.pallas import tpu as pltpu
from jax.sharding import PartitionSpec as P

WIN_T = 5
WIN_S = 8
WINDOW = WIN_T * WIN_S * WIN_S
CELL = WIN_S * WIN_S
SPAN = 2 * WIN_S - 1
TSPAN = 2 * WIN_T - 1
HEAD = 64
LANES = 128
CORES = 2
EPS = 1e-06
NEG = -30000.0
GELU_C = math.sqrt(2.0 / math.pi)
GELU_A = 0.044715
F32 = jnp.float32
BF16 = jnp.bfloat16
VMEM_SPARE = 58 * 1024 * 1024

NN = (((1,), (0,)), ((), ()))
NT = (((1,), (1,)), ((), ()))
TN = (((0,), (0,)), ((), ()))


def mm(a, b, dims=NN):
    return lax.dot_general(a, b, dims, preferred_element_type=F32)


def any_spec():
    return pl.BlockSpec(memory_space=pl.ANY)


def vmem_need(specs, shapes, scratch):
    total = VMEM_SPARE
    for spec, shape in zip(specs, shapes):
        if spec.block_shape is not None:
            block = [b for b in spec.block_shape if b is not None]
            total += 2 * math.prod(block) * max(shape.dtype.itemsize, 2)
    for ref in scratch:
        if ref.memory_space == pltpu.VMEM:
            total += math.prod(ref.shape) * np.dtype(ref.dtype).itemsize
    return total


def ring_order(n):
    ny = 1 << (int(math.log2(n)) // 2)
    nz = n // ny
    if ny < 2 or nz % 2:
        return list(range(n))
    walk = []
    for z in range(nz):
        ys = list(range(1, ny))
        walk += [z * ny + y for y in (ys if z % 2 == 0 else ys[::-1])]
    return walk + [z * ny for z in reversed(range(nz))]


def after(value, *deps):
    return together(value, *deps)[0]


def together(*values):
    flat, tree = jax.tree.flatten(values)
    return jax.tree.unflatten(tree, lax.optimization_barrier(flat))


def stage(groups, *values):
    states = [(g.a, g.b) for g in groups]
    states, values = together(states, values)
    for g, (a, b) in zip(groups, states):
        g.settle(a, b)
    return values


class Ring:
    def __init__(self, n):
        self.n = n
        order = ring_order(n)
        self.rank = lax.axis_index("clip")
        self.core = lax.axis_index("win") % CORES
        self.up = [(order[i], order[(i + 1) % n]) for i in range(n)]
        self.down = [(b, a) for a, b in self.up]
        rows = [
            [order[(order.index(r) + k) % n] for k in range(n)] + [c]
            for r in range(n)
            for c in range(CORES)
        ]
        self.index = lax.dynamic_slice_in_dim(
            jnp.asarray(np.array(rows, np.int32)), self.rank * CORES + self.core, 1, 0
        ).reshape(n + 1)
        wins = lax.axis_size("win")
        self.swap = [(w, w ^ 1) for w in range(wins)]
        powers = [1 << i for i in range(8)]
        self.pairs = [[(w, w ^ k) for w in range(wins)] for k in powers if k < wins]
        self.across = self.pairs[1:]

    def steps(self, flip):
        far, near = self.n // 2, (self.n - 1) // 2
        return (near, far) if flip else (far, near)

    def gather_small(self, row):
        return lax.all_to_all(jnp.broadcast_to(row[None], (self.n, *row.shape)), "clip", 0, 0)

    def scatter_small(self, block):
        return jnp.sum(lax.all_to_all(block, "clip", 0, 0, tiled=True), axis=0)

    def sum_win(self, row):
        wins = lax.axis_size("win")
        return jnp.sum(
            lax.all_to_all(jnp.broadcast_to(row[None], (wins, *row.shape)), "win", 0, 0), axis=0
        )

    def sum_all(self, rows):
        both = ("clip", "win")
        devices = self.n * lax.axis_size("win")
        part = jnp.sum(lax.all_to_all(rows.reshape(devices, -1, LANES), both, 0, 0, tiled=True), axis=0)
        whole = lax.all_to_all(jnp.broadcast_to(part[None], (devices, *part.shape)), both, 0, 0)
        return whole.reshape(-1, LANES)


class Gather:
    def __init__(self, ring, piece, flip):
        self.ring, self.ahead, self.back = ring, [], []
        self.far, self.near = ring.steps(flip)
        self.a = self.b = piece
        self.swapped = {}

    def step(self):
        ring = self.ring
        s = max(len(self.ahead), len(self.back))
        if s < self.far:
            self.a = lax.ppermute(self.a, "clip", ring.up)
            self.ahead.append(self.a)
        if s < self.near:
            self.b = lax.ppermute(self.b, "clip", ring.down)
            self.back.append(self.b)

    def settle(self, a, b):
        self.a, self.b = a, b
        if self.ahead:
            self.ahead[-1] = a
        if self.back:
            self.back[-1] = b

    def pieces(self):
        own = self.back + self.ahead[::-1]
        return own, [lax.ppermute(o, "win", self.ring.swap) for o in own]


class Scatter:
    def __init__(self, ring, keep, got, flip):
        self.ring, self.keep, self.got = ring, keep, got
        self.far, self.near = ring.steps(flip)
        self.a, self.b = self.part(self.far).astype(BF16), self.part(-self.near).astype(BF16)
        self.s = 0

    def part(self, k):
        k = k % self.ring.n
        return self.keep[k].astype(F32) + self.got[k].astype(F32)

    def step(self):
        s, far, near = self.s, self.far, self.near
        if s < far:
            if s > 0:
                self.a = (self.a.astype(F32) + self.part(far - s)).astype(BF16)
            self.a = lax.ppermute(self.a, "clip", self.ring.up)
        if s < near:
            if s > 0:
                self.b = (self.b.astype(F32) + self.part(s - near)).astype(BF16)
            self.b = lax.ppermute(self.b, "clip", self.ring.down)
        self.s += 1

    def settle(self, a, b):
        self.a, self.b = a, b

    def start_finish(self):
        ring = self.ring
        total = (self.part(0) + self.a.astype(F32) + self.b.astype(F32)).astype(BF16)
        for perm in ring.across:
            other = lax.ppermute(total, "win", perm)
            total = (total.astype(F32) + other.astype(F32)).astype(BF16)
        return total

    def finish(self, total):
        ring = self.ring
        other = lax.ppermute(total, "win", ring.swap)
        total, other = lax.optimization_barrier((total, other))
        first = jnp.where(ring.core == 0, total, other)
        second = jnp.where(ring.core == 0, other, total)
        return first, second


class Weight:
    def __init__(self, local, own, sib, col=0):
        self.local, self.own, self.sib, self.col = local, own, sib, col
        self.rows, self.cols = local.shape
        self.count = len(own)

    def operands(self):
        return [self.local, *self.own, *self.sib]

    def specs(self):
        return [any_spec()] * (1 + 2 * self.count)

    def shape(self):
        return (self.rows * (self.count + 1), self.cols)

    def n_sems(self):
        return 2 * self.count + 1

    def piece(self, idx, refs, dst, sems, i, base, start, width):
        half = self.rows // 2
        cols = pl.ds(start, width)
        into = pl.ds(start, width)
        if i == 0:
            rows = pl.ds(pl.multiple_of(base, self.rows), self.rows)
            return [
                pltpu.make_async_copy(refs[0].at[:, cols], dst.at[rows, into], sems.at[0])
            ]
        from_cols = pl.ds(self.col + start, width)
        core = idx[self.count + 1]
        copies = []
        for which, place in ((0, core), (1, 1 - core)):
            slot = which * self.count + i
            rows = pl.ds(pl.multiple_of(base + place * half, half), half)
            copies.append(
                pltpu.make_async_copy(
                    refs[slot].at[:, from_cols], dst.at[rows, into], sems.at[slot]
                )
            )
        return copies

    def whole(self, idx, refs, dst, sems, start=0, width=None):
        copies = []
        for i in range(self.count + 1):
            copies += self.piece(
                idx, refs, dst, sems, i, idx[i] * self.rows, start, width or self.cols
            )
        return copies


def kernel_call(
    body, idx, grid, in_specs, out_specs, out_shape, scratch, operands, flops, nbytes, aliases=None
):
    return pl.pallas_call(
        body,
        grid_spec=pltpu.PrefetchScalarGridSpec(
            num_scalar_prefetch=1,
            grid=grid,
            in_specs=in_specs,
            out_specs=out_specs,
            scratch_shapes=scratch,
        ),
        out_shape=out_shape,
        input_output_aliases=aliases or {},
        compiler_params=pltpu.CompilerParams(
            dimension_semantics=("arbitrary",) * len(grid),
            vmem_limit_bytes=VMEM_SPARE + 0 * vmem_need(
                [*in_specs, *out_specs], [*operands, *out_shape], scratch
            ),
        ),
        cost_estimate=pl.CostEstimate(
            flops=int(flops), bytes_accessed=int(nbytes), transcendentals=0
        ),
    )(idx, *operands)


def norm_rows(v):
    center = v - jnp.mean(v, axis=-1, keepdims=True)
    inverse = lax.rsqrt(jnp.mean(center * center, axis=-1, keepdims=True) + EPS)
    return center * inverse, inverse


def norm_back(grad, normed, inverse):
    mean_grad = jnp.mean(grad, axis=-1, keepdims=True)
    mean_cross = jnp.mean(grad * normed, axis=-1, keepdims=True)
    return inverse * (grad - mean_grad - normed * mean_cross)


CHUNK = 64


def pack_rows(condition, vectors):
    lined = lambda v: jnp.pad(v, (0, -v.size % LANES)).reshape(-1, LANES)
    operands = [condition.reshape(-1, LANES), *(lined(v) for v in vectors)]
    ends = np.cumsum([0] + [v.shape[0] for v in operands])

    def body(*refs):
        out_ref = refs[-1]
        for i, ref in enumerate(refs[:-1]):
            v = ref[...].astype(F32)
            if i == 0:
                v = v / (1.0 + jnp.exp(-v))
            out_ref[ends[i] : ends[i + 1], :] = v.astype(BF16).astype(F32)

    rows = pl.pallas_call(
        body, out_shape=jax.ShapeDtypeStruct((int(ends[-1]), LANES), F32)
    )(*operands)
    return rows, ends


def qkv_project(idx, x, mod, weight, bias):
    tokens, width = x.shape
    cols = weight.cols
    block = 512
    steps = cols // block
    rows = tokens
    nw = tokens // rows
    nref = weight.n_sems()

    def body(idx, x_ref, mod_ref, bias_ref, *rest):
        w_refs, rest = rest[:nref], rest[nref:]
        norm_ref, out_ref, w_buf, sems = rest
        j, w = pl.program_id(0), pl.program_id(1)

        @pl.when((j == 0) & (w == 0))
        def _():
            for s in range(steps):
                for c in weight.whole(idx, w_refs, w_buf, sems.at[s], s * block, block):
                    c.start()

            def chunk(i, _):
                r = pl.ds(pl.multiple_of(i * CHUNK, CHUNK), CHUNK)
                normed, _inv = norm_rows(x_ref[r, :].astype(F32))
                norm_ref[r, :] = (normed * (1.0 + mod_ref[1:2, :]) + mod_ref[0:1, :]).astype(BF16)
                return 0

            lax.fori_loop(0, tokens // CHUNK, chunk, 0)

        for s in range(steps):

            @pl.when((j == s) & (w == 0))
            def _():
                for c in weight.whole(idx, w_refs, w_buf, sems.at[s], s * block, block):
                    c.wait()

        a = norm_ref[pl.ds(pl.multiple_of(w * rows, rows), rows), :]
        b = w_buf[:, pl.ds(pl.multiple_of(j * block, block), block)]
        out_ref[...] = (mm(a, b) + bias_ref[...]).astype(BF16)

    return kernel_call(
        body,
        idx,
        (steps, nw),
        [
            pl.BlockSpec((tokens, width), lambda j, w, idx: (0, 0)),
            pl.BlockSpec((6, width), lambda j, w, idx: (0, 0)),
            pl.BlockSpec((1, block), lambda j, w, idx: (0, j)),
            *weight.specs(),
        ],
        [
            pl.BlockSpec((tokens, width), lambda j, w, idx: (0, 0)),
            pl.BlockSpec((rows, block), lambda j, w, idx: (w, j)),
        ],
        [
            jax.ShapeDtypeStruct((tokens, width), BF16),
            jax.ShapeDtypeStruct((tokens, cols), BF16),
        ],
        [pltpu.VMEM((width, cols), BF16), pltpu.SemaphoreType.DMA((steps, nref))],
        [x, mod, bias, *weight.operands()],
        2 * tokens * width * cols,
        2 * (tokens * (2 * width + cols) + width * cols),
    )


def fill_table(near, rows):
    for y in range(WIN_S):
        for f in range(TSPAN):
            at = f * LANES + (WIN_S - 1 - y) * WIN_S
            rows[y * WIN_S : (y + 1) * WIN_S, f * CELL : (f + 1) * CELL] = near[:, at : at + CELL]


def fold_table(rows, near):
    near[...] = jnp.zeros_like(near)
    for y in range(WIN_S):
        for f in range(TSPAN):
            at = f * LANES + (WIN_S - 1 - y) * WIN_S
            near[:, at : at + CELL] += rows[y * WIN_S : (y + 1) * WIN_S, f * CELL : (f + 1) * CELL]


def bias_rows(table):
    return jnp.concatenate(
        [table[:, (WIN_T - 1 - f) * CELL : (WIN_T - 1 - f) * CELL + WINDOW] for f in range(WIN_T)],
        axis=0,
    )


def attention_specs(pairs, lo=0):
    q = pl.BlockSpec((WINDOW, 2 * HEAD), lambda h, w, nv: (w, lo + h))
    k = pl.BlockSpec((WINDOW, 2 * HEAD), lambda h, w, nv: (w, pairs + lo + h))
    v = pl.BlockSpec((WINDOW, 2 * HEAD), lambda h, w, nv: (w, 2 * pairs + lo + h))
    t = pl.BlockSpec((2, WIN_S, TSPAN * LANES), lambda h, w, nv: (lo + h, 0, 0))
    return q, k, v, t


def attend(valid, triple, table, part, parts, before=None):
    tokens = triple.shape[0]
    width = triple.shape[1] // 3
    nw = tokens // WINDOW
    pairs = width // (2 * HEAD)
    here = pairs // parts
    lo = part * here

    def body(nv, q_ref, k_ref, v_ref, t_ref, *rest):
        o_ref, l_ref, rows = rest[-3:]
        w = pl.program_id(1)
        keep = lax.broadcasted_iota(jnp.int32, (WINDOW, 1), 0) < nv[w] * CELL

        @pl.when(w == 0)
        def _():
            for a in range(2):
                fill_table(t_ref.at[a], rows.at[a])

        outs = []
        for a in range(2):
            cols = slice(a * HEAD, (a + 1) * HEAD)
            q = q_ref[:, cols] * jnp.asarray(HEAD**-0.5, BF16)
            s = mm(k_ref[:, cols], q, NT)
            s = jnp.where(keep, s + bias_rows(rows[a]), NEG)
            peak = jnp.max(s, axis=0, keepdims=True)
            e = jnp.exp(s - peak)
            total = jnp.sum(e, axis=0, keepdims=True)
            p = (e * (1.0 / total)).astype(BF16)
            l_ref[0, 0, a : a + 1, :] = peak + jnp.log(total)
            outs.append(mm(v_ref[:, cols], p, TN))
        o_ref[...] = jnp.concatenate(outs, axis=0).T.astype(BF16)

    kept = list(before) if before else []
    return kernel_call(
        body,
        valid,
        (here, nw),
        [*attention_specs(pairs, lo), *[any_spec()] * len(kept)],
        [
            pl.BlockSpec((WINDOW, 2 * HEAD), lambda h, w, nv: (w, lo + h)),
            pl.BlockSpec((1, 1, 2, WINDOW), lambda h, w, nv: (w, lo + h, 0, 0)),
        ],
        [
            jax.ShapeDtypeStruct((tokens, width), BF16),
            jax.ShapeDtypeStruct((nw, pairs, 2, WINDOW), F32),
        ],
        [pltpu.VMEM((2, CELL, TSPAN * CELL), F32)],
        [triple, triple, triple, table, *kept],
        4 * tokens * WINDOW * width * 4 // parts,
        2 * tokens * 4 * width // parts,
        {5 + i: i for i in range(len(kept))},
    )


def attend_back(valid, triple, table, grad, logs):
    tokens = triple.shape[0]
    width = triple.shape[1] // 3
    nw = tokens // WINDOW
    pairs = width // (2 * HEAD)

    def body(
        nv, q_ref, k_ref, v_ref, t_ref, g_ref, l_ref, dq_ref, dk_ref, dv_ref, dt_ref, rows, drows
    ):
        w = pl.program_id(1)
        keep = lax.broadcasted_iota(jnp.int32, (WINDOW, 1), 0) < nv[w] * CELL
        dqs, dks, dvs = [], [], []

        @pl.when(w == 0)
        def _():
            for a in range(2):
                fill_table(t_ref.at[a], rows.at[a])
            drows[...] = jnp.zeros_like(drows)

        for a in range(2):
            cols = slice(a * HEAD, (a + 1) * HEAD)
            q = q_ref[:, cols] * jnp.asarray(HEAD**-0.5, BF16)
            k, g = k_ref[:, cols], g_ref[:, cols]
            s = mm(k, q, NT)
            s = jnp.where(keep, s + bias_rows(rows[a]), NEG)
            p = jnp.exp(s - l_ref[0, 0, a : a + 1, :])
            gp = mm(v_ref[:, cols], g, NT)
            delta = jnp.sum(gp * p, axis=0, keepdims=True)
            ds = jnp.where(keep, p * (gp - delta), 0.0).astype(BF16)
            dvs.append(mm(p.astype(BF16), g))
            dks.append(mm(ds, q))
            dqs.append(mm(k, ds, TN))
            wide = ds.astype(F32)
            for f in range(WIN_T):
                at = (WIN_T - 1 - f) * CELL
                drows[a, :, at : at + WINDOW] += wide[f * CELL : (f + 1) * CELL, :]
        scale = HEAD**-0.5
        dq_ref[...] = (jnp.concatenate(dqs, axis=0) * scale).T.astype(BF16)
        dk_ref[...] = jnp.concatenate(dks, axis=1).astype(BF16)
        dv_ref[...] = jnp.concatenate(dvs, axis=1).astype(BF16)

        @pl.when(w == nw - 1)
        def _():
            for a in range(2):
                fold_table(drows.at[a], dt_ref.at[a])

    q, k, v, t = attention_specs(pairs)
    one = pl.BlockSpec((WINDOW, 2 * HEAD), lambda h, w, nv: (w, h))
    return kernel_call(
        body,
        valid,
        (pairs, nw),
        [q, k, v, t, one, pl.BlockSpec((1, 1, 2, WINDOW), lambda h, w, nv: (w, h, 0, 0))],
        [one, one, one, t],
        [jax.ShapeDtypeStruct((tokens, width), BF16)] * 3
        + [jax.ShapeDtypeStruct((2 * pairs, WIN_S, TSPAN * LANES), F32)],
        [pltpu.VMEM((2, CELL, TSPAN * CELL), F32)] * 2,
        [triple, triple, triple, table, grad, logs],
        10 * tokens * WINDOW * width * 4,
        2 * tokens * 8 * width,
    )


def attention_out(idx, mixed, x, mod, keep, weight, bias):
    tokens, width = x.shape
    rows = WINDOW
    nref = weight.n_sems()

    def body(idx, mixed_ref, x_ref, mod_ref, keep_ref, bias_ref, *rest):
        w_refs, rest = rest[:nref], rest[nref:]
        att_ref, mid_ref, norm_ref, w_buf, acc, sems = rest

        @pl.when(pl.program_id(0) == 0)
        def _():
            copies = weight.whole(idx, w_refs, w_buf, sems)
            for c in copies:
                c.start()
            for c in copies:
                c.wait()

        acc[...] = mm(mixed_ref[...], w_buf[...])

        def chunk(i, _):
            r = pl.ds(pl.multiple_of(i * CHUNK, CHUNK), CHUNK)
            att = acc[r, :] + bias_ref[...]
            mid = x_ref[r, :].astype(F32) + keep_ref[r, :] * mod_ref[2:3, :] * att
            normed, _inv = norm_rows(mid)
            att_ref[r, :] = att.astype(BF16)
            mid_ref[r, :] = mid
            norm_ref[r, :] = (normed * (1.0 + mod_ref[4:5, :]) + mod_ref[3:4, :]).astype(BF16)
            return 0

        lax.fori_loop(0, rows // CHUNK, chunk, 0)

    block = pl.BlockSpec((rows, width), lambda w, idx: (w, 0))
    return kernel_call(
        body,
        idx,
        (tokens // rows,),
        [
            block,
            block,
            pl.BlockSpec((6, width), lambda w, idx: (0, 0)),
            pl.BlockSpec((rows, 1), lambda w, idx: (w, 0)),
            pl.BlockSpec((1, width), lambda w, idx: (0, 0)),
            *weight.specs(),
        ],
        [block, block, block],
        [
            jax.ShapeDtypeStruct((tokens, width), BF16),
            jax.ShapeDtypeStruct((tokens, width), F32),
            jax.ShapeDtypeStruct((tokens, width), BF16),
        ],
        [
            pltpu.VMEM((width, width), BF16),
            pltpu.VMEM((rows, width), F32),
            pltpu.SemaphoreType.DMA((nref,)),
        ],
        [mixed, x, mod, keep, bias, *weight.operands()],
        2 * tokens * width * width,
        tokens * width * 12 + 2 * width * width,
    )


def gelu_up(idx, norm_mid, weight, bias, part, parts, before=None):
    tokens, width = norm_mid.shape
    cols = weight.cols
    block = 512
    steps = cols // block // parts
    lo = part * steps
    kept = list(before) if before else []
    rows = tokens
    nw = tokens // rows
    nref = weight.n_sems()

    def body(idx, x_ref, bias_ref, *rest):
        w_refs = rest[:nref]
        act_ref, slope_ref, w_buf, sems = rest[-4:]
        j, w = pl.program_id(0), pl.program_id(1)

        @pl.when((j == 0) & (w == 0))
        def _():
            for s in range(steps):
                for c in weight.whole(idx, w_refs, w_buf, sems.at[s], (lo + s) * block, block):
                    c.start()

        for s in range(steps):

            @pl.when((j == s) & (w == 0))
            def _():
                for c in weight.whole(idx, w_refs, w_buf, sems.at[s], (lo + s) * block, block):
                    c.wait()

        a = x_ref[pl.ds(pl.multiple_of(w * rows, rows), rows), :]
        b = w_buf[:, pl.ds(pl.multiple_of((lo + j) * block, block), block)]
        h = mm(a, b) + bias_ref[...]
        square = h * h
        inner = GELU_C * h * (1.0 + GELU_A * square)
        th = jnp.tanh(inner)
        left = 0.5 * (1.0 + th)
        act_ref[...] = (h * left).astype(BF16)
        slope = left + 0.5 * h * (1.0 - th * th) * (GELU_C * (1.0 + 3.0 * GELU_A * square))
        slope_ref[...] = slope.astype(BF16)

    return kernel_call(
        body,
        idx,
        (steps, nw),
        [
            pl.BlockSpec((tokens, width), lambda j, w, idx: (0, 0)),
            pl.BlockSpec((1, block), lambda j, w, idx: (0, lo + j)),
            *weight.specs(),
            *[any_spec()] * len(kept),
        ],
        [pl.BlockSpec((rows, block), lambda j, w, idx: (w, lo + j))] * 2,
        [jax.ShapeDtypeStruct((tokens, cols), BF16)] * 2,
        [pltpu.VMEM((width, cols), BF16), pltpu.SemaphoreType.DMA((steps, nref))],
        [norm_mid, bias, *weight.operands(), *kept],
        2 * tokens * width * cols // parts,
        2 * (tokens * (width + 2 * cols) + width * cols) // parts,
        {3 + nref + i: i for i in range(len(kept))},
    )


def ffn_down(idx, activated, middle, cot, keep, gate, weight, bias):
    tokens, inner = activated.shape
    width = weight.cols
    block = 256
    steps = width // block
    rows = tokens
    nw = tokens // rows
    nref = weight.n_sems()

    def body(idx, act_ref, mid_ref, cot_ref, keep_ref, gate_ref, bias_ref, *rest):
        w_refs, rest = rest[:nref], rest[nref:]
        out_ref, gg_ref, w_buf, sems = rest
        j, w = pl.program_id(0), pl.program_id(1)

        @pl.when((j == 0) & (w == 0))
        def _():
            for s in range(steps):
                for c in weight.whole(idx, w_refs, w_buf, sems.at[s], s * block, block):
                    c.start()

        for s in range(steps):

            @pl.when((j == s) & (w == 0))
            def _():
                for c in weight.whole(idx, w_refs, w_buf, sems.at[s], s * block, block):
                    c.wait()

        a = act_ref[pl.ds(pl.multiple_of(w * rows, rows), rows), :]
        b = w_buf[:, pl.ds(pl.multiple_of(j * block, block), block)]
        ff = (mm(a, b) + bias_ref[...]) * keep_ref[...]
        out_ref[...] = (mid_ref[...] + ff * gate_ref[...]).astype(BF16)
        part = jnp.sum(ff * cot_ref[...].astype(F32), axis=0, keepdims=True)

        @pl.when(w == 0)
        def _():
            gg_ref[...] = part

        @pl.when(w > 0)
        def _():
            gg_ref[...] += part

    cell = pl.BlockSpec((rows, block), lambda j, w, idx: (w, j))
    line = pl.BlockSpec((1, block), lambda j, w, idx: (0, j))
    return kernel_call(
        body,
        idx,
        (steps, nw),
        [
            pl.BlockSpec((tokens, inner), lambda j, w, idx: (0, 0)),
            cell,
            cell,
            pl.BlockSpec((rows, 1), lambda j, w, idx: (w, 0)),
            line,
            line,
            *weight.specs(),
        ],
        [cell, line],
        [jax.ShapeDtypeStruct((tokens, width), BF16), jax.ShapeDtypeStruct((1, width), F32)],
        [pltpu.VMEM((inner, width), BF16), pltpu.SemaphoreType.DMA((steps, nref))],
        [activated, middle, cot, keep, gate, bias, *weight.operands()],
        2 * tokens * inner * width,
        2 * (tokens * (inner + 4 * width) + width * inner),
    )


def walk_rows(idx, refs, bufs, n):
    for ref, buf in zip(refs, bufs):
        size = buf.shape[0] // n
        for k in range(n):
            rows = pl.ds(pl.multiple_of(idx[k] * size, size), size)
            buf[k * size : (k + 1) * size, :] = ref[rows, :]


def half_specs(half, tokens, n):
    return [
        pl.BlockSpec((None, half, tokens), lambda j, idx: (idx[n], 0, 0)),
        pl.BlockSpec((None, half, tokens), lambda j, idx: (1 - idx[n], 0, 0)),
    ]


def down_outer(idx, left, right):
    _, half, tokens = left.shape
    n = idx.shape[0] - 1
    block = right.shape[1] // n

    def body(idx, mine_ref, other_ref, right_ref, keep_ref, send_ref):
        b = right_ref[...]
        send_ref[...] = mm(other_ref[...], b).astype(BF16)
        keep_ref[...] = mm(mine_ref[...], b).astype(BF16)

    out = pl.BlockSpec((None, half, block), lambda j, idx: (j, 0, 0))
    shape = jax.ShapeDtypeStruct((n, half, block), BF16)
    return kernel_call(
        body,
        idx,
        (n,),
        [
            *half_specs(half, tokens, n),
            pl.BlockSpec((tokens, block), lambda j, idx: (0, idx[j])),
        ],
        [out, out],
        [shape, shape],
        [],
        [left, left, right],
        4 * tokens * half * block * n,
        2 * (2 * half * tokens + tokens * block * n + 2 * half * block * n),
    )


def hidden_back(idx, grad_ffn, slope, norm_t, weight):
    tokens, width = grad_ffn.shape
    inner = slope.shape[1]
    block = weight.rows
    steps = weight.count + 1
    half = norm_t.shape[1]
    n = weight.count + 1
    nref = weight.n_sems()

    def body(idx, g_ref, slope_ref, mine_ref, other_ref, *rest):
        w_refs, rest = rest[:nref], rest[nref:]
        gh_ref, keep_ref, send_ref, sum_ref, w_buf, mine, other, sems = rest
        j = pl.program_id(0)

        def copies(s):
            return weight.piece(idx, w_refs, w_buf, sems, s, s * block, 0, width)

        @pl.when(j == 0)
        def _():
            for s in range(steps):
                for c in copies(s):
                    c.start()
            walk_rows(idx, (mine_ref, other_ref), (mine, other), n)

        for s in range(steps):

            @pl.when(j == s)
            def _():
                for c in copies(s):
                    c.wait()

        b = w_buf[pl.ds(pl.multiple_of(j * block, block), block), :]
        gh = (mm(g_ref[...], b, NT) * slope_ref[...].astype(F32)).astype(BF16)
        gh_ref[...] = gh
        sum_ref[...] = jnp.sum(gh.astype(F32), axis=0, keepdims=True)
        send_ref[...] = mm(other[...], gh).astype(BF16)
        keep_ref[...] = mm(mine[...], gh).astype(BF16)

    out = pl.BlockSpec((half, block), lambda j, idx: (0, idx[j]))
    return kernel_call(
        body,
        idx,
        (steps,),
        [
            pl.BlockSpec((tokens, width), lambda j, idx: (0, 0)),
            pl.BlockSpec((tokens, block), lambda j, idx: (0, idx[j])),
            *half_specs(half, tokens, n),
            *weight.specs(),
        ],
        [
            pl.BlockSpec((tokens, block), lambda j, idx: (0, idx[j])),
            out,
            out,
            pl.BlockSpec((1, block), lambda j, idx: (0, idx[j])),
        ],
        [
            jax.ShapeDtypeStruct((tokens, inner), BF16),
            jax.ShapeDtypeStruct((half, inner), BF16),
            jax.ShapeDtypeStruct((half, inner), BF16),
            jax.ShapeDtypeStruct((1, inner), F32),
        ],
        [
            pltpu.VMEM((inner, width), BF16),
            pltpu.VMEM((half, tokens), BF16),
            pltpu.VMEM((half, tokens), BF16),
            pltpu.SemaphoreType.DMA((nref,)),
        ],
        [grad_ffn, slope, norm_t, norm_t, *weight.operands()],
        8 * tokens * width * inner,
        2 * (tokens * (width + 2 * inner) + 2 * width * inner),
    )


def middle_back(idx, grad_hidden, middle, cot, attention, keep, mod, up, project):
    tokens, inner = grad_hidden.shape
    width = middle.shape[1]
    rows = WINDOW
    n_up, n_pr = up.n_sems(), project.n_sems()

    def body(idx, gh_ref, mid_ref, cot_ref, att_ref, keep_ref, mod_ref, *rest):
        up_refs, rest = rest[:n_up], rest[n_up:]
        pr_refs, rest = rest[:n_pr], rest[n_pr:]
        gm_ref, ga_ref, gx_ref, sum_ref, up_buf, pr_buf, acc, up_sems, pr_sems = rest

        @pl.when(pl.program_id(0) == 0)
        def _():
            first = up.whole(idx, up_refs, up_buf, up_sems)
            second = project.whole(idx, pr_refs, pr_buf, pr_sems)
            for c in first + second:
                c.start()
            sum_ref[...] = jnp.zeros_like(sum_ref)
            for c in first + second:
                c.wait()

        acc[...] = mm(gh_ref[...], up_buf[...], NT)

        def chunk(i, sums):
            r = pl.ds(pl.multiple_of(i * CHUNK, CHUNK), CHUNK)
            grad = acc[r, :]
            normed, inverse = norm_rows(mid_ref[r, :])
            whole = cot_ref[r, :].astype(F32) + norm_back(
                grad * (1.0 + mod_ref[4:5, :]), normed, inverse
            )
            gm_ref[r, :] = whole
            gated = keep_ref[r, :] * whole
            ga = (gated * mod_ref[2:3, :]).astype(BF16)
            ga_ref[r, :] = ga
            terms = (grad, grad * normed, gated * att_ref[r, :].astype(F32), ga.astype(F32))
            return tuple(
                s + jnp.sum(t.reshape(CHUNK // 8, 8, width), axis=0)
                for s, t in zip(sums, terms)
            )

        zero = jnp.zeros((8, width), F32)
        sums = lax.fori_loop(0, rows // CHUNK, chunk, (zero,) * 4)
        for i, s in enumerate(sums):
            sum_ref[i : i + 1, :] += jnp.sum(s, axis=0, keepdims=True)
        gx_ref[...] = mm(ga_ref[...], pr_buf[...], NT).astype(BF16)

    block = pl.BlockSpec((rows, width), lambda w, idx: (w, 0))
    return kernel_call(
        body,
        idx,
        (tokens // rows,),
        [
            pl.BlockSpec((rows, inner), lambda w, idx: (w, 0)),
            block,
            block,
            block,
            pl.BlockSpec((rows, 1), lambda w, idx: (w, 0)),
            pl.BlockSpec((6, width), lambda w, idx: (0, 0)),
            *up.specs(),
            *project.specs(),
        ],
        [block, block, block, pl.BlockSpec((4, width), lambda w, idx: (0, 0))],
        [
            jax.ShapeDtypeStruct((tokens, width), F32),
            jax.ShapeDtypeStruct((tokens, width), BF16),
            jax.ShapeDtypeStruct((tokens, width), BF16),
            jax.ShapeDtypeStruct((4, width), F32),
        ],
        [
            pltpu.VMEM((width, inner), BF16),
            pltpu.VMEM((width, width), BF16),
            pltpu.VMEM((rows, width), F32),
            pltpu.SemaphoreType.DMA((n_up,)),
            pltpu.SemaphoreType.DMA((n_pr,)),
        ],
        [grad_hidden, middle, cot, attention, keep, mod, *up.operands(), *project.operands()],
        2 * tokens * width * (inner + width),
        2 * (tokens * (inner + 8 * width) + width * (inner + width)),
    )


def input_back(idx, grads, x, grad_middle, mod, weight):
    tokens, width = x.shape
    rows = WINDOW
    nref = weight.n_sems()

    def body(idx, dq_ref, dk_ref, dv_ref, x_ref, gm_ref, mod_ref, *rest):
        w_refs, rest = rest[:nref], rest[nref:]
        out_ref, sum_ref, w_buf, acc, sems = rest

        @pl.when(pl.program_id(0) == 0)
        def _():
            copies = weight.whole(idx, w_refs, w_buf, sems)
            for c in copies:
                c.start()
            sum_ref[...] = jnp.zeros_like(sum_ref)
            for c in copies:
                c.wait()

        acc[...] = (
            mm(dq_ref[...], w_buf[:, 0:width], NT)
            + mm(dk_ref[...], w_buf[:, width : 2 * width], NT)
            + mm(dv_ref[...], w_buf[:, 2 * width : 3 * width], NT)
        )

        def chunk(i, sums):
            r = pl.ds(pl.multiple_of(i * CHUNK, CHUNK), CHUNK)
            grad = acc[r, :]
            normed, inverse = norm_rows(x_ref[r, :].astype(F32))
            back = norm_back(grad * (1.0 + mod_ref[1:2, :]), normed, inverse)
            out_ref[r, :] = (gm_ref[r, :] + back).astype(BF16)
            return tuple(
                s + jnp.sum(t.reshape(CHUNK // 8, 8, width), axis=0)
                for s, t in zip(sums, (grad, grad * normed))
            )

        zero = jnp.zeros((8, width), F32)
        sums = lax.fori_loop(0, rows // CHUNK, chunk, (zero,) * 2)
        for i, s in enumerate(sums):
            sum_ref[i : i + 1, :] += jnp.sum(s, axis=0, keepdims=True)

    block = pl.BlockSpec((rows, width), lambda w, idx: (w, 0))
    return kernel_call(
        body,
        idx,
        (tokens // rows,),
        [
            *([block] * 5),
            pl.BlockSpec((6, width), lambda w, idx: (0, 0)),
            *weight.specs(),
        ],
        [block, pl.BlockSpec((2, width), lambda w, idx: (0, 0))],
        [jax.ShapeDtypeStruct((tokens, width), BF16), jax.ShapeDtypeStruct((2, width), F32)],
        [
            pltpu.VMEM((width, 3 * width), BF16),
            pltpu.VMEM((rows, width), F32),
            pltpu.SemaphoreType.DMA((nref,)),
        ],
        [*grads, x, grad_middle, mod, *weight.operands()],
        6 * tokens * width * width,
        2 * (tokens * 9 * width + 3 * width * width),
    )


def last_outer(idx, norm_t, mixed_t, grads, grad_attention, block, other):
    _, half, tokens = norm_t.shape
    width = grad_attention.shape[1]
    per = width // block
    n = idx.shape[0] - 1

    def body(idx, *refs):
        ins, rest = refs[:6], refs[6:]
        out_ref, mine = rest[0], rest[-1]
        j = pl.program_id(0)

        @pl.when(j == 0)
        def _():
            walk_rows(idx, ins[0:1], (mine,), n)

        @pl.when(j == 3 * per)
        def _():
            walk_rows(idx, ins[1:2], (mine,), n)

        for part, ref in enumerate(ins[2:]):

            @pl.when(j // per == part)
            def _():
                b = ref[...]
                out_ref[...] = mm(mine[...], b).astype(BF16)
                if other:
                    rest[1][...] = jnp.sum(b.astype(F32), axis=0, keepdims=True)

    def part_spec(part):
        return pl.BlockSpec(
            (tokens, block), lambda j, idx: (0, jnp.clip(j - part * per, 0, per - 1))
        )

    left = half_specs(half, tokens, n)[1 if other else 0]
    out_specs = [pl.BlockSpec((half, block), lambda j, idx: (0, j))]
    out_shape = [jax.ShapeDtypeStruct((half, 4 * width), BF16)]
    if other:
        out_specs.append(pl.BlockSpec((1, block), lambda j, idx: (0, j)))
        out_shape.append(jax.ShapeDtypeStruct((1, 4 * width), F32))
    return kernel_call(
        body,
        idx,
        (4 * per,),
        [left, left, *(part_spec(p) for p in range(4))],
        out_specs,
        out_shape,
        [pltpu.VMEM((half, tokens), BF16)],
        [norm_t, mixed_t, *grads, grad_attention],
        8 * tokens * half * width,
        2 * (2 * half * tokens + 4 * tokens * width + 4 * half * width),
    )


def column_pick():
    pick = np.zeros((SPAN, SPAN, WIN_S, LANES // WIN_S, WIN_S), np.float32)
    for b in range(SPAN):
        for key in range(WIN_S):
            for query in range(WIN_S):
                pick[b, query - key + WIN_S - 1, key, b, query] = 1.0
    return jnp.asarray(pick.reshape(SPAN * SPAN, WIN_S * LANES))


def spread_table(table):
    heads = table.shape[0]
    wide = jnp.dot(
        table.reshape(heads * TSPAN, SPAN * SPAN), column_pick(), precision=lax.Precision.HIGHEST
    )
    wide = wide.reshape(heads, TSPAN, WIN_S, LANES).transpose(0, 2, 1, 3)
    return wide.reshape(heads, WIN_S, TSPAN * LANES)


def gather_table(grad):
    heads = grad.shape[0]
    wide = grad.reshape(heads, WIN_S, TSPAN, LANES).transpose(0, 2, 1, 3)
    wide = wide.reshape(heads * TSPAN, WIN_S * LANES)
    table = lax.dot_general(wide, column_pick(), NT, precision=lax.Precision.HIGHEST)
    return table.reshape(heads, TSPAN * SPAN * SPAN)


def window_rows(grid, groups):
    clips_here, frames, halves, rows, side, width = grid.shape
    periods = frames // WIN_T
    cells = grid.reshape(clips_here, periods, WIN_T, halves, rows, halves, WIN_S, width)
    cells = cells.transpose(0, 1, 3, 5, 2, 4, 6, 7)
    return cells.reshape(groups, -1, WIN_T, rows, WIN_S, width)


def window_back(pieces, shape):
    clips_here, frames, halves, rows, side, width = shape
    periods = frames // WIN_T
    cells = pieces.reshape(clips_here, periods, halves, halves, WIN_T, rows, WIN_S, width)
    return cells.transpose(0, 1, 4, 2, 5, 3, 6, 7).reshape(shape)


def to_windows(grid, groups):
    got = lax.all_to_all(
        window_rows(grid, groups), "win", split_axis=0, concat_axis=3, tiled=True
    )
    return got.reshape(-1, grid.shape[-1])


def from_windows(rows, per_dev, shape):
    out = lax.all_to_all(
        rows.reshape(1, per_dev, WIN_T, WIN_S, WIN_S, shape[-1]),
        "win",
        split_axis=3,
        concat_axis=0,
        tiled=True,
    )
    return window_back(out, shape)


def body(
    tokens,
    condition,
    frame_count,
    triple_weight,
    triple_bias,
    project_weight,
    project_bias,
    up_weight,
    up_bias,
    down_weight,
    down_bias,
    modulate_weight,
    modulate_bias,
    position_table,
    cotangent,
):
    width = tokens.shape[-1]
    n = lax.axis_size("clip")
    groups = lax.axis_size("win")
    halves = tokens.shape[2]
    per_time = tokens.shape[1] // WIN_T
    per_dev = per_time * halves * halves // groups
    count = per_dev * WINDOW
    ring = Ring(n)
    core = ring.core
    rows = width // n

    def half_of(shard):
        size = shard.shape[0] // CORES
        return lax.dynamic_slice_in_dim(shard, core * size, size, 0)

    def turned(v):
        v = v.reshape(count, n, CORES, rows // CORES).transpose(2, 1, 3, 0)
        return v.reshape(CORES, width // CORES, count)

    flat = lambda v: v.reshape(1, -1).astype(F32)
    split_rows = lambda g: g.reshape(n, rows // CORES, -1)
    swap = lambda g: lax.ppermute(g, "win", ring.swap)
    idx = ring.index
    steps = max(ring.steps(False))
    spare = lambda group, used: [group.step() for _ in range(used, steps)]

    first = jnp.concatenate([half_of(triple_weight), half_of(project_weight)], axis=1)
    group_a = Gather(ring, first, False)
    group_b = Gather(ring, half_of(up_weight), True)
    group_c = Gather(ring, half_of(down_weight), False)

    sigma = jax.nn.sigmoid(condition)
    group_a.step()
    tokens_here, condition_here = after((tokens, condition), first)
    vectors = [triple_bias, project_bias, up_bias, down_bias, modulate_bias]
    packed, ends = pack_rows(condition_here, vectors)
    small = ring.gather_small(packed.astype(BF16))
    x = to_windows(tokens_here, groups)
    cond_all, triple_b, project_b, up_b, down_b, modulate_b = (
        small[:, ends[i] : ends[i + 1]].reshape(n, -1)[:, : v.size]
        for i, v in enumerate([condition, *vectors])
    )
    triple_b, project_b, up_b, down_b = map(flat, (triple_b, project_b, up_b, down_b))
    bias_all = jnp.concatenate(
        [triple_b[:, :width], jnp.zeros((1, width), F32), triple_b[:, width:]], axis=1
    )
    cond_rows = lax.dynamic_slice_in_dim(cond_all, ring.rank * rows, rows, 1)
    mod = ring.scatter_small(mm(cond_rows, modulate_weight)) + modulate_b.reshape(-1).astype(F32)
    table = spread_table(position_table)
    mod = mod.reshape(6, width)
    stage([group_a])
    group_a.step()
    mod, table = stage([group_a], mod, table)

    window_id = lax.axis_index("win") * per_dev + jnp.arange(per_dev)
    start = window_id // (halves * halves) * WIN_T
    valid = jnp.clip(frame_count[0] - start, 0, WIN_T).astype(jnp.int32)
    keep = (jnp.arange(WINDOW)[None] // CELL < valid[:, None]).astype(F32).reshape(count, 1)
    group_a.step()
    x, bias_all = stage([group_a], x, bias_all)
    spare(group_a, 3)
    stage([group_a])
    triple_w = Weight(triple_weight, *group_a.pieces())
    project_w = Weight(project_weight, triple_w.own, triple_w.sib, 3 * width)

    (group_b.a, group_b.b), idx, valid = together(
        after((group_b.a, group_b.b), (group_a.a, group_a.b)), idx, valid
    )
    group_b.step()
    norm_in, triple, cotangent = stage(
        [group_b], *qkv_project(idx, x, mod, triple_w, bias_all), cotangent
    )
    group_b.step()
    cot = to_windows(cotangent, groups)
    norm_t = turned(norm_in)
    half_mixed = attend(valid, triple, table, 0, 2)
    *half_mixed, norm_t = stage([group_b], *half_mixed, norm_t)
    group_b.step()
    gate_two = mod[5:6]
    grad_ffn = (keep * cot.astype(F32) * gate_two).astype(BF16)
    mixed, logs = attend(valid, triple, table, 1, 2, half_mixed)
    mixed, logs, grad_ffn = stage([group_b], mixed, logs, grad_ffn)
    spare(group_b, 3)
    ffn_t = grad_ffn.T.reshape(CORES, width // CORES, count)
    mixed_t = turned(mixed)
    attention, middle, norm_mid, ffn_t, mixed_t = stage(
        [group_b],
        *attention_out(idx, mixed, x, mod, keep, project_w, project_b),
        ffn_t,
        mixed_t,
    )
    up_w = Weight(up_weight, *group_b.pieces())

    group_c.a, group_c.b = after((group_c.a, group_c.b), (group_b.a, group_b.b))
    group_c.step()
    half_act = stage([group_c], *gelu_up(idx, norm_mid, up_w, up_b, 0, 2))
    group_c.step()
    mid_t = turned(norm_mid)
    activated, slope, mid_t = stage(
        [group_c], *gelu_up(idx, norm_mid, up_w, up_b, 1, 2, half_act), mid_t
    )
    group_c.step()
    down_keep, down_send = stage([group_c], *down_outer(idx, ffn_t, activated))
    down_got = swap(down_send)
    spare(group_c, 3)
    (down_got,) = stage([group_c], down_got)
    down_w = Weight(down_weight, *group_c.pieces())

    sums_d = Scatter(ring, down_keep, down_got, False)
    grad_ffn, idx = stage([sums_d], after((grad_ffn, idx), (group_c.a, group_c.b)))[0]
    sums_d.step()
    down_bias_grad = jnp.sum(grad_ffn.astype(F32), axis=0)
    (grad_hidden, up_keep, up_send, up_bias_grad), idx = stage(
        [sums_d], hidden_back(idx, grad_ffn, slope, mid_t, down_w), idx
    )
    sums_u = Scatter(ring, split_rows(up_keep), swap(split_rows(up_send)), True)
    sums_d.step()
    (grad_middle, grad_attention, grad_mixed, mid_sums), idx, valid = stage(
        [sums_d, sums_u],
        middle_back(
            idx, grad_hidden, middle, cot, attention, keep, mod, up_w, project_w
        ),
        idx,
        valid,
    )
    grad_shift_two, grad_scale_two, grad_gate_one, project_bias_grad = mid_sums
    sums_d.step()
    sums_u.step()
    (*grads, grad_table), idx = stage(
        [sums_d, sums_u], attend_back(valid, triple, table, grad_mixed, logs), idx
    )
    spare(sums_d, 3)
    sums_u.step()
    last = (norm_t, mixed_t, grads, grad_attention, 1024)
    (last_send, last_sums), idx = together(last_outer(idx, *last, True), idx)
    last_got = swap(split_rows(last_send))
    table_grad = gather_table(grad_table)
    last_keep, last_got, idx, table_grad = stage(
        [sums_d, sums_u], last_outer(idx, *last, False)[0], last_got, idx, table_grad
    )
    sums_l = Scatter(ring, split_rows(last_keep), last_got, False)
    sums_u.step()
    sums_l.step()
    (grad_rows, in_sums), idx, down_sum = stage(
        [sums_u, sums_l],
        input_back(idx, grads, x, grad_middle, mod, triple_w),
        idx,
        sums_d.start_finish(),
    )
    spare(sums_u, 3)
    sums_l.step()
    input_grad = from_windows(grad_rows, per_dev, tokens.shape)
    input_grad, (result, grad_gate_two), down_parts = stage(
        [sums_l, sums_u],
        input_grad,
        ffn_down(idx, activated, middle, cot, keep, gate_two, down_w, down_b),
        sums_d.finish(down_sum),
    )

    rows_of = lambda v: v.reshape(-1, LANES)
    grad_mod = jnp.concatenate(
        [in_sums, grad_gate_one[None], mid_sums[0:2], grad_gate_two], axis=0
    )
    here = jnp.arange(n)[:, None, None] == ring.rank
    spans = position_table.shape[1]
    wide = -(-spans // LANES) * LANES
    pieces = [
        rows_of(jnp.pad(table_grad, ((0, 0), (0, wide - spans)))),
        rows_of(last_sums[0, :width]),
        rows_of(last_sums[0, 2 * width : 3 * width]),
        rows_of(project_bias_grad),
        rows_of(up_bias_grad[0]),
        rows_of(down_bias_grad),
        jnp.where(here, rows_of(grad_mod)[None], 0.0).reshape(-1, LANES),
    ]
    ends = np.cumsum([0] + [p.shape[0] for p in pieces])
    pad = -int(ends[-1]) % (n * groups * 8)
    packed = jnp.concatenate(pieces + [jnp.zeros((pad, LANES), F32)])
    sums_l.step()
    packed = ring.sum_all(packed)
    output = from_windows(result, per_dev, tokens.shape)
    up_sum, packed, output = stage([sums_l], sums_u.start_finish(), packed, output)
    spare(sums_l, 3)
    up_parts = sums_u.finish(up_sum)

    down_weight_grad = jnp.concatenate([p.T for p in down_parts], axis=1).astype(F32)
    up_weight_grad = jnp.concatenate(up_parts, axis=0).astype(F32)
    table_grad, *bias_grads, grad_mod = (packed[ends[i] : ends[i + 1]] for i in range(len(pieces)))
    table_grad = table_grad.reshape(-1, wide)[:, :spans]
    bias_grads = [jnp.concatenate(bias_grads[:2]), *bias_grads[2:]]
    bias_grads = [
        lax.dynamic_slice_in_dim(g.reshape(-1), ring.rank * (g.size // n), g.size // n)
        for g in bias_grads
    ]
    grad_mod = grad_mod.reshape(n, -1).astype(BF16)
    modulate_weight_grad = mm(cond_rows, grad_mod, TN)
    modulate_bias_grad = lax.dynamic_slice_in_dim(
        jnp.sum(grad_mod.astype(F32), axis=0), ring.rank * (6 * rows), 6 * rows
    )
    back = lax.all_to_all(mm(grad_mod, modulate_weight, NT), "clip", 0, 0, tiled=True)
    condition_grad = back.reshape(1, width) * (sigma * (1.0 + condition * (1.0 - sigma)))
    halves_l = sums_l.finish(sums_l.start_finish())
    triple_weight_grad, project_weight_grad = (
        jnp.concatenate([h[:, cols] for h in halves_l], axis=0).astype(F32)
        for cols in (slice(0, 3 * width), slice(3 * width, 4 * width))
    )
    triple_bias_grad, project_bias_grad, up_bias_grad, down_bias_grad = bias_grads
    return (
        output,
        input_grad,
        condition_grad,
        triple_weight_grad,
        triple_bias_grad,
        project_weight_grad,
        project_bias_grad,
        up_weight_grad,
        up_bias_grad,
        down_weight_grad,
        down_bias_grad,
        modulate_weight_grad,
        modulate_bias_grad,
        table_grad,
    )


def solution(mesh):
    grid = P("clip", None, None, "win", None, None)
    matrix, vector = P("clip", None), P("clip")
    placed = (
        grid,
        matrix,
        vector,
        matrix,
        vector,
        matrix,
        vector,
        matrix,
        vector,
        matrix,
        vector,
        matrix,
        vector,
        P(),
        grid,
    )
    return jax.shard_map(
        body,
        mesh=mesh,
        in_specs=placed,
        out_specs=(grid, grid, *placed[1:2], *placed[3:14]),
        check_vma=False,
    )
```

```python
import math
import jax
import jax.numpy as jnp
import numpy as np
from jax import lax
from jax.experimental import pallas as pl
from jax.experimental.pallas import tpu as pltpu
from jax.sharding import PartitionSpec as P

WIN_T = 5
WIN_S = 8
WINDOW = WIN_T * WIN_S * WIN_S
CELL = WIN_S * WIN_S
SPAN = 2 * WIN_S - 1
TSPAN = 2 * WIN_T - 1
HEAD = 64
LANES = 128
CORES = 2
EPS = 1e-06
NEG = -30000.0
GELU_C = math.sqrt(2.0 / math.pi)
GELU_A = 0.044715
F32 = jnp.float32
BF16 = jnp.bfloat16
VMEM_SPARE = 58 * 1024 * 1024

NN = (((1,), (0,)), ((), ()))
NT = (((1,), (1,)), ((), ()))
TN = (((0,), (0,)), ((), ()))


def mm(a, b, dims=NN):
    return lax.dot_general(a, b, dims, preferred_element_type=F32)


def any_spec():
    return pl.BlockSpec(memory_space=pl.ANY)


def vmem_need(specs, shapes, scratch):
    total = VMEM_SPARE
    for spec, shape in zip(specs, shapes):
        if spec.block_shape is not None:
            block = [b for b in spec.block_shape if b is not None]
            total += 2 * math.prod(block) * max(shape.dtype.itemsize, 2)
    for ref in scratch:
        if ref.memory_space == pltpu.VMEM:
            total += math.prod(ref.shape) * np.dtype(ref.dtype).itemsize
    return total


def ring_order(n):
    ny = 1 << (int(math.log2(n)) // 2)
    nz = n // ny
    if ny < 2 or nz % 2:
        return list(range(n))
    walk = []
    for z in range(nz):
        ys = list(range(1, ny))
        walk += [z * ny + y for y in (ys if z % 2 == 0 else ys[::-1])]
    return walk + [z * ny for z in reversed(range(nz))]


def after(value, *deps):
    return together(value, *deps)[0]


def together(*values):
    flat, tree = jax.tree.flatten(values)
    return jax.tree.unflatten(tree, lax.optimization_barrier(flat))


def stage(groups, *values):
    states = [(g.a, g.b) for g in groups]
    states, values = together(states, values)
    for g, (a, b) in zip(groups, states):
        g.settle(a, b)
    return values


class Ring:
    def __init__(self, n):
        self.n = n
        order = ring_order(n)
        self.rank = lax.axis_index("clip")
        self.core = lax.axis_index("win") % CORES
        self.up = [(order[i], order[(i + 1) % n]) for i in range(n)]
        self.down = [(b, a) for a, b in self.up]
        rows = [
            [order[(order.index(r) + k) % n] for k in range(n)] + [c]
            for r in range(n)
            for c in range(CORES)
        ]
        self.index = lax.dynamic_slice_in_dim(
            jnp.asarray(np.array(rows, np.int32)), self.rank * CORES + self.core, 1, 0
        ).reshape(n + 1)
        wins = lax.axis_size("win")
        self.swap = [(w, w ^ 1) for w in range(wins)]
        powers = [1 << i for i in range(8)]
        self.pairs = [[(w, w ^ k) for w in range(wins)] for k in powers if k < wins]
        self.across = self.pairs[1:]

    def steps(self, flip):
        far, near = self.n // 2, (self.n - 1) // 2
        return (near, far) if flip else (far, near)

    def gather_small(self, row):
        return lax.all_to_all(jnp.broadcast_to(row[None], (self.n, *row.shape)), "clip", 0, 0)

    def scatter_small(self, block):
        return jnp.sum(lax.all_to_all(block, "clip", 0, 0, tiled=True), axis=0)

    def sum_win(self, row):
        wins = lax.axis_size("win")
        return jnp.sum(
            lax.all_to_all(jnp.broadcast_to(row[None], (wins, *row.shape)), "win", 0, 0), axis=0
        )

    def sum_part(self, rows):
        devices = self.n * lax.axis_size("win")
        rows = rows.reshape(devices, -1, LANES)
        return jnp.sum(lax.all_to_all(rows, ("clip", "win"), 0, 0, tiled=True), axis=0)

    def share_parts(self, part):
        devices = self.n * lax.axis_size("win")
        part = jnp.broadcast_to(part[None], (devices, *part.shape))
        return lax.all_to_all(part, ("clip", "win"), 0, 0).reshape(-1, LANES)


class Gather:
    def __init__(self, ring, piece, flip):
        self.ring, self.ahead, self.back = ring, [], []
        self.far, self.near = ring.steps(flip)
        self.a = self.b = piece
        self.swapped = {}

    def step(self):
        ring = self.ring
        s = max(len(self.ahead), len(self.back))
        if s < self.far:
            self.a = lax.ppermute(self.a, "clip", ring.up)
            self.ahead.append(self.a)
        if s < self.near:
            self.b = lax.ppermute(self.b, "clip", ring.down)
            self.back.append(self.b)

    def settle(self, a, b):
        self.a, self.b = a, b
        if self.ahead:
            self.ahead[-1] = a
        if self.back:
            self.back[-1] = b

    def pieces(self):
        own = self.back + self.ahead[::-1]
        return own, [lax.ppermute(o, "win", self.ring.swap) for o in own]


class Scatter:
    def __init__(self, ring, keep, got, flip):
        self.ring, self.keep, self.got = ring, keep, got
        self.far, self.near = ring.steps(flip)
        self.a, self.b = self.part(self.far).astype(BF16), self.part(-self.near).astype(BF16)
        self.s = 0

    def part(self, k):
        k = k % self.ring.n
        return self.keep[k].astype(F32) + self.got[k].astype(F32)

    def step(self, *values):
        s, far, near = self.s, self.far, self.near
        if 0 < s < far:
            self.a = (self.a.astype(F32) + self.part(far - s)).astype(BF16)
        if 0 < s < near:
            self.b = (self.b.astype(F32) + self.part(s - near)).astype(BF16)
        if values:
            (self.a, self.b), *values = together((self.a, self.b), *values)
        if s < far:
            self.a = lax.ppermute(self.a, "clip", self.ring.up)
        if s < near:
            self.b = lax.ppermute(self.b, "clip", self.ring.down)
        self.s += 1
        return values

    def settle(self, a, b):
        self.a, self.b = a, b

    def start_finish(self):
        ring = self.ring
        total = (self.part(0) + self.a.astype(F32) + self.b.astype(F32)).astype(BF16)
        for perm in ring.across:
            other = lax.ppermute(total, "win", perm)
            total = (total.astype(F32) + other.astype(F32)).astype(BF16)
        return total

    def finish(self, total):
        return total, lax.ppermute(total, "win", self.ring.swap)


class Weight:
    def __init__(self, local, own, sib, col=0):
        self.local, self.own, self.sib, self.col = local, own, sib, col
        self.rows, self.cols = local.shape
        self.count = len(own)

    def operands(self):
        return [self.local, *self.own, *self.sib]

    def specs(self):
        return [any_spec()] * (1 + 2 * self.count)

    def shape(self):
        return (self.rows * (self.count + 1), self.cols)

    def n_sems(self):
        return 2 * self.count + 1

    def piece(self, idx, refs, dst, sems, i, base, start, width):
        half = self.rows // 2
        cols = pl.ds(start, width)
        into = pl.ds(start, width)
        if i == 0:
            rows = pl.ds(pl.multiple_of(base, self.rows), self.rows)
            return [
                pltpu.make_async_copy(refs[0].at[:, cols], dst.at[rows, into], sems.at[0])
            ]
        from_cols = pl.ds(self.col + start, width)
        core = idx[self.count + 1]
        copies = []
        for which, place in ((0, core), (1, 1 - core)):
            slot = which * self.count + i
            rows = pl.ds(pl.multiple_of(base + place * half, half), half)
            copies.append(
                pltpu.make_async_copy(
                    refs[slot].at[:, from_cols], dst.at[rows, into], sems.at[slot]
                )
            )
        return copies

    def whole(self, idx, refs, dst, sems, start=0, width=None):
        copies = []
        for i in range(self.count + 1):
            copies += self.piece(
                idx, refs, dst, sems, i, idx[i] * self.rows, start, width or self.cols
            )
        return copies


def kernel_call(
    body, idx, grid, in_specs, out_specs, out_shape, scratch, operands, flops, nbytes, aliases=None
):
    return pl.pallas_call(
        body,
        grid_spec=pltpu.PrefetchScalarGridSpec(
            num_scalar_prefetch=1,
            grid=grid,
            in_specs=in_specs,
            out_specs=out_specs,
            scratch_shapes=scratch,
        ),
        out_shape=out_shape,
        input_output_aliases=aliases or {},
        compiler_params=pltpu.CompilerParams(
            dimension_semantics=("arbitrary",) * len(grid),
            vmem_limit_bytes=VMEM_SPARE + 0 * vmem_need(
                [*in_specs, *out_specs], [*operands, *out_shape], scratch
            ),
        ),
        cost_estimate=pl.CostEstimate(
            flops=int(flops), bytes_accessed=int(nbytes), transcendentals=0
        ),
    )(idx, *operands)


def norm_rows(v):
    center = v - jnp.mean(v, axis=-1, keepdims=True)
    inverse = lax.rsqrt(jnp.mean(center * center, axis=-1, keepdims=True) + EPS)
    return center * inverse, inverse


def norm_back(grad, normed, inverse):
    mean_grad = jnp.mean(grad, axis=-1, keepdims=True)
    mean_cross = jnp.mean(grad * normed, axis=-1, keepdims=True)
    return inverse * (grad - mean_grad - normed * mean_cross)


CHUNK = 64


def pack_rows(condition, vectors):
    lined = lambda v: jnp.pad(v, (0, -v.size % LANES)).reshape(-1, LANES)
    operands = [condition.reshape(-1, LANES), *(lined(v) for v in vectors)]
    ends = np.cumsum([0] + [v.shape[0] for v in operands])

    def body(*refs):
        out_ref = refs[-1]
        for i, ref in enumerate(refs[:-1]):
            v = ref[...].astype(F32)
            if i == 0:
                v = v / (1.0 + jnp.exp(-v))
            out_ref[ends[i] : ends[i + 1], :] = v.astype(BF16).astype(F32)

    rows = pl.pallas_call(
        body, out_shape=jax.ShapeDtypeStruct((int(ends[-1]), LANES), F32)
    )(*operands)
    return rows, ends


def qkv_project(idx, x, mod, weight, bias):
    tokens, width = x.shape
    cols = weight.cols
    block = 512
    steps = cols // block
    rows = tokens
    nw = tokens // rows
    nref = weight.n_sems()

    def body(idx, x_ref, mod_ref, bias_ref, *rest):
        w_refs, rest = rest[:nref], rest[nref:]
        norm_ref, out_ref, w_buf, sems = rest
        j, w = pl.program_id(0), pl.program_id(1)

        @pl.when((j == 0) & (w == 0))
        def _():
            for s in range(steps):
                for c in weight.whole(idx, w_refs, w_buf, sems.at[s], s * block, block):
                    c.start()

            def chunk(i, _):
                r = pl.ds(pl.multiple_of(i * CHUNK, CHUNK), CHUNK)
                normed, _inv = norm_rows(x_ref[r, :].astype(F32))
                norm_ref[r, :] = (normed * (1.0 + mod_ref[1:2, :]) + mod_ref[0:1, :]).astype(BF16)
                return 0

            lax.fori_loop(0, tokens // CHUNK, chunk, 0)

        for s in range(steps):

            @pl.when((j == s) & (w == 0))
            def _():
                for c in weight.whole(idx, w_refs, w_buf, sems.at[s], s * block, block):
                    c.wait()

        a = norm_ref[pl.ds(pl.multiple_of(w * rows, rows), rows), :]
        b = w_buf[:, pl.ds(pl.multiple_of(j * block, block), block)]
        out_ref[...] = (mm(a, b) + bias_ref[...]).astype(BF16)

    return kernel_call(
        body,
        idx,
        (steps, nw),
        [
            pl.BlockSpec((tokens, width), lambda j, w, idx: (0, 0)),
            pl.BlockSpec((6, width), lambda j, w, idx: (0, 0)),
            pl.BlockSpec((1, block), lambda j, w, idx: (0, j)),
            *weight.specs(),
        ],
        [
            pl.BlockSpec((tokens, width), lambda j, w, idx: (0, 0)),
            pl.BlockSpec((rows, block), lambda j, w, idx: (w, j)),
        ],
        [
            jax.ShapeDtypeStruct((tokens, width), BF16),
            jax.ShapeDtypeStruct((tokens, cols), BF16),
        ],
        [pltpu.VMEM((width, cols), BF16), pltpu.SemaphoreType.DMA((steps, nref))],
        [x, mod, bias, *weight.operands()],
        2 * tokens * width * cols,
        2 * (tokens * (2 * width + cols) + width * cols),
    )


def fill_table(near, rows):
    for y in range(WIN_S):
        for f in range(TSPAN):
            at = f * LANES + (WIN_S - 1 - y) * WIN_S
            rows[y * WIN_S : (y + 1) * WIN_S, f * CELL : (f + 1) * CELL] = near[:, at : at + CELL]


def fold_table(rows, near):
    near[...] = jnp.zeros_like(near)
    for y in range(WIN_S):
        for f in range(TSPAN):
            at = f * LANES + (WIN_S - 1 - y) * WIN_S
            near[:, at : at + CELL] += rows[y * WIN_S : (y + 1) * WIN_S, f * CELL : (f + 1) * CELL]


def bias_rows(table):
    return jnp.concatenate(
        [table[:, (WIN_T - 1 - f) * CELL : (WIN_T - 1 - f) * CELL + WINDOW] for f in range(WIN_T)],
        axis=0,
    )


def attention_specs(pairs, lo=0):
    q = pl.BlockSpec((WINDOW, 2 * HEAD), lambda h, w, nv: (w, lo + h))
    k = pl.BlockSpec((WINDOW, 2 * HEAD), lambda h, w, nv: (w, pairs + lo + h))
    v = pl.BlockSpec((WINDOW, 2 * HEAD), lambda h, w, nv: (w, 2 * pairs + lo + h))
    t = pl.BlockSpec((2, WIN_S, TSPAN * LANES), lambda h, w, nv: (lo + h, 0, 0))
    return q, k, v, t


def attend(valid, triple, table, part, parts, before=None):
    tokens = triple.shape[0]
    width = triple.shape[1] // 3
    nw = tokens // WINDOW
    pairs = width // (2 * HEAD)
    here = pairs // parts
    lo = part * here

    def body(nv, q_ref, k_ref, v_ref, t_ref, *rest):
        o_ref, l_ref, rows = rest[-3:]
        w = pl.program_id(1)
        keep = lax.broadcasted_iota(jnp.int32, (WINDOW, 1), 0) < nv[w] * CELL

        @pl.when(w == 0)
        def _():
            for a in range(2):
                fill_table(t_ref.at[a], rows.at[a])

        outs = []
        for a in range(2):
            cols = slice(a * HEAD, (a + 1) * HEAD)
            q = q_ref[:, cols] * jnp.asarray(HEAD**-0.5, BF16)
            s = mm(k_ref[:, cols], q, NT)
            s = jnp.where(keep, s + bias_rows(rows[a]), NEG)
            peak = jnp.max(s, axis=0, keepdims=True)
            e = jnp.exp(s - peak)
            total = jnp.sum(e, axis=0, keepdims=True)
            p = (e * (1.0 / total)).astype(BF16)
            l_ref[0, 0, a : a + 1, :] = peak + jnp.log(total)
            outs.append(mm(v_ref[:, cols], p, TN))
        o_ref[...] = jnp.concatenate(outs, axis=0).T.astype(BF16)

    kept = list(before) if before else []
    return kernel_call(
        body,
        valid,
        (here, nw),
        [*attention_specs(pairs, lo), *[any_spec()] * len(kept)],
        [
            pl.BlockSpec((WINDOW, 2 * HEAD), lambda h, w, nv: (w, lo + h)),
            pl.BlockSpec((1, 1, 2, WINDOW), lambda h, w, nv: (w, lo + h, 0, 0)),
        ],
        [
            jax.ShapeDtypeStruct((tokens, width), BF16),
            jax.ShapeDtypeStruct((nw, pairs, 2, WINDOW), F32),
        ],
        [pltpu.VMEM((2, CELL, TSPAN * CELL), F32)],
        [triple, triple, triple, table, *kept],
        4 * tokens * WINDOW * width * 4 // parts,
        2 * tokens * 4 * width // parts,
        {5 + i: i for i in range(len(kept))},
    )


def attend_back(valid, triple, table, grad, logs):
    tokens = triple.shape[0]
    width = triple.shape[1] // 3
    nw = tokens // WINDOW
    pairs = width // (2 * HEAD)

    def body(
        nv, q_ref, k_ref, v_ref, t_ref, g_ref, l_ref, dq_ref, dk_ref, dv_ref, dt_ref, rows, drows
    ):
        w = pl.program_id(1)
        keep = lax.broadcasted_iota(jnp.int32, (WINDOW, 1), 0) < nv[w] * CELL
        dqs, dks, dvs = [], [], []

        @pl.when(w == 0)
        def _():
            for a in range(2):
                fill_table(t_ref.at[a], rows.at[a])
            drows[...] = jnp.zeros_like(drows)

        for a in range(2):
            cols = slice(a * HEAD, (a + 1) * HEAD)
            q = q_ref[:, cols] * jnp.asarray(HEAD**-0.5, BF16)
            k, g = k_ref[:, cols], g_ref[:, cols]
            s = mm(k, q, NT)
            s = jnp.where(keep, s + bias_rows(rows[a]), NEG)
            p = jnp.exp(s - l_ref[0, 0, a : a + 1, :])
            gp = mm(v_ref[:, cols], g, NT)
            delta = jnp.sum(gp * p, axis=0, keepdims=True)
            ds = jnp.where(keep, p * (gp - delta), 0.0).astype(BF16)
            dvs.append(mm(p.astype(BF16), g))
            dks.append(mm(ds, q))
            dqs.append(mm(k, ds, TN))
            wide = ds.astype(F32)
            for f in range(WIN_T):
                at = (WIN_T - 1 - f) * CELL
                drows[a, :, at : at + WINDOW] += wide[f * CELL : (f + 1) * CELL, :]
        scale = HEAD**-0.5
        dq_ref[...] = (jnp.concatenate(dqs, axis=0) * scale).T.astype(BF16)
        dk_ref[...] = jnp.concatenate(dks, axis=1).astype(BF16)
        dv_ref[...] = jnp.concatenate(dvs, axis=1).astype(BF16)

        @pl.when(w == nw - 1)
        def _():
            for a in range(2):
                fold_table(drows.at[a], dt_ref.at[a])

    q, k, v, t = attention_specs(pairs)
    one = pl.BlockSpec((WINDOW, 2 * HEAD), lambda h, w, nv: (w, h))
    return kernel_call(
        body,
        valid,
        (pairs, nw),
        [q, k, v, t, one, pl.BlockSpec((1, 1, 2, WINDOW), lambda h, w, nv: (w, h, 0, 0))],
        [one, one, one, t],
        [jax.ShapeDtypeStruct((tokens, width), BF16)] * 3
        + [jax.ShapeDtypeStruct((2 * pairs, WIN_S, TSPAN * LANES), F32)],
        [pltpu.VMEM((2, CELL, TSPAN * CELL), F32)] * 2,
        [triple, triple, triple, table, grad, logs],
        10 * tokens * WINDOW * width * 4,
        2 * tokens * 8 * width,
    )


def attention_out(idx, mixed, x, mod, keep, weight, bias):
    tokens, width = x.shape
    rows = WINDOW
    nref = weight.n_sems()

    def body(idx, mixed_ref, x_ref, mod_ref, keep_ref, bias_ref, *rest):
        w_refs, rest = rest[:nref], rest[nref:]
        att_ref, mid_ref, norm_ref, w_buf, acc, sems = rest

        @pl.when(pl.program_id(0) == 0)
        def _():
            copies = weight.whole(idx, w_refs, w_buf, sems)
            for c in copies:
                c.start()
            for c in copies:
                c.wait()

        acc[...] = mm(mixed_ref[...], w_buf[...])

        def chunk(i, _):
            r = pl.ds(pl.multiple_of(i * CHUNK, CHUNK), CHUNK)
            att = acc[r, :] + bias_ref[...]
            mid = x_ref[r, :].astype(F32) + keep_ref[r, :] * mod_ref[2:3, :] * att
            normed, _inv = norm_rows(mid)
            att_ref[r, :] = att.astype(BF16)
            mid_ref[r, :] = mid
            norm_ref[r, :] = (normed * (1.0 + mod_ref[4:5, :]) + mod_ref[3:4, :]).astype(BF16)
            return 0

        lax.fori_loop(0, rows // CHUNK, chunk, 0)

    block = pl.BlockSpec((rows, width), lambda w, idx: (w, 0))
    return kernel_call(
        body,
        idx,
        (tokens // rows,),
        [
            block,
            block,
            pl.BlockSpec((6, width), lambda w, idx: (0, 0)),
            pl.BlockSpec((rows, 1), lambda w, idx: (w, 0)),
            pl.BlockSpec((1, width), lambda w, idx: (0, 0)),
            *weight.specs(),
        ],
        [block, block, block],
        [
            jax.ShapeDtypeStruct((tokens, width), BF16),
            jax.ShapeDtypeStruct((tokens, width), F32),
            jax.ShapeDtypeStruct((tokens, width), BF16),
        ],
        [
            pltpu.VMEM((width, width), BF16),
            pltpu.VMEM((rows, width), F32),
            pltpu.SemaphoreType.DMA((nref,)),
        ],
        [mixed, x, mod, keep, bias, *weight.operands()],
        2 * tokens * width * width,
        tokens * width * 12 + 2 * width * width,
    )


def gelu_up(idx, norm_mid, weight, bias, part, parts, before=None):
    tokens, width = norm_mid.shape
    cols = weight.cols
    block = 512
    steps = cols // block // parts
    lo = part * steps
    kept = list(before) if before else []
    rows = tokens
    nw = tokens // rows
    nref = weight.n_sems()

    def body(idx, x_ref, bias_ref, *rest):
        w_refs = rest[:nref]
        act_ref, slope_ref, w_buf, sems = rest[-4:]
        j, w = pl.program_id(0), pl.program_id(1)

        @pl.when((j == 0) & (w == 0))
        def _():
            for s in range(steps):
                for c in weight.whole(idx, w_refs, w_buf, sems.at[s], (lo + s) * block, block):
                    c.start()

        for s in range(steps):

            @pl.when((j == s) & (w == 0))
            def _():
                for c in weight.whole(idx, w_refs, w_buf, sems.at[s], (lo + s) * block, block):
                    c.wait()

        a = x_ref[pl.ds(pl.multiple_of(w * rows, rows), rows), :]
        b = w_buf[:, pl.ds(pl.multiple_of((lo + j) * block, block), block)]
        h = mm(a, b) + bias_ref[...]
        square = h * h
        inner = GELU_C * h * (1.0 + GELU_A * square)
        th = jnp.tanh(inner)
        left = 0.5 * (1.0 + th)
        act_ref[...] = (h * left).astype(BF16)
        slope = left + 0.5 * h * (1.0 - th * th) * (GELU_C * (1.0 + 3.0 * GELU_A * square))
        slope_ref[...] = slope.astype(BF16)

    return kernel_call(
        body,
        idx,
        (steps, nw),
        [
            pl.BlockSpec((tokens, width), lambda j, w, idx: (0, 0)),
            pl.BlockSpec((1, block), lambda j, w, idx: (0, lo + j)),
            *weight.specs(),
            *[any_spec()] * len(kept),
        ],
        [pl.BlockSpec((rows, block), lambda j, w, idx: (w, lo + j))] * 2,
        [jax.ShapeDtypeStruct((tokens, cols), BF16)] * 2,
        [pltpu.VMEM((width, cols), BF16), pltpu.SemaphoreType.DMA((steps, nref))],
        [norm_mid, bias, *weight.operands(), *kept],
        2 * tokens * width * cols // parts,
        2 * (tokens * (width + 2 * cols) + width * cols) // parts,
        {3 + nref + i: i for i in range(len(kept))},
    )


def ffn_down(idx, activated, middle, cot, keep, gate, weight, bias):
    tokens, inner = activated.shape
    width = weight.cols
    block = 256
    steps = width // block
    rows = tokens
    nw = tokens // rows
    nref = weight.n_sems()

    def body(idx, act_ref, mid_ref, cot_ref, keep_ref, gate_ref, bias_ref, *rest):
        w_refs, rest = rest[:nref], rest[nref:]
        out_ref, gg_ref, w_buf, sems = rest
        j, w = pl.program_id(0), pl.program_id(1)

        @pl.when((j == 0) & (w == 0))
        def _():
            for s in range(steps):
                for c in weight.whole(idx, w_refs, w_buf, sems.at[s], s * block, block):
                    c.start()

        for s in range(steps):

            @pl.when((j == s) & (w == 0))
            def _():
                for c in weight.whole(idx, w_refs, w_buf, sems.at[s], s * block, block):
                    c.wait()

        a = act_ref[pl.ds(pl.multiple_of(w * rows, rows), rows), :]
        b = w_buf[:, pl.ds(pl.multiple_of(j * block, block), block)]
        ff = (mm(a, b) + bias_ref[...]) * keep_ref[...]
        out_ref[...] = (mid_ref[...] + ff * gate_ref[...]).astype(BF16)
        part = jnp.sum(ff * cot_ref[...].astype(F32), axis=0, keepdims=True)

        @pl.when(w == 0)
        def _():
            gg_ref[...] = part

        @pl.when(w > 0)
        def _():
            gg_ref[...] += part

    cell = pl.BlockSpec((rows, block), lambda j, w, idx: (w, j))
    line = pl.BlockSpec((1, block), lambda j, w, idx: (0, j))
    return kernel_call(
        body,
        idx,
        (steps, nw),
        [
            pl.BlockSpec((tokens, inner), lambda j, w, idx: (0, 0)),
            cell,
            cell,
            pl.BlockSpec((rows, 1), lambda j, w, idx: (w, 0)),
            line,
            line,
            *weight.specs(),
        ],
        [cell, line],
        [jax.ShapeDtypeStruct((tokens, width), BF16), jax.ShapeDtypeStruct((1, width), F32)],
        [pltpu.VMEM((inner, width), BF16), pltpu.SemaphoreType.DMA((steps, nref))],
        [activated, middle, cot, keep, gate, bias, *weight.operands()],
        2 * tokens * inner * width,
        2 * (tokens * (inner + 4 * width) + width * inner),
    )


def walk_rows(idx, refs, bufs, n):
    for ref, buf in zip(refs, bufs):
        size = buf.shape[0] // n
        for k in range(n):
            rows = pl.ds(pl.multiple_of(idx[k] * size, size), size)
            buf[k * size : (k + 1) * size, :] = ref[rows, :]


def half_specs(half, tokens, n):
    return [
        pl.BlockSpec((None, half, tokens), lambda j, idx: (idx[n], 0, 0)),
        pl.BlockSpec((None, half, tokens), lambda j, idx: (1 - idx[n], 0, 0)),
    ]


def down_outer(idx, left, right):
    _, half, tokens = left.shape
    n = idx.shape[0] - 1
    block = right.shape[1] // n

    def body(idx, mine_ref, other_ref, right_ref, keep_ref, send_ref):
        b = right_ref[...]
        send_ref[...] = mm(other_ref[...], b).astype(BF16)
        keep_ref[...] = mm(mine_ref[...], b).astype(BF16)

    out = pl.BlockSpec((None, half, block), lambda j, idx: (j, 0, 0))
    shape = jax.ShapeDtypeStruct((n, half, block), BF16)
    return kernel_call(
        body,
        idx,
        (n,),
        [
            *half_specs(half, tokens, n),
            pl.BlockSpec((tokens, block), lambda j, idx: (0, idx[j])),
        ],
        [out, out],
        [shape, shape],
        [],
        [left, left, right],
        4 * tokens * half * block * n,
        2 * (2 * half * tokens + tokens * block * n + 2 * half * block * n),
    )


def hidden_back(idx, grad_ffn, slope, norm_t, weight):
    tokens, width = grad_ffn.shape
    inner = slope.shape[1]
    block = weight.rows
    steps = weight.count + 1
    half = norm_t.shape[1]
    n = weight.count + 1
    nref = weight.n_sems()

    def body(idx, g_ref, slope_ref, mine_ref, other_ref, *rest):
        w_refs, rest = rest[:nref], rest[nref:]
        gh_ref, keep_ref, send_ref, sum_ref, w_buf, mine, other, sems = rest
        j = pl.program_id(0)

        def copies(s):
            return weight.piece(idx, w_refs, w_buf, sems, s, s * block, 0, width)

        @pl.when(j == 0)
        def _():
            for s in range(steps):
                for c in copies(s):
                    c.start()
            walk_rows(idx, (mine_ref, other_ref), (mine, other), n)

        for s in range(steps):

            @pl.when(j == s)
            def _():
                for c in copies(s):
                    c.wait()

        b = w_buf[pl.ds(pl.multiple_of(j * block, block), block), :]
        gh = (mm(g_ref[...], b, NT) * slope_ref[...].astype(F32)).astype(BF16)
        gh_ref[...] = gh
        sum_ref[...] = jnp.sum(gh.astype(F32), axis=0, keepdims=True)
        send_ref[...] = mm(other[...], gh).astype(BF16)
        keep_ref[...] = mm(mine[...], gh).astype(BF16)

    out = pl.BlockSpec((half, block), lambda j, idx: (0, idx[j]))
    return kernel_call(
        body,
        idx,
        (steps,),
        [
            pl.BlockSpec((tokens, width), lambda j, idx: (0, 0)),
            pl.BlockSpec((tokens, block), lambda j, idx: (0, idx[j])),
            *half_specs(half, tokens, n),
            *weight.specs(),
        ],
        [
            pl.BlockSpec((tokens, block), lambda j, idx: (0, idx[j])),
            out,
            out,
            pl.BlockSpec((1, block), lambda j, idx: (0, idx[j])),
        ],
        [
            jax.ShapeDtypeStruct((tokens, inner), BF16),
            jax.ShapeDtypeStruct((half, inner), BF16),
            jax.ShapeDtypeStruct((half, inner), BF16),
            jax.ShapeDtypeStruct((1, inner), F32),
        ],
        [
            pltpu.VMEM((inner, width), BF16),
            pltpu.VMEM((half, tokens), BF16),
            pltpu.VMEM((half, tokens), BF16),
            pltpu.SemaphoreType.DMA((nref,)),
        ],
        [grad_ffn, slope, norm_t, norm_t, *weight.operands()],
        8 * tokens * width * inner,
        2 * (tokens * (width + 2 * inner) + 2 * width * inner),
    )


def middle_back(idx, grad_hidden, middle, cot, attention, keep, mod, up, project):
    tokens, inner = grad_hidden.shape
    width = middle.shape[1]
    rows = WINDOW
    n_up, n_pr = up.n_sems(), project.n_sems()

    def body(idx, gh_ref, mid_ref, cot_ref, att_ref, keep_ref, mod_ref, *rest):
        up_refs, rest = rest[:n_up], rest[n_up:]
        pr_refs, rest = rest[:n_pr], rest[n_pr:]
        gm_ref, ga_ref, gx_ref, sum_ref, up_buf, pr_buf, acc, up_sems, pr_sems = rest

        @pl.when(pl.program_id(0) == 0)
        def _():
            first = up.whole(idx, up_refs, up_buf, up_sems)
            second = project.whole(idx, pr_refs, pr_buf, pr_sems)
            for c in first + second:
                c.start()
            sum_ref[...] = jnp.zeros_like(sum_ref)
            for c in first + second:
                c.wait()

        acc[...] = mm(gh_ref[...], up_buf[...], NT)

        def chunk(i, sums):
            r = pl.ds(pl.multiple_of(i * CHUNK, CHUNK), CHUNK)
            grad = acc[r, :]
            normed, inverse = norm_rows(mid_ref[r, :])
            whole = cot_ref[r, :].astype(F32) + norm_back(
                grad * (1.0 + mod_ref[4:5, :]), normed, inverse
            )
            gm_ref[r, :] = whole
            gated = keep_ref[r, :] * whole
            ga = (gated * mod_ref[2:3, :]).astype(BF16)
            ga_ref[r, :] = ga
            terms = (grad, grad * normed, gated * att_ref[r, :].astype(F32), ga.astype(F32))
            return tuple(
                s + jnp.sum(t.reshape(CHUNK // 8, 8, width), axis=0)
                for s, t in zip(sums, terms)
            )

        zero = jnp.zeros((8, width), F32)
        sums = lax.fori_loop(0, rows // CHUNK, chunk, (zero,) * 4)
        for i, s in enumerate(sums):
            sum_ref[i : i + 1, :] += jnp.sum(s, axis=0, keepdims=True)
        gx_ref[...] = mm(ga_ref[...], pr_buf[...], NT).astype(BF16)

    block = pl.BlockSpec((rows, width), lambda w, idx: (w, 0))
    return kernel_call(
        body,
        idx,
        (tokens // rows,),
        [
            pl.BlockSpec((rows, inner), lambda w, idx: (w, 0)),
            block,
            block,
            block,
            pl.BlockSpec((rows, 1), lambda w, idx: (w, 0)),
            pl.BlockSpec((6, width), lambda w, idx: (0, 0)),
            *up.specs(),
            *project.specs(),
        ],
        [block, block, block, pl.BlockSpec((4, width), lambda w, idx: (0, 0))],
        [
            jax.ShapeDtypeStruct((tokens, width), F32),
            jax.ShapeDtypeStruct((tokens, width), BF16),
            jax.ShapeDtypeStruct((tokens, width), BF16),
            jax.ShapeDtypeStruct((4, width), F32),
        ],
        [
            pltpu.VMEM((width, inner), BF16),
            pltpu.VMEM((width, width), BF16),
            pltpu.VMEM((rows, width), F32),
            pltpu.SemaphoreType.DMA((n_up,)),
            pltpu.SemaphoreType.DMA((n_pr,)),
        ],
        [grad_hidden, middle, cot, attention, keep, mod, *up.operands(), *project.operands()],
        2 * tokens * width * (inner + width),
        2 * (tokens * (inner + 8 * width) + width * (inner + width)),
    )


def input_back(idx, grads, x, grad_middle, mod, weight):
    tokens, width = x.shape
    rows = WINDOW
    nref = weight.n_sems()

    def body(idx, dq_ref, dk_ref, dv_ref, x_ref, gm_ref, mod_ref, *rest):
        w_refs, rest = rest[:nref], rest[nref:]
        out_ref, sum_ref, w_buf, acc, sems = rest

        @pl.when(pl.program_id(0) == 0)
        def _():
            copies = weight.whole(idx, w_refs, w_buf, sems)
            for c in copies:
                c.start()
            sum_ref[...] = jnp.zeros_like(sum_ref)
            for c in copies:
                c.wait()

        acc[...] = (
            mm(dq_ref[...], w_buf[:, 0:width], NT)
            + mm(dk_ref[...], w_buf[:, width : 2 * width], NT)
            + mm(dv_ref[...], w_buf[:, 2 * width : 3 * width], NT)
        )

        def chunk(i, sums):
            r = pl.ds(pl.multiple_of(i * CHUNK, CHUNK), CHUNK)
            grad = acc[r, :]
            normed, inverse = norm_rows(x_ref[r, :].astype(F32))
            back = norm_back(grad * (1.0 + mod_ref[1:2, :]), normed, inverse)
            out_ref[r, :] = (gm_ref[r, :] + back).astype(BF16)
            return tuple(
                s + jnp.sum(t.reshape(CHUNK // 8, 8, width), axis=0)
                for s, t in zip(sums, (grad, grad * normed))
            )

        zero = jnp.zeros((8, width), F32)
        sums = lax.fori_loop(0, rows // CHUNK, chunk, (zero,) * 2)
        for i, s in enumerate(sums):
            sum_ref[i : i + 1, :] += jnp.sum(s, axis=0, keepdims=True)

    block = pl.BlockSpec((rows, width), lambda w, idx: (w, 0))
    return kernel_call(
        body,
        idx,
        (tokens // rows,),
        [
            *([block] * 5),
            pl.BlockSpec((6, width), lambda w, idx: (0, 0)),
            *weight.specs(),
        ],
        [block, pl.BlockSpec((2, width), lambda w, idx: (0, 0))],
        [jax.ShapeDtypeStruct((tokens, width), BF16), jax.ShapeDtypeStruct((2, width), F32)],
        [
            pltpu.VMEM((width, 3 * width), BF16),
            pltpu.VMEM((rows, width), F32),
            pltpu.SemaphoreType.DMA((nref,)),
        ],
        [*grads, x, grad_middle, mod, *weight.operands()],
        6 * tokens * width * width,
        2 * (tokens * 9 * width + 3 * width * width),
    )


def last_outer(idx, norm_t, mixed_t, grads, grad_attention, block, other):
    _, half, tokens = norm_t.shape
    width = grad_attention.shape[1]
    per = width // block
    n = idx.shape[0] - 1

    def body(idx, *refs):
        ins, rest = refs[:6], refs[6:]
        out_ref, mine = rest[0], rest[-1]
        j = pl.program_id(0)

        @pl.when(j == 0)
        def _():
            walk_rows(idx, ins[0:1], (mine,), n)

        @pl.when(j == 3 * per)
        def _():
            walk_rows(idx, ins[1:2], (mine,), n)

        for part, ref in enumerate(ins[2:]):

            @pl.when(j // per == part)
            def _():
                b = ref[...]
                out_ref[...] = mm(mine[...], b).astype(BF16)
                if other:
                    rest[1][...] = jnp.sum(b.astype(F32), axis=0, keepdims=True)

    def part_spec(part):
        return pl.BlockSpec(
            (tokens, block), lambda j, idx: (0, jnp.clip(j - part * per, 0, per - 1))
        )

    left = half_specs(half, tokens, n)[1 if other else 0]
    out_specs = [pl.BlockSpec((half, block), lambda j, idx: (0, j))]
    out_shape = [jax.ShapeDtypeStruct((half, 4 * width), BF16)]
    if other:
        out_specs.append(pl.BlockSpec((1, block), lambda j, idx: (0, j)))
        out_shape.append(jax.ShapeDtypeStruct((1, 4 * width), F32))
    return kernel_call(
        body,
        idx,
        (4 * per,),
        [left, left, *(part_spec(p) for p in range(4))],
        out_specs,
        out_shape,
        [pltpu.VMEM((half, tokens), BF16)],
        [norm_t, mixed_t, *grads, grad_attention],
        8 * tokens * half * width,
        2 * (2 * half * tokens + 4 * tokens * width + 4 * half * width),
    )


def join_halves(idx, own, other, widths, turn=False):
    n = idx.shape[0] - 1
    half, cols = own.shape
    shapes = [(cols, CORES * half)] if turn else [(CORES * half, w) for w in widths]

    def body(idx, own_ref, other_ref, *outs):
        core = idx[n]
        for ref, place in ((own_ref, core), (other_ref, 1 - core)):
            at = pl.ds(pl.multiple_of(place * half, half), half)
            if turn:
                outs[0][:, at] = ref[...].astype(F32).T
            else:
                start = 0
                for out, w in zip(outs, widths):
                    out[at, :] = ref[:, start : start + w].astype(F32)
                    start += w

    whole = lambda shape: pl.BlockSpec(shape, lambda i, idx: (0, 0))
    return kernel_call(
        body,
        idx,
        (1,),
        [whole(own.shape), whole(own.shape)],
        [whole(shape) for shape in shapes],
        [jax.ShapeDtypeStruct(shape, F32) for shape in shapes],
        [],
        [own, other],
        3e10,
        8 * half * cols,
    )


def turn_half(idx, piece, own, before=None):
    n = idx.shape[0] - 1
    half, cols = piece.shape
    kept = [before] if before is not None else []

    def body(idx, ref, *rest):
        rest[-1][...] = ref[...].astype(F32).T

    return kernel_call(
        body,
        idx,
        (1,),
        [pl.BlockSpec((half, cols), lambda i, idx: (0, 0)), *[any_spec()] * len(kept)],
        [pl.BlockSpec((cols, half), lambda i, idx: (0, idx[n] if own else 1 - idx[n]))],
        [jax.ShapeDtypeStruct((cols, CORES * half), F32)],
        [],
        [piece, *kept],
        3e10,
        6 * half * cols,
        {2: 0} if kept else None,
    )[0]


def column_pick():
    pick = np.zeros((SPAN, SPAN, WIN_S, LANES // WIN_S, WIN_S), np.float32)
    for b in range(SPAN):
        for key in range(WIN_S):
            for query in range(WIN_S):
                pick[b, query - key + WIN_S - 1, key, b, query] = 1.0
    return jnp.asarray(pick.reshape(SPAN * SPAN, WIN_S * LANES))


def spread_table(table):
    heads = table.shape[0]
    wide = jnp.dot(
        table.reshape(heads * TSPAN, SPAN * SPAN), column_pick(), precision=lax.Precision.HIGHEST
    )
    wide = wide.reshape(heads, TSPAN, WIN_S, LANES).transpose(0, 2, 1, 3)
    return wide.reshape(heads, WIN_S, TSPAN * LANES)


def gather_table(grad):
    heads = grad.shape[0]
    wide = grad.reshape(heads, WIN_S, TSPAN, LANES).transpose(0, 2, 1, 3)
    wide = wide.reshape(heads * TSPAN, WIN_S * LANES)
    table = lax.dot_general(wide, column_pick(), NT, precision=lax.Precision.HIGHEST)
    return table.reshape(heads, TSPAN * SPAN * SPAN)


def window_rows(grid, groups):
    clips_here, frames, halves, rows, side, width = grid.shape
    periods = frames // WIN_T
    cells = grid.reshape(clips_here, periods, WIN_T, halves, rows, halves, WIN_S, width)
    cells = cells.transpose(0, 1, 3, 5, 2, 4, 6, 7)
    return cells.reshape(groups, -1, WIN_T, rows, WIN_S, width)


def window_back(pieces, shape):
    clips_here, frames, halves, rows, side, width = shape
    periods = frames // WIN_T
    cells = pieces.reshape(clips_here, periods, halves, halves, WIN_T, rows, WIN_S, width)
    return cells.transpose(0, 1, 4, 2, 5, 3, 6, 7).reshape(shape)


def to_windows(grid, groups):
    got = lax.all_to_all(
        window_rows(grid, groups), "win", split_axis=0, concat_axis=3, tiled=True
    )
    return got.reshape(-1, grid.shape[-1])


def from_windows(rows, per_dev, shape):
    out = lax.all_to_all(
        rows.reshape(1, per_dev, WIN_T, WIN_S, WIN_S, shape[-1]),
        "win",
        split_axis=3,
        concat_axis=0,
        tiled=True,
    )
    return window_back(out, shape)


def from_windows_apart(rows, per_dev, shape):
    groups = lax.axis_size("win")
    me = lax.axis_index("win")
    cells = rows.reshape(per_dev, WIN_T, groups, WIN_S // groups, WIN_S, shape[-1])
    out = jnp.zeros((groups, *cells.shape[:2], *cells.shape[3:]), rows.dtype)
    for k in range(groups):
        piece = lax.dynamic_index_in_dim(cells, me ^ k, 2, keepdims=False)
        if k:
            piece = lax.ppermute(piece, "win", [(w, w ^ k) for w in range(groups)])
        out = lax.dynamic_update_slice_in_dim(out, piece[None], me ^ k, 0)
    return window_back(out, shape)


def body(
    tokens,
    condition,
    frame_count,
    triple_weight,
    triple_bias,
    project_weight,
    project_bias,
    up_weight,
    up_bias,
    down_weight,
    down_bias,
    modulate_weight,
    modulate_bias,
    position_table,
    cotangent,
):
    width = tokens.shape[-1]
    n = lax.axis_size("clip")
    groups = lax.axis_size("win")
    halves = tokens.shape[2]
    per_time = tokens.shape[1] // WIN_T
    per_dev = per_time * halves * halves // groups
    count = per_dev * WINDOW
    ring = Ring(n)
    core = ring.core
    rows = width // n

    def half_of(shard):
        size = shard.shape[0] // CORES
        return lax.dynamic_slice_in_dim(shard, core * size, size, 0)

    def turned(v):
        v = v.reshape(count, n, CORES, rows // CORES).transpose(2, 1, 3, 0)
        return v.reshape(CORES, width // CORES, count)

    flat = lambda v: v.reshape(1, -1).astype(F32)
    split_rows = lambda g: g.reshape(n, rows // CORES, -1)
    swap = lambda g: lax.ppermute(g, "win", ring.swap)
    idx = ring.index
    steps = max(ring.steps(False))
    spare = lambda group, used: [group.step() for _ in range(used, steps)]

    first = jnp.concatenate([half_of(triple_weight), half_of(project_weight)], axis=1)
    group_a = Gather(ring, first, False)
    group_b = Gather(ring, half_of(up_weight), True)
    group_c = Gather(ring, half_of(down_weight), False)

    sigma = jax.nn.sigmoid(condition)
    group_a.step()
    tokens_here, condition_here = after((tokens, condition), first)
    vectors = [triple_bias, project_bias, up_bias, down_bias, modulate_bias]
    packed, ends = pack_rows(condition_here, vectors)
    small = ring.gather_small(packed.astype(BF16))
    x = to_windows(tokens_here, groups)
    cond_all, triple_b, project_b, up_b, down_b, modulate_b = (
        small[:, ends[i] : ends[i + 1]].reshape(n, -1)[:, : v.size]
        for i, v in enumerate([condition, *vectors])
    )
    triple_b, project_b, up_b, down_b = map(flat, (triple_b, project_b, up_b, down_b))
    bias_all = jnp.concatenate(
        [triple_b[:, :width], jnp.zeros((1, width), F32), triple_b[:, width:]], axis=1
    )
    cond_rows = lax.dynamic_slice_in_dim(cond_all, ring.rank * rows, rows, 1)
    mod = ring.scatter_small(mm(cond_rows, modulate_weight)) + modulate_b.reshape(-1).astype(F32)
    table = spread_table(position_table)
    mod = mod.reshape(6, width)
    stage([group_a])
    group_a.step()
    mod, table = stage([group_a], mod, table)

    window_id = lax.axis_index("win") * per_dev + jnp.arange(per_dev)
    start = window_id // (halves * halves) * WIN_T
    valid = jnp.clip(frame_count[0] - start, 0, WIN_T).astype(jnp.int32)
    keep = (jnp.arange(WINDOW)[None] // CELL < valid[:, None]).astype(F32).reshape(count, 1)
    group_a.step()
    x, bias_all = stage([group_a], x, bias_all)
    spare(group_a, 3)
    stage([group_a])
    triple_w = Weight(triple_weight, *group_a.pieces())
    project_w = Weight(project_weight, triple_w.own, triple_w.sib, 3 * width)

    (group_b.a, group_b.b), idx, valid = together(
        after((group_b.a, group_b.b), (group_a.a, group_a.b)), idx, valid
    )
    group_b.step()
    norm_in, triple, cotangent = stage(
        [group_b], *qkv_project(idx, x, mod, triple_w, bias_all), cotangent
    )
    group_b.step()
    cot = to_windows(cotangent, groups)
    half_mixed = attend(valid, triple, table, 0, 2)
    half_mixed = stage([group_b], *half_mixed)
    group_b.step()
    gate_two = mod[5:6]
    grad_ffn = (keep * cot.astype(F32) * gate_two).astype(BF16)
    mixed, logs = attend(valid, triple, table, 1, 2, half_mixed)
    mixed, logs, grad_ffn = stage([group_b], mixed, logs, grad_ffn)
    spare(group_b, 3)
    ffn_t = grad_ffn.T.reshape(CORES, width // CORES, count)
    attention, middle, norm_mid, ffn_t = stage(
        [group_b],
        *attention_out(idx, mixed, x, mod, keep, project_w, project_b),
        ffn_t,
    )
    up_w = Weight(up_weight, *group_b.pieces())

    group_c.a, group_c.b = after((group_c.a, group_c.b), (group_b.a, group_b.b))
    group_c.step()
    half_act = stage([group_c], *gelu_up(idx, norm_mid, up_w, up_b, 0, 2))
    group_c.step()
    activated, slope = stage([group_c], *gelu_up(idx, norm_mid, up_w, up_b, 1, 2, half_act))
    group_c.step()
    down_keep, down_send, norm_in, mixed, mid_rows = stage(
        [group_c], *down_outer(idx, ffn_t, activated), norm_in, mixed, norm_mid
    )
    down_got = swap(down_send)
    spare(group_c, 3)
    norm_t, mixed_t, mid_t = turned(norm_in), turned(mixed), turned(mid_rows)
    down_got, norm_t, mixed_t, mid_t = stage([group_c], down_got, norm_t, mixed_t, mid_t)
    down_w = Weight(down_weight, *group_c.pieces())

    sums_d = Scatter(ring, down_keep, down_got, False)
    grad_ffn, idx = stage([sums_d], after((grad_ffn, idx), (group_c.a, group_c.b)))[0]
    sums_d.step()
    down_bias_grad = jnp.sum(grad_ffn.astype(F32), axis=0)
    (grad_hidden, up_keep, up_send, up_bias_grad), idx = stage(
        [sums_d], hidden_back(idx, grad_ffn, slope, mid_t, down_w), idx
    )
    sums_u = Scatter(ring, split_rows(up_keep), swap(split_rows(up_send)), True)
    sums_d.step()
    (grad_middle, grad_attention, grad_mixed, mid_sums), idx, valid = stage(
        [sums_d, sums_u],
        middle_back(
            idx, grad_hidden, middle, cot, attention, keep, mod, up_w, project_w
        ),
        idx,
        valid,
    )
    grad_shift_two, grad_scale_two, grad_gate_one, project_bias_grad = mid_sums
    sums_d.step()
    sums_u.step()
    (*grads, grad_table), idx = stage(
        [sums_d, sums_u], attend_back(valid, triple, table, grad_mixed, logs), idx
    )
    for _ in range(3, steps):
        (idx,) = sums_d.step(idx)
    (idx,) = sums_u.step(idx)
    last = (norm_t, mixed_t, grads, grad_attention, 1024)
    (last_send, last_sums), idx = together(last_outer(idx, *last, True), idx)
    last_got = swap(split_rows(last_send))
    table_grad = gather_table(grad_table)
    last_keep, last_got, idx, table_grad = stage(
        [sums_d], last_outer(idx, *last, False)[0], last_got, idx, table_grad
    )
    inner = activated.shape[-1]
    sums_l = Scatter(ring, split_rows(last_keep), last_got, False)
    (idx,) = sums_l.step(idx)
    (idx,) = sums_u.step(idx)
    (result, grad_gate_two), idx, down_sum = stage(
        [sums_u, sums_l],
        ffn_down(idx, activated, middle, cot, keep, gate_two, down_w, down_b),
        idx,
        sums_d.start_finish(),
    )
    idx, down_sum, result = sums_l.step(idx, down_sum, result)
    for _ in range(3, steps):
        (idx,) = sums_u.step(idx)
    output = from_windows(result, per_dev, tokens.shape)
    (grad_rows, in_sums), output, down_parts = stage(
        [sums_l, sums_u],
        input_back(idx, grads, x, grad_middle, mod, triple_w),
        output,
        sums_d.finish(down_sum),
    )

    rows_of = lambda v: v.reshape(-1, LANES)
    grad_mod = jnp.concatenate(
        [in_sums, grad_gate_one[None], mid_sums[0:2], grad_gate_two], axis=0
    )
    here = jnp.arange(n)[:, None, None] == ring.rank
    spans = position_table.shape[1]
    wide = -(-spans // LANES) * LANES
    pieces = [
        rows_of(jnp.pad(table_grad, ((0, 0), (0, wide - spans)))),
        rows_of(last_sums[0, :width]),
        rows_of(last_sums[0, 2 * width : 3 * width]),
        rows_of(project_bias_grad),
        rows_of(up_bias_grad[0]),
        rows_of(down_bias_grad),
        jnp.where(here, rows_of(grad_mod)[None], 0.0).reshape(-1, LANES),
    ]
    ends = np.cumsum([0] + [p.shape[0] for p in pieces])
    pad = -int(ends[-1]) % (n * groups * 8)
    packed = jnp.concatenate(pieces + [jnp.zeros((pad, LANES), F32)])
    packed, idx = sums_l.step(packed, idx)
    packed, down_half, idx, down_other, input_grad = stage(
        [sums_l],
        ring.sum_part(packed),
        turn_half(idx, down_parts[0], True),
        idx,
        down_parts[1],
        from_windows_apart(grad_rows, per_dev, tokens.shape),
    )
    for _ in range(3, steps):
        packed, idx, sums_u.a, sums_u.b = sums_l.step(packed, idx, sums_u.a, sums_u.b)
    packed, down_weight_grad, up_sum, idx = stage(
        [sums_l],
        ring.share_parts(packed),
        turn_half(idx, down_other, False, down_half),
        sums_u.start_finish(),
        idx,
    )
    last_sum = sums_l.start_finish()
    (up_weight_grad,) = join_halves(idx, *sums_u.finish(up_sum), [inner])
    table_grad, *bias_grads, grad_mod = (packed[ends[i] : ends[i + 1]] for i in range(len(pieces)))
    table_grad = table_grad.reshape(-1, wide)[:, :spans]
    bias_grads = [jnp.concatenate(bias_grads[:2]), *bias_grads[2:]]
    bias_grads = [
        lax.dynamic_slice_in_dim(g.reshape(-1), ring.rank * (g.size // n), g.size // n)
        for g in bias_grads
    ]
    grad_mod = grad_mod.reshape(n, -1).astype(BF16)
    modulate_weight_grad = mm(cond_rows, grad_mod, TN)
    modulate_bias_grad = lax.dynamic_slice_in_dim(
        jnp.sum(grad_mod.astype(F32), axis=0), ring.rank * (6 * rows), 6 * rows
    )
    back = lax.all_to_all(mm(grad_mod, modulate_weight, NT), "clip", 0, 0, tiled=True)
    condition_grad = back.reshape(1, width) * (sigma * (1.0 + condition * (1.0 - sigma)))
    last_sum, condition_grad, up_weight_grad, table_grad, bias_grads = together(
        last_sum, condition_grad, up_weight_grad, table_grad, bias_grads
    )
    triple_weight_grad, project_weight_grad = join_halves(
        idx, *sums_l.finish(last_sum), [3 * width, width]
    )
    triple_bias_grad, project_bias_grad, up_bias_grad, down_bias_grad = bias_grads
    return (
        output,
        input_grad,
        condition_grad,
        triple_weight_grad,
        triple_bias_grad,
        project_weight_grad,
        project_bias_grad,
        up_weight_grad,
        up_bias_grad,
        down_weight_grad,
        down_bias_grad,
        modulate_weight_grad,
        modulate_bias_grad,
        table_grad,
    )


def solution(mesh):
    grid = P("clip", None, None, "win", None, None)
    matrix, vector = P("clip", None), P("clip")
    placed = (
        grid,
        matrix,
        vector,
        matrix,
        vector,
        matrix,
        vector,
        matrix,
        vector,
        matrix,
        vector,
        matrix,
        vector,
        P(),
        grid,
    )
    return jax.shard_map(
        body,
        mesh=mesh,
        in_specs=placed,
        out_specs=(grid, grid, *placed[1:2], *placed[3:14]),
        check_vma=False,
    )
```

```python
import math
import jax
import jax.numpy as jnp
import numpy as np
from jax import lax
from jax.experimental import pallas as pl
from jax.experimental.pallas import tpu as pltpu
from jax.sharding import PartitionSpec as P

WIN_T = 5
WIN_S = 8
WINDOW = WIN_T * WIN_S * WIN_S
CELL = WIN_S * WIN_S
SPAN = 2 * WIN_S - 1
TSPAN = 2 * WIN_T - 1
HEAD = 64
LANES = 128
CORES = 2
EPS = 1e-06
NEG = -30000.0
GELU_C = math.sqrt(2.0 / math.pi)
GELU_A = 0.044715
F32 = jnp.float32
BF16 = jnp.bfloat16
VMEM_SPARE = 58 * 1024 * 1024

NN = (((1,), (0,)), ((), ()))
NT = (((1,), (1,)), ((), ()))
TN = (((0,), (0,)), ((), ()))


def mm(a, b, dims=NN):
    return lax.dot_general(a, b, dims, preferred_element_type=F32)


def any_spec():
    return pl.BlockSpec(memory_space=pl.ANY)


def vmem_need(specs, shapes, scratch):
    total = VMEM_SPARE
    for spec, shape in zip(specs, shapes):
        if spec.block_shape is not None:
            block = [b for b in spec.block_shape if b is not None]
            total += 2 * math.prod(block) * max(shape.dtype.itemsize, 2)
    for ref in scratch:
        if ref.memory_space == pltpu.VMEM:
            total += math.prod(ref.shape) * np.dtype(ref.dtype).itemsize
    return total


def ring_order(n):
    ny = 1 << (int(math.log2(n)) // 2)
    nz = n // ny
    if ny < 2 or nz % 2:
        return list(range(n))
    walk = []
    for z in range(nz):
        ys = list(range(1, ny))
        walk += [z * ny + y for y in (ys if z % 2 == 0 else ys[::-1])]
    return walk + [z * ny for z in reversed(range(nz))]


def after(value, *deps):
    return together(value, *deps)[0]


def together(*values):
    flat, tree = jax.tree.flatten(values)
    return jax.tree.unflatten(tree, lax.optimization_barrier(flat))


def stage(groups, *values):
    states = [(g.a, g.b) for g in groups]
    states, values = together(states, values)
    for g, (a, b) in zip(groups, states):
        g.settle(a, b)
    return values


class Ring:
    def __init__(self, n):
        self.n = n
        order = ring_order(n)
        self.rank = lax.axis_index("clip")
        self.core = lax.axis_index("win") % CORES
        self.up = [(order[i], order[(i + 1) % n]) for i in range(n)]
        self.down = [(b, a) for a, b in self.up]
        rows = [
            [order[(order.index(r) + k) % n] for k in range(n)] + [c]
            for r in range(n)
            for c in range(CORES)
        ]
        self.index = lax.dynamic_slice_in_dim(
            jnp.asarray(np.array(rows, np.int32)), self.rank * CORES + self.core, 1, 0
        ).reshape(n + 1)
        wins = lax.axis_size("win")
        self.swap = [(w, w ^ 1) for w in range(wins)]
        powers = [1 << i for i in range(8)]
        self.pairs = [[(w, w ^ k) for w in range(wins)] for k in powers if k < wins]
        self.across = self.pairs[1:]

    def steps(self, flip):
        far, near = self.n // 2, (self.n - 1) // 2
        return (near, far) if flip else (far, near)

    def gather_small(self, row):
        return lax.all_to_all(jnp.broadcast_to(row[None], (self.n, *row.shape)), "clip", 0, 0)

    def scatter_small(self, block):
        return jnp.sum(lax.all_to_all(block, "clip", 0, 0, tiled=True), axis=0)

    def sum_win(self, row):
        wins = lax.axis_size("win")
        return jnp.sum(
            lax.all_to_all(jnp.broadcast_to(row[None], (wins, *row.shape)), "win", 0, 0), axis=0
        )

    def sum_part(self, rows):
        devices = self.n * lax.axis_size("win")
        rows = rows.reshape(devices, -1, LANES)
        return jnp.sum(lax.all_to_all(rows, ("clip", "win"), 0, 0, tiled=True), axis=0)

    def share_parts(self, part):
        devices = self.n * lax.axis_size("win")
        part = jnp.broadcast_to(part[None], (devices, *part.shape))
        return lax.all_to_all(part, ("clip", "win"), 0, 0).reshape(-1, LANES)


class Gather:
    def __init__(self, ring, piece, flip):
        self.ring, self.ahead, self.back = ring, [], []
        self.far, self.near = ring.steps(flip)
        self.a = self.b = piece
        self.swapped = {}

    def step(self):
        ring = self.ring
        s = max(len(self.ahead), len(self.back))
        if s < self.far:
            self.a = lax.ppermute(self.a, "clip", ring.up)
            self.ahead.append(self.a)
        if s < self.near:
            self.b = lax.ppermute(self.b, "clip", ring.down)
            self.back.append(self.b)

    def settle(self, a, b):
        self.a, self.b = a, b
        if self.ahead:
            self.ahead[-1] = a
        if self.back:
            self.back[-1] = b

    def pieces(self):
        own = self.back + self.ahead[::-1]
        return own, [lax.ppermute(o, "win", self.ring.swap) for o in own]


class Scatter:
    def __init__(self, ring, keep, got, flip):
        self.ring, self.keep, self.got = ring, keep, got
        self.far, self.near = ring.steps(flip)
        self.a, self.b = self.part(self.far).astype(BF16), self.part(-self.near).astype(BF16)
        self.s = 0

    def part(self, k):
        k = k % self.ring.n
        return self.keep[k].astype(F32) + self.got[k].astype(F32)

    def step(self, *values):
        s, far, near = self.s, self.far, self.near
        if 0 < s < far:
            self.a = (self.a.astype(F32) + self.part(far - s)).astype(BF16)
        if 0 < s < near:
            self.b = (self.b.astype(F32) + self.part(s - near)).astype(BF16)
        if values:
            (self.a, self.b), *values = together((self.a, self.b), *values)
        if s < far:
            self.a = lax.ppermute(self.a, "clip", self.ring.up)
        if s < near:
            self.b = lax.ppermute(self.b, "clip", self.ring.down)
        self.s += 1
        return values

    def settle(self, a, b):
        self.a, self.b = a, b

    def start_finish(self):
        ring = self.ring
        total = (self.part(0) + self.a.astype(F32) + self.b.astype(F32)).astype(BF16)
        for perm in ring.across:
            other = lax.ppermute(total, "win", perm)
            total = (total.astype(F32) + other.astype(F32)).astype(BF16)
        return total

    def finish(self, total):
        return total, lax.ppermute(total, "win", self.ring.swap)


class Weight:
    def __init__(self, local, own, sib, col=0):
        self.local, self.own, self.sib, self.col = local, own, sib, col
        self.rows, self.cols = local.shape
        self.count = len(own)

    def operands(self):
        return [self.local, *self.own, *self.sib]

    def specs(self):
        return [any_spec()] * (1 + 2 * self.count)

    def shape(self):
        return (self.rows * (self.count + 1), self.cols)

    def n_sems(self):
        return 2 * self.count + 1

    def piece(self, idx, refs, dst, sems, i, base, start, width):
        half = self.rows // 2
        cols = pl.ds(start, width)
        into = pl.ds(start, width)
        if i == 0:
            rows = pl.ds(pl.multiple_of(base, self.rows), self.rows)
            return [
                pltpu.make_async_copy(refs[0].at[:, cols], dst.at[rows, into], sems.at[0])
            ]
        from_cols = pl.ds(self.col + start, width)
        core = idx[self.count + 1]
        copies = []
        for which, place in ((0, core), (1, 1 - core)):
            slot = which * self.count + i
            rows = pl.ds(pl.multiple_of(base + place * half, half), half)
            copies.append(
                pltpu.make_async_copy(
                    refs[slot].at[:, from_cols], dst.at[rows, into], sems.at[slot]
                )
            )
        return copies

    def whole(self, idx, refs, dst, sems, start=0, width=None):
        copies = []
        for i in range(self.count + 1):
            copies += self.piece(
                idx, refs, dst, sems, i, idx[i] * self.rows, start, width or self.cols
            )
        return copies


def kernel_call(
    body, idx, grid, in_specs, out_specs, out_shape, scratch, operands, flops, nbytes, aliases=None
):
    return pl.pallas_call(
        body,
        grid_spec=pltpu.PrefetchScalarGridSpec(
            num_scalar_prefetch=1,
            grid=grid,
            in_specs=in_specs,
            out_specs=out_specs,
            scratch_shapes=scratch,
        ),
        out_shape=out_shape,
        input_output_aliases=aliases or {},
        compiler_params=pltpu.CompilerParams(
            dimension_semantics=("arbitrary",) * len(grid),
            vmem_limit_bytes=VMEM_SPARE + 0 * vmem_need(
                [*in_specs, *out_specs], [*operands, *out_shape], scratch
            ),
        ),
        cost_estimate=pl.CostEstimate(
            flops=int(flops), bytes_accessed=int(nbytes), transcendentals=0
        ),
    )(idx, *operands)


def norm_rows(v):
    center = v - jnp.mean(v, axis=-1, keepdims=True)
    inverse = lax.rsqrt(jnp.mean(center * center, axis=-1, keepdims=True) + EPS)
    return center * inverse, inverse


def norm_back(grad, normed, inverse):
    mean_grad = jnp.mean(grad, axis=-1, keepdims=True)
    mean_cross = jnp.mean(grad * normed, axis=-1, keepdims=True)
    return inverse * (grad - mean_grad - normed * mean_cross)


CHUNK = 64


def pack_rows(condition, vectors):
    lined = lambda v: jnp.pad(v, (0, -v.size % LANES)).reshape(-1, LANES)
    operands = [condition.reshape(-1, LANES), *(lined(v) for v in vectors)]
    ends = np.cumsum([0] + [v.shape[0] for v in operands])

    def body(*refs):
        out_ref = refs[-1]
        for i, ref in enumerate(refs[:-1]):
            v = ref[...].astype(F32)
            if i == 0:
                v = v / (1.0 + jnp.exp(-v))
            out_ref[ends[i] : ends[i + 1], :] = v.astype(BF16).astype(F32)

    rows = pl.pallas_call(
        body, out_shape=jax.ShapeDtypeStruct((int(ends[-1]), LANES), F32)
    )(*operands)
    return rows, ends


def qkv_project(idx, x, mod, weight, bias):
    tokens, width = x.shape
    cols = weight.cols
    block = 512
    steps = cols // block
    rows = tokens
    nw = tokens // rows
    nref = weight.n_sems()

    def body(idx, x_ref, mod_ref, bias_ref, *rest):
        w_refs, rest = rest[:nref], rest[nref:]
        norm_ref, out_ref, w_buf, sems = rest
        j, w = pl.program_id(0), pl.program_id(1)

        @pl.when((j == 0) & (w == 0))
        def _():
            for s in range(steps):
                for c in weight.whole(idx, w_refs, w_buf, sems.at[s], s * block, block):
                    c.start()

            def chunk(i, _):
                r = pl.ds(pl.multiple_of(i * CHUNK, CHUNK), CHUNK)
                normed, _inv = norm_rows(x_ref[r, :].astype(F32))
                norm_ref[r, :] = (normed * (1.0 + mod_ref[1:2, :]) + mod_ref[0:1, :]).astype(BF16)
                return 0

            lax.fori_loop(0, tokens // CHUNK, chunk, 0)

        for s in range(steps):

            @pl.when((j == s) & (w == 0))
            def _():
                for c in weight.whole(idx, w_refs, w_buf, sems.at[s], s * block, block):
                    c.wait()

        a = norm_ref[pl.ds(pl.multiple_of(w * rows, rows), rows), :]
        b = w_buf[:, pl.ds(pl.multiple_of(j * block, block), block)]
        out_ref[...] = (mm(a, b) + bias_ref[...]).astype(BF16)

    return kernel_call(
        body,
        idx,
        (steps, nw),
        [
            pl.BlockSpec((tokens, width), lambda j, w, idx: (0, 0)),
            pl.BlockSpec((6, width), lambda j, w, idx: (0, 0)),
            pl.BlockSpec((1, block), lambda j, w, idx: (0, j)),
            *weight.specs(),
        ],
        [
            pl.BlockSpec((tokens, width), lambda j, w, idx: (0, 0)),
            pl.BlockSpec((rows, block), lambda j, w, idx: (w, j)),
        ],
        [
            jax.ShapeDtypeStruct((tokens, width), BF16),
            jax.ShapeDtypeStruct((tokens, cols), BF16),
        ],
        [pltpu.VMEM((width, cols), BF16), pltpu.SemaphoreType.DMA((steps, nref))],
        [x, mod, bias, *weight.operands()],
        2 * tokens * width * cols,
        2 * (tokens * (2 * width + cols) + width * cols),
    )


def fill_table(near, rows):
    for y in range(WIN_S):
        for f in range(TSPAN):
            at = f * LANES + (WIN_S - 1 - y) * WIN_S
            rows[y * WIN_S : (y + 1) * WIN_S, f * CELL : (f + 1) * CELL] = near[:, at : at + CELL]


def fold_table(rows, near):
    near[...] = jnp.zeros_like(near)
    for y in range(WIN_S):
        for f in range(TSPAN):
            at = f * LANES + (WIN_S - 1 - y) * WIN_S
            near[:, at : at + CELL] += rows[y * WIN_S : (y + 1) * WIN_S, f * CELL : (f + 1) * CELL]


def bias_rows(table):
    return jnp.concatenate(
        [table[:, (WIN_T - 1 - f) * CELL : (WIN_T - 1 - f) * CELL + WINDOW] for f in range(WIN_T)],
        axis=0,
    )


def attention_specs(pairs, lo=0):
    q = pl.BlockSpec((WINDOW, 2 * HEAD), lambda h, w, nv: (w, lo + h))
    k = pl.BlockSpec((WINDOW, 2 * HEAD), lambda h, w, nv: (w, pairs + lo + h))
    v = pl.BlockSpec((WINDOW, 2 * HEAD), lambda h, w, nv: (w, 2 * pairs + lo + h))
    t = pl.BlockSpec((2, WIN_S, TSPAN * LANES), lambda h, w, nv: (lo + h, 0, 0))
    return q, k, v, t


def attend(valid, triple, table, part, parts, before=None):
    tokens = triple.shape[0]
    width = triple.shape[1] // 3
    nw = tokens // WINDOW
    pairs = width // (2 * HEAD)
    here = pairs // parts
    lo = part * here

    def body(nv, q_ref, k_ref, v_ref, t_ref, *rest):
        o_ref, l_ref, rows = rest[-3:]
        w = pl.program_id(1)
        keep = lax.broadcasted_iota(jnp.int32, (WINDOW, 1), 0) < nv[w] * CELL

        @pl.when(w == 0)
        def _():
            for a in range(2):
                fill_table(t_ref.at[a], rows.at[a])

        outs = []
        for a in range(2):
            cols = slice(a * HEAD, (a + 1) * HEAD)
            q = q_ref[:, cols] * jnp.asarray(HEAD**-0.5, BF16)
            s = mm(k_ref[:, cols], q, NT)
            s = jnp.where(keep, s + bias_rows(rows[a]), NEG)
            peak = jnp.max(s, axis=0, keepdims=True)
            e = jnp.exp(s - peak)
            total = jnp.sum(e, axis=0, keepdims=True)
            p = (e * (1.0 / total)).astype(BF16)
            l_ref[0, 0, a : a + 1, :] = peak + jnp.log(total)
            outs.append(mm(v_ref[:, cols], p, TN))
        o_ref[...] = jnp.concatenate(outs, axis=0).T.astype(BF16)

    kept = list(before) if before else []
    return kernel_call(
        body,
        valid,
        (here, nw),
        [*attention_specs(pairs, lo), *[any_spec()] * len(kept)],
        [
            pl.BlockSpec((WINDOW, 2 * HEAD), lambda h, w, nv: (w, lo + h)),
            pl.BlockSpec((1, 1, 2, WINDOW), lambda h, w, nv: (w, lo + h, 0, 0)),
        ],
        [
            jax.ShapeDtypeStruct((tokens, width), BF16),
            jax.ShapeDtypeStruct((nw, pairs, 2, WINDOW), F32),
        ],
        [pltpu.VMEM((2, CELL, TSPAN * CELL), F32)],
        [triple, triple, triple, table, *kept],
        4 * tokens * WINDOW * width * 4 // parts,
        2 * tokens * 4 * width // parts,
        {5 + i: i for i in range(len(kept))},
    )


def attend_back(valid, triple, table, grad, logs):
    tokens = triple.shape[0]
    width = triple.shape[1] // 3
    nw = tokens // WINDOW
    pairs = width // (2 * HEAD)

    def body(
        nv, q_ref, k_ref, v_ref, t_ref, g_ref, l_ref, dq_ref, dk_ref, dv_ref, dt_ref, rows, drows
    ):
        w = pl.program_id(1)
        keep = lax.broadcasted_iota(jnp.int32, (WINDOW, 1), 0) < nv[w] * CELL
        dqs, dks, dvs = [], [], []

        @pl.when(w == 0)
        def _():
            for a in range(2):
                fill_table(t_ref.at[a], rows.at[a])
            drows[...] = jnp.zeros_like(drows)

        for a in range(2):
            cols = slice(a * HEAD, (a + 1) * HEAD)
            q = q_ref[:, cols] * jnp.asarray(HEAD**-0.5, BF16)
            k, g = k_ref[:, cols], g_ref[:, cols]
            s = mm(k, q, NT)
            s = jnp.where(keep, s + bias_rows(rows[a]), NEG)
            p = jnp.exp(s - l_ref[0, 0, a : a + 1, :])
            gp = mm(v_ref[:, cols], g, NT)
            delta = jnp.sum(gp * p, axis=0, keepdims=True)
            ds = jnp.where(keep, p * (gp - delta), 0.0).astype(BF16)
            dvs.append(mm(p.astype(BF16), g))
            dks.append(mm(ds, q))
            dqs.append(mm(k, ds, TN))
            wide = ds.astype(F32)
            for f in range(WIN_T):
                at = (WIN_T - 1 - f) * CELL
                drows[a, :, at : at + WINDOW] += wide[f * CELL : (f + 1) * CELL, :]
        scale = HEAD**-0.5
        dq_ref[...] = (jnp.concatenate(dqs, axis=0) * scale).T.astype(BF16)
        dk_ref[...] = jnp.concatenate(dks, axis=1).astype(BF16)
        dv_ref[...] = jnp.concatenate(dvs, axis=1).astype(BF16)

        @pl.when(w == nw - 1)
        def _():
            for a in range(2):
                fold_table(drows.at[a], dt_ref.at[a])

    q, k, v, t = attention_specs(pairs)
    one = pl.BlockSpec((WINDOW, 2 * HEAD), lambda h, w, nv: (w, h))
    return kernel_call(
        body,
        valid,
        (pairs, nw),
        [q, k, v, t, one, pl.BlockSpec((1, 1, 2, WINDOW), lambda h, w, nv: (w, h, 0, 0))],
        [one, one, one, t],
        [jax.ShapeDtypeStruct((tokens, width), BF16)] * 3
        + [jax.ShapeDtypeStruct((2 * pairs, WIN_S, TSPAN * LANES), F32)],
        [pltpu.VMEM((2, CELL, TSPAN * CELL), F32)] * 2,
        [triple, triple, triple, table, grad, logs],
        10 * tokens * WINDOW * width * 4,
        2 * tokens * 8 * width,
    )


def attention_out(idx, mixed, x, mod, keep, weight, bias):
    tokens, width = x.shape
    rows = WINDOW
    nref = weight.n_sems()

    def body(idx, mixed_ref, x_ref, mod_ref, keep_ref, bias_ref, *rest):
        w_refs, rest = rest[:nref], rest[nref:]
        att_ref, mid_ref, norm_ref, w_buf, acc, sems = rest

        @pl.when(pl.program_id(0) == 0)
        def _():
            copies = weight.whole(idx, w_refs, w_buf, sems)
            for c in copies:
                c.start()
            for c in copies:
                c.wait()

        acc[...] = mm(mixed_ref[...], w_buf[...])

        def chunk(i, _):
            r = pl.ds(pl.multiple_of(i * CHUNK, CHUNK), CHUNK)
            att = acc[r, :] + bias_ref[...]
            mid = x_ref[r, :].astype(F32) + keep_ref[r, :] * mod_ref[2:3, :] * att
            normed, _inv = norm_rows(mid)
            att_ref[r, :] = att.astype(BF16)
            mid_ref[r, :] = mid
            norm_ref[r, :] = (normed * (1.0 + mod_ref[4:5, :]) + mod_ref[3:4, :]).astype(BF16)
            return 0

        lax.fori_loop(0, rows // CHUNK, chunk, 0)

    block = pl.BlockSpec((rows, width), lambda w, idx: (w, 0))
    return kernel_call(
        body,
        idx,
        (tokens // rows,),
        [
            block,
            block,
            pl.BlockSpec((6, width), lambda w, idx: (0, 0)),
            pl.BlockSpec((rows, 1), lambda w, idx: (w, 0)),
            pl.BlockSpec((1, width), lambda w, idx: (0, 0)),
            *weight.specs(),
        ],
        [block, block, block],
        [
            jax.ShapeDtypeStruct((tokens, width), BF16),
            jax.ShapeDtypeStruct((tokens, width), F32),
            jax.ShapeDtypeStruct((tokens, width), BF16),
        ],
        [
            pltpu.VMEM((width, width), BF16),
            pltpu.VMEM((rows, width), F32),
            pltpu.SemaphoreType.DMA((nref,)),
        ],
        [mixed, x, mod, keep, bias, *weight.operands()],
        2 * tokens * width * width,
        tokens * width * 12 + 2 * width * width,
    )


def gelu_up(idx, norm_mid, weight, bias, part, parts, before=None):
    tokens, width = norm_mid.shape
    cols = weight.cols
    block = 512
    steps = cols // block // parts
    lo = part * steps
    kept = list(before) if before else []
    rows = tokens
    nw = tokens // rows
    nref = weight.n_sems()

    def body(idx, x_ref, bias_ref, *rest):
        w_refs = rest[:nref]
        act_ref, slope_ref, w_buf, sems = rest[-4:]
        j, w = pl.program_id(0), pl.program_id(1)

        @pl.when((j == 0) & (w == 0))
        def _():
            for s in range(steps):
                for c in weight.whole(idx, w_refs, w_buf, sems.at[s], (lo + s) * block, block):
                    c.start()

        for s in range(steps):

            @pl.when((j == s) & (w == 0))
            def _():
                for c in weight.whole(idx, w_refs, w_buf, sems.at[s], (lo + s) * block, block):
                    c.wait()

        a = x_ref[pl.ds(pl.multiple_of(w * rows, rows), rows), :]
        b = w_buf[:, pl.ds(pl.multiple_of((lo + j) * block, block), block)]
        h = mm(a, b) + bias_ref[...]
        square = h * h
        inner = GELU_C * h * (1.0 + GELU_A * square)
        th = jnp.tanh(inner)
        left = 0.5 * (1.0 + th)
        act_ref[...] = (h * left).astype(BF16)
        slope = left + 0.5 * h * (1.0 - th * th) * (GELU_C * (1.0 + 3.0 * GELU_A * square))
        slope_ref[...] = slope.astype(BF16)

    return kernel_call(
        body,
        idx,
        (steps, nw),
        [
            pl.BlockSpec((tokens, width), lambda j, w, idx: (0, 0)),
            pl.BlockSpec((1, block), lambda j, w, idx: (0, lo + j)),
            *weight.specs(),
            *[any_spec()] * len(kept),
        ],
        [pl.BlockSpec((rows, block), lambda j, w, idx: (w, lo + j))] * 2,
        [jax.ShapeDtypeStruct((tokens, cols), BF16)] * 2,
        [pltpu.VMEM((width, cols), BF16), pltpu.SemaphoreType.DMA((steps, nref))],
        [norm_mid, bias, *weight.operands(), *kept],
        2 * tokens * width * cols // parts,
        2 * (tokens * (width + 2 * cols) + width * cols) // parts,
        {3 + nref + i: i for i in range(len(kept))},
    )


def ffn_down(idx, activated, middle, cot, keep, gate, weight, bias):
    tokens, inner = activated.shape
    width = weight.cols
    block = 256
    steps = width // block
    rows = tokens
    nw = tokens // rows
    nref = weight.n_sems()

    def body(idx, act_ref, mid_ref, cot_ref, keep_ref, gate_ref, bias_ref, *rest):
        w_refs, rest = rest[:nref], rest[nref:]
        out_ref, gg_ref, w_buf, sems = rest
        j, w = pl.program_id(0), pl.program_id(1)

        @pl.when((j == 0) & (w == 0))
        def _():
            for s in range(steps):
                for c in weight.whole(idx, w_refs, w_buf, sems.at[s], s * block, block):
                    c.start()

        for s in range(steps):

            @pl.when((j == s) & (w == 0))
            def _():
                for c in weight.whole(idx, w_refs, w_buf, sems.at[s], s * block, block):
                    c.wait()

        a = act_ref[pl.ds(pl.multiple_of(w * rows, rows), rows), :]
        b = w_buf[:, pl.ds(pl.multiple_of(j * block, block), block)]
        ff = (mm(a, b) + bias_ref[...]) * keep_ref[...]
        out_ref[...] = (mid_ref[...] + ff * gate_ref[...]).astype(BF16)
        part = jnp.sum(ff * cot_ref[...].astype(F32), axis=0, keepdims=True)

        @pl.when(w == 0)
        def _():
            gg_ref[...] = part

        @pl.when(w > 0)
        def _():
            gg_ref[...] += part

    cell = pl.BlockSpec((rows, block), lambda j, w, idx: (w, j))
    line = pl.BlockSpec((1, block), lambda j, w, idx: (0, j))
    return kernel_call(
        body,
        idx,
        (steps, nw),
        [
            pl.BlockSpec((tokens, inner), lambda j, w, idx: (0, 0)),
            cell,
            cell,
            pl.BlockSpec((rows, 1), lambda j, w, idx: (w, 0)),
            line,
            line,
            *weight.specs(),
        ],
        [cell, line],
        [jax.ShapeDtypeStruct((tokens, width), BF16), jax.ShapeDtypeStruct((1, width), F32)],
        [pltpu.VMEM((inner, width), BF16), pltpu.SemaphoreType.DMA((steps, nref))],
        [activated, middle, cot, keep, gate, bias, *weight.operands()],
        2 * tokens * inner * width,
        2 * (tokens * (inner + 4 * width) + width * inner),
    )


def walk_rows(idx, refs, bufs, n):
    for ref, buf in zip(refs, bufs):
        size = buf.shape[0] // n
        for k in range(n):
            rows = pl.ds(pl.multiple_of(idx[k] * size, size), size)
            buf[k * size : (k + 1) * size, :] = ref[rows, :]


def half_specs(half, tokens, n):
    return [
        pl.BlockSpec((None, half, tokens), lambda j, idx: (idx[n], 0, 0)),
        pl.BlockSpec((None, half, tokens), lambda j, idx: (1 - idx[n], 0, 0)),
    ]


def down_outer(idx, left, right):
    _, half, tokens = left.shape
    n = idx.shape[0] - 1
    block = right.shape[1] // n

    def body(idx, mine_ref, other_ref, right_ref, keep_ref, send_ref):
        b = right_ref[...]
        send_ref[...] = mm(other_ref[...], b).astype(BF16)
        keep_ref[...] = mm(mine_ref[...], b).astype(BF16)

    out = pl.BlockSpec((None, half, block), lambda j, idx: (j, 0, 0))
    shape = jax.ShapeDtypeStruct((n, half, block), BF16)
    return kernel_call(
        body,
        idx,
        (n,),
        [
            *half_specs(half, tokens, n),
            pl.BlockSpec((tokens, block), lambda j, idx: (0, idx[j])),
        ],
        [out, out],
        [shape, shape],
        [],
        [left, left, right],
        4 * tokens * half * block * n,
        2 * (2 * half * tokens + tokens * block * n + 2 * half * block * n),
    )


def hidden_back(idx, grad_ffn, slope, norm_t, weight):
    tokens, width = grad_ffn.shape
    inner = slope.shape[1]
    block = weight.rows
    steps = weight.count + 1
    half = norm_t.shape[1]
    n = weight.count + 1
    nref = weight.n_sems()

    def body(idx, g_ref, slope_ref, mine_ref, other_ref, *rest):
        w_refs, rest = rest[:nref], rest[nref:]
        gh_ref, keep_ref, send_ref, sum_ref, w_buf, mine, other, sems = rest
        j = pl.program_id(0)

        def copies(s):
            return weight.piece(idx, w_refs, w_buf, sems, s, s * block, 0, width)

        @pl.when(j == 0)
        def _():
            for s in range(steps):
                for c in copies(s):
                    c.start()
            walk_rows(idx, (mine_ref, other_ref), (mine, other), n)

        for s in range(steps):

            @pl.when(j == s)
            def _():
                for c in copies(s):
                    c.wait()

        b = w_buf[pl.ds(pl.multiple_of(j * block, block), block), :]
        gh = (mm(g_ref[...], b, NT) * slope_ref[...].astype(F32)).astype(BF16)
        gh_ref[...] = gh
        sum_ref[...] = jnp.sum(gh.astype(F32), axis=0, keepdims=True)
        send_ref[...] = mm(other[...], gh).astype(BF16)
        keep_ref[...] = mm(mine[...], gh).astype(BF16)

    out = pl.BlockSpec((half, block), lambda j, idx: (0, idx[j]))
    return kernel_call(
        body,
        idx,
        (steps,),
        [
            pl.BlockSpec((tokens, width), lambda j, idx: (0, 0)),
            pl.BlockSpec((tokens, block), lambda j, idx: (0, idx[j])),
            *half_specs(half, tokens, n),
            *weight.specs(),
        ],
        [
            pl.BlockSpec((tokens, block), lambda j, idx: (0, idx[j])),
            out,
            out,
            pl.BlockSpec((1, block), lambda j, idx: (0, idx[j])),
        ],
        [
            jax.ShapeDtypeStruct((tokens, inner), BF16),
            jax.ShapeDtypeStruct((half, inner), BF16),
            jax.ShapeDtypeStruct((half, inner), BF16),
            jax.ShapeDtypeStruct((1, inner), F32),
        ],
        [
            pltpu.VMEM((inner, width), BF16),
            pltpu.VMEM((half, tokens), BF16),
            pltpu.VMEM((half, tokens), BF16),
            pltpu.SemaphoreType.DMA((nref,)),
        ],
        [grad_ffn, slope, norm_t, norm_t, *weight.operands()],
        8 * tokens * width * inner,
        2 * (tokens * (width + 2 * inner) + 2 * width * inner),
    )


def middle_back(idx, grad_hidden, middle, cot, attention, keep, mod, up, project):
    tokens, inner = grad_hidden.shape
    width = middle.shape[1]
    rows = WINDOW
    n_up, n_pr = up.n_sems(), project.n_sems()

    def body(idx, gh_ref, mid_ref, cot_ref, att_ref, keep_ref, mod_ref, *rest):
        up_refs, rest = rest[:n_up], rest[n_up:]
        pr_refs, rest = rest[:n_pr], rest[n_pr:]
        gm_ref, ga_ref, gx_ref, sum_ref, up_buf, pr_buf, acc, up_sems, pr_sems = rest

        @pl.when(pl.program_id(0) == 0)
        def _():
            first = up.whole(idx, up_refs, up_buf, up_sems)
            second = project.whole(idx, pr_refs, pr_buf, pr_sems)
            for c in first + second:
                c.start()
            sum_ref[...] = jnp.zeros_like(sum_ref)
            for c in first + second:
                c.wait()

        acc[...] = mm(gh_ref[...], up_buf[...], NT)

        def chunk(i, sums):
            r = pl.ds(pl.multiple_of(i * CHUNK, CHUNK), CHUNK)
            grad = acc[r, :]
            normed, inverse = norm_rows(mid_ref[r, :])
            whole = cot_ref[r, :].astype(F32) + norm_back(
                grad * (1.0 + mod_ref[4:5, :]), normed, inverse
            )
            gm_ref[r, :] = whole
            gated = keep_ref[r, :] * whole
            ga = (gated * mod_ref[2:3, :]).astype(BF16)
            ga_ref[r, :] = ga
            terms = (grad, grad * normed, gated * att_ref[r, :].astype(F32), ga.astype(F32))
            return tuple(
                s + jnp.sum(t.reshape(CHUNK // 8, 8, width), axis=0)
                for s, t in zip(sums, terms)
            )

        zero = jnp.zeros((8, width), F32)
        sums = lax.fori_loop(0, rows // CHUNK, chunk, (zero,) * 4)
        for i, s in enumerate(sums):
            sum_ref[i : i + 1, :] += jnp.sum(s, axis=0, keepdims=True)
        gx_ref[...] = mm(ga_ref[...], pr_buf[...], NT).astype(BF16)

    block = pl.BlockSpec((rows, width), lambda w, idx: (w, 0))
    return kernel_call(
        body,
        idx,
        (tokens // rows,),
        [
            pl.BlockSpec((rows, inner), lambda w, idx: (w, 0)),
            block,
            block,
            block,
            pl.BlockSpec((rows, 1), lambda w, idx: (w, 0)),
            pl.BlockSpec((6, width), lambda w, idx: (0, 0)),
            *up.specs(),
            *project.specs(),
        ],
        [block, block, block, pl.BlockSpec((4, width), lambda w, idx: (0, 0))],
        [
            jax.ShapeDtypeStruct((tokens, width), F32),
            jax.ShapeDtypeStruct((tokens, width), BF16),
            jax.ShapeDtypeStruct((tokens, width), BF16),
            jax.ShapeDtypeStruct((4, width), F32),
        ],
        [
            pltpu.VMEM((width, inner), BF16),
            pltpu.VMEM((width, width), BF16),
            pltpu.VMEM((rows, width), F32),
            pltpu.SemaphoreType.DMA((n_up,)),
            pltpu.SemaphoreType.DMA((n_pr,)),
        ],
        [grad_hidden, middle, cot, attention, keep, mod, *up.operands(), *project.operands()],
        2 * tokens * width * (inner + width),
        2 * (tokens * (inner + 8 * width) + width * (inner + width)),
    )


def input_back(idx, grads, x, grad_middle, mod, weight):
    tokens, width = x.shape
    rows = WINDOW
    nref = weight.n_sems()

    def body(idx, dq_ref, dk_ref, dv_ref, x_ref, gm_ref, mod_ref, *rest):
        w_refs, rest = rest[:nref], rest[nref:]
        out_ref, sum_ref, w_buf, acc, sems = rest

        @pl.when(pl.program_id(0) == 0)
        def _():
            copies = weight.whole(idx, w_refs, w_buf, sems)
            for c in copies:
                c.start()
            sum_ref[...] = jnp.zeros_like(sum_ref)
            for c in copies:
                c.wait()

        acc[...] = (
            mm(dq_ref[...], w_buf[:, 0:width], NT)
            + mm(dk_ref[...], w_buf[:, width : 2 * width], NT)
            + mm(dv_ref[...], w_buf[:, 2 * width : 3 * width], NT)
        )

        def chunk(i, sums):
            r = pl.ds(pl.multiple_of(i * CHUNK, CHUNK), CHUNK)
            grad = acc[r, :]
            normed, inverse = norm_rows(x_ref[r, :].astype(F32))
            back = norm_back(grad * (1.0 + mod_ref[1:2, :]), normed, inverse)
            out_ref[r, :] = (gm_ref[r, :] + back).astype(BF16)
            return tuple(
                s + jnp.sum(t.reshape(CHUNK // 8, 8, width), axis=0)
                for s, t in zip(sums, (grad, grad * normed))
            )

        zero = jnp.zeros((8, width), F32)
        sums = lax.fori_loop(0, rows // CHUNK, chunk, (zero,) * 2)
        for i, s in enumerate(sums):
            sum_ref[i : i + 1, :] += jnp.sum(s, axis=0, keepdims=True)

    block = pl.BlockSpec((rows, width), lambda w, idx: (w, 0))
    return kernel_call(
        body,
        idx,
        (tokens // rows,),
        [
            *([block] * 5),
            pl.BlockSpec((6, width), lambda w, idx: (0, 0)),
            *weight.specs(),
        ],
        [block, pl.BlockSpec((2, width), lambda w, idx: (0, 0))],
        [jax.ShapeDtypeStruct((tokens, width), BF16), jax.ShapeDtypeStruct((2, width), F32)],
        [
            pltpu.VMEM((width, 3 * width), BF16),
            pltpu.VMEM((rows, width), F32),
            pltpu.SemaphoreType.DMA((nref,)),
        ],
        [*grads, x, grad_middle, mod, *weight.operands()],
        6 * tokens * width * width,
        2 * (tokens * 9 * width + 3 * width * width),
    )


def last_outer(idx, norm_t, mixed_t, grads, grad_attention, block, other):
    _, half, tokens = norm_t.shape
    width = grad_attention.shape[1]
    per = width // block
    n = idx.shape[0] - 1

    def body(idx, *refs):
        ins, rest = refs[:6], refs[6:]
        out_ref, mine = rest[0], rest[-1]
        j = pl.program_id(0)

        @pl.when(j == 0)
        def _():
            walk_rows(idx, ins[0:1], (mine,), n)

        @pl.when(j == 3 * per)
        def _():
            walk_rows(idx, ins[1:2], (mine,), n)

        for part, ref in enumerate(ins[2:]):

            @pl.when(j // per == part)
            def _():
                b = ref[...]
                out_ref[...] = mm(mine[...], b).astype(BF16)
                if other:
                    rest[1][...] = jnp.sum(b.astype(F32), axis=0, keepdims=True)

    def part_spec(part):
        return pl.BlockSpec(
            (tokens, block), lambda j, idx: (0, jnp.clip(j - part * per, 0, per - 1))
        )

    left = half_specs(half, tokens, n)[1 if other else 0]
    out_specs = [pl.BlockSpec((half, block), lambda j, idx: (0, j))]
    out_shape = [jax.ShapeDtypeStruct((half, 4 * width), BF16)]
    if other:
        out_specs.append(pl.BlockSpec((1, block), lambda j, idx: (0, j)))
        out_shape.append(jax.ShapeDtypeStruct((1, 4 * width), F32))
    return kernel_call(
        body,
        idx,
        (4 * per,),
        [left, left, *(part_spec(p) for p in range(4))],
        out_specs,
        out_shape,
        [pltpu.VMEM((half, tokens), BF16)],
        [norm_t, mixed_t, *grads, grad_attention],
        8 * tokens * half * width,
        2 * (2 * half * tokens + 4 * tokens * width + 4 * half * width),
    )


def join_halves(idx, own, other, widths, turn=False):
    n = idx.shape[0] - 1
    half, cols = own.shape
    shapes = [(cols, CORES * half)] if turn else [(CORES * half, w) for w in widths]

    def body(idx, own_ref, other_ref, *outs):
        core = idx[n]
        for ref, place in ((own_ref, core), (other_ref, 1 - core)):
            at = pl.ds(pl.multiple_of(place * half, half), half)
            if turn:
                outs[0][:, at] = ref[...].astype(F32).T
            else:
                start = 0
                for out, w in zip(outs, widths):
                    out[at, :] = ref[:, start : start + w].astype(F32)
                    start += w

    whole = lambda shape: pl.BlockSpec(shape, lambda i, idx: (0, 0))
    return kernel_call(
        body,
        idx,
        (1,),
        [whole(own.shape), whole(own.shape)],
        [whole(shape) for shape in shapes],
        [jax.ShapeDtypeStruct(shape, F32) for shape in shapes],
        [],
        [own, other],
        3e10,
        8 * half * cols,
    )


def turn_half(idx, piece, own, before=None):
    n = idx.shape[0] - 1
    half, cols = piece.shape
    kept = [before] if before is not None else []

    def body(idx, ref, *rest):
        rest[-1][...] = ref[...].astype(F32).T

    return kernel_call(
        body,
        idx,
        (1,),
        [pl.BlockSpec((half, cols), lambda i, idx: (0, 0)), *[any_spec()] * len(kept)],
        [pl.BlockSpec((cols, half), lambda i, idx: (0, idx[n] if own else 1 - idx[n]))],
        [jax.ShapeDtypeStruct((cols, CORES * half), F32)],
        [],
        [piece, *kept],
        3e10,
        6 * half * cols,
        {2: 0} if kept else None,
    )[0]


def column_pick():
    pick = np.zeros((SPAN, SPAN, WIN_S, LANES // WIN_S, WIN_S), np.float32)
    for b in range(SPAN):
        for key in range(WIN_S):
            for query in range(WIN_S):
                pick[b, query - key + WIN_S - 1, key, b, query] = 1.0
    return jnp.asarray(pick.reshape(SPAN * SPAN, WIN_S * LANES))


def spread_table(table):
    heads = table.shape[0]
    wide = jnp.dot(
        table.reshape(heads * TSPAN, SPAN * SPAN), column_pick(), precision=lax.Precision.HIGHEST
    )
    wide = wide.reshape(heads, TSPAN, WIN_S, LANES).transpose(0, 2, 1, 3)
    return wide.reshape(heads, WIN_S, TSPAN * LANES)


def gather_table(grad):
    heads = grad.shape[0]
    wide = grad.reshape(heads, WIN_S, TSPAN, LANES).transpose(0, 2, 1, 3)
    wide = wide.reshape(heads * TSPAN, WIN_S * LANES)
    table = lax.dot_general(wide, column_pick(), NT, precision=lax.Precision.HIGHEST)
    return table.reshape(heads, TSPAN * SPAN * SPAN)


def window_rows(grid, groups):
    clips_here, frames, halves, rows, side, width = grid.shape
    periods = frames // WIN_T
    cells = grid.reshape(clips_here, periods, WIN_T, halves, rows, halves, WIN_S, width)
    cells = cells.transpose(0, 1, 3, 5, 2, 4, 6, 7)
    return cells.reshape(groups, -1, WIN_T, rows, WIN_S, width)


def window_back(pieces, shape):
    clips_here, frames, halves, rows, side, width = shape
    periods = frames // WIN_T
    cells = pieces.reshape(clips_here, periods, halves, halves, WIN_T, rows, WIN_S, width)
    return cells.transpose(0, 1, 4, 2, 5, 3, 6, 7).reshape(shape)


def to_windows(grid, groups):
    got = lax.all_to_all(
        window_rows(grid, groups), "win", split_axis=0, concat_axis=3, tiled=True
    )
    return got.reshape(-1, grid.shape[-1])


def from_windows(rows, per_dev, shape):
    out = lax.all_to_all(
        rows.reshape(1, per_dev, WIN_T, WIN_S, WIN_S, shape[-1]),
        "win",
        split_axis=3,
        concat_axis=0,
        tiled=True,
    )
    return window_back(out, shape)


def from_windows_apart(rows, per_dev, shape):
    groups = lax.axis_size("win")
    me = lax.axis_index("win")
    cells = rows.reshape(per_dev, WIN_T, groups, WIN_S // groups, WIN_S, shape[-1])
    out = jnp.zeros((groups, *cells.shape[:2], *cells.shape[3:]), rows.dtype)
    for k in range(groups):
        piece = lax.dynamic_index_in_dim(cells, me ^ k, 2, keepdims=False)
        if k:
            piece = lax.ppermute(piece, "win", [(w, w ^ k) for w in range(groups)])
        out = lax.dynamic_update_slice_in_dim(out, piece[None], me ^ k, 0)
    return window_back(out, shape)


def body(
    tokens,
    condition,
    frame_count,
    triple_weight,
    triple_bias,
    project_weight,
    project_bias,
    up_weight,
    up_bias,
    down_weight,
    down_bias,
    modulate_weight,
    modulate_bias,
    position_table,
    cotangent,
):
    width = tokens.shape[-1]
    n = lax.axis_size("clip")
    groups = lax.axis_size("win")
    halves = tokens.shape[2]
    per_time = tokens.shape[1] // WIN_T
    per_dev = per_time * halves * halves // groups
    count = per_dev * WINDOW
    ring = Ring(n)
    core = ring.core
    rows = width // n

    def half_of(shard):
        size = shard.shape[0] // CORES
        return lax.dynamic_slice_in_dim(shard, core * size, size, 0)

    def turned(v):
        v = v.reshape(count, n, CORES, rows // CORES).transpose(2, 1, 3, 0)
        return v.reshape(CORES, width // CORES, count)

    flat = lambda v: v.reshape(1, -1).astype(F32)
    split_rows = lambda g: g.reshape(n, rows // CORES, -1)
    swap = lambda g: lax.ppermute(g, "win", ring.swap)
    idx = ring.index
    steps = max(ring.steps(False))
    spare = lambda group, used: [group.step() for _ in range(used, steps)]

    first = jnp.concatenate([half_of(triple_weight), half_of(project_weight)], axis=1)
    group_a = Gather(ring, first, False)
    group_b = Gather(ring, half_of(up_weight), True)
    group_c = Gather(ring, half_of(down_weight), False)

    sigma = jax.nn.sigmoid(condition)
    group_a.step()
    tokens_here, condition_here = after((tokens, condition), first)
    vectors = [triple_bias, project_bias, up_bias, down_bias, modulate_bias]
    packed, ends = pack_rows(condition_here, vectors)
    small = ring.gather_small(packed.astype(BF16))
    x = to_windows(tokens_here, groups)
    cond_all, triple_b, project_b, up_b, down_b, modulate_b = (
        small[:, ends[i] : ends[i + 1]].reshape(n, -1)[:, : v.size]
        for i, v in enumerate([condition, *vectors])
    )
    triple_b, project_b, up_b, down_b = map(flat, (triple_b, project_b, up_b, down_b))
    bias_all = jnp.concatenate(
        [triple_b[:, :width], jnp.zeros((1, width), F32), triple_b[:, width:]], axis=1
    )
    cond_rows = lax.dynamic_slice_in_dim(cond_all, ring.rank * rows, rows, 1)
    mod = ring.scatter_small(mm(cond_rows, modulate_weight)) + modulate_b.reshape(-1).astype(F32)
    table = spread_table(position_table)
    mod = mod.reshape(6, width)
    stage([group_a])
    group_a.step()
    mod, table = stage([group_a], mod, table)

    window_id = lax.axis_index("win") * per_dev + jnp.arange(per_dev)
    start = window_id // (halves * halves) * WIN_T
    valid = jnp.clip(frame_count[0] - start, 0, WIN_T).astype(jnp.int32)
    keep = (jnp.arange(WINDOW)[None] // CELL < valid[:, None]).astype(F32).reshape(count, 1)
    group_a.step()
    x, bias_all = stage([group_a], x, bias_all)
    spare(group_a, 3)
    stage([group_a])
    triple_w = Weight(triple_weight, *group_a.pieces())
    project_w = Weight(project_weight, triple_w.own, triple_w.sib, 3 * width)

    (group_b.a, group_b.b), idx, valid = together(
        after((group_b.a, group_b.b), (group_a.a, group_a.b)), idx, valid
    )
    group_b.step()
    norm_in, triple, cotangent = stage(
        [group_b], *qkv_project(idx, x, mod, triple_w, bias_all), cotangent
    )
    group_b.step()
    cot = to_windows(cotangent, groups)
    half_mixed = attend(valid, triple, table, 0, 2)
    half_mixed = stage([group_b], *half_mixed)
    group_b.step()
    gate_two = mod[5:6]
    grad_ffn = (keep * cot.astype(F32) * gate_two).astype(BF16)
    mixed, logs = attend(valid, triple, table, 1, 2, half_mixed)
    mixed, logs, grad_ffn = stage([group_b], mixed, logs, grad_ffn)
    spare(group_b, 3)
    ffn_t = grad_ffn.T.reshape(CORES, width // CORES, count)
    attention, middle, norm_mid, ffn_t = stage(
        [group_b],
        *attention_out(idx, mixed, x, mod, keep, project_w, project_b),
        ffn_t,
    )
    up_w = Weight(up_weight, *group_b.pieces())

    group_c.a, group_c.b = after((group_c.a, group_c.b), (group_b.a, group_b.b))
    group_c.step()
    half_act = stage([group_c], *gelu_up(idx, norm_mid, up_w, up_b, 0, 2))
    group_c.step()
    activated, slope = stage([group_c], *gelu_up(idx, norm_mid, up_w, up_b, 1, 2, half_act))
    group_c.step()
    down_keep, down_send, norm_in, mixed, mid_rows = stage(
        [group_c], *down_outer(idx, ffn_t, activated), norm_in, mixed, norm_mid
    )
    down_got = swap(down_send)
    spare(group_c, 3)
    norm_t, mixed_t, mid_t = turned(norm_in), turned(mixed), turned(mid_rows)
    down_got, norm_t, mixed_t, mid_t = stage([group_c], down_got, norm_t, mixed_t, mid_t)
    down_w = Weight(down_weight, *group_c.pieces())

    sums_d = Scatter(ring, down_keep, down_got, False)
    grad_ffn, idx = stage([sums_d], after((grad_ffn, idx), (group_c.a, group_c.b)))[0]
    sums_d.step()
    down_bias_grad = jnp.sum(grad_ffn.astype(F32), axis=0)
    (grad_hidden, up_keep, up_send, up_bias_grad), idx = stage(
        [sums_d], hidden_back(idx, grad_ffn, slope, mid_t, down_w), idx
    )
    sums_u = Scatter(ring, split_rows(up_keep), swap(split_rows(up_send)), True)
    sums_d.step()
    (grad_middle, grad_attention, grad_mixed, mid_sums), idx, valid = stage(
        [sums_d, sums_u],
        middle_back(
            idx, grad_hidden, middle, cot, attention, keep, mod, up_w, project_w
        ),
        idx,
        valid,
    )
    grad_shift_two, grad_scale_two, grad_gate_one, project_bias_grad = mid_sums
    sums_d.step()
    sums_u.step()
    (*grads, grad_table), idx = stage(
        [sums_d, sums_u], attend_back(valid, triple, table, grad_mixed, logs), idx
    )
    for _ in range(3, steps):
        (idx,) = sums_d.step(idx)
    (idx,) = sums_u.step(idx)
    last = (norm_t, mixed_t, grads, grad_attention, 1024)
    (last_send, last_sums), idx = together(last_outer(idx, *last, True), idx)
    last_got = swap(split_rows(last_send))
    table_grad = gather_table(grad_table)
    last_keep, last_got, idx, table_grad = stage(
        [], last_outer(idx, *last, False)[0], last_got, idx, table_grad
    )
    inner = activated.shape[-1]
    sums_l = Scatter(ring, split_rows(last_keep), last_got, False)
    (idx,) = sums_l.step(idx)
    (idx,) = sums_u.step(idx)
    (result, grad_gate_two), idx, down_sum = stage(
        [sums_u, sums_l],
        ffn_down(idx, activated, middle, cot, keep, gate_two, down_w, down_b),
        idx,
        sums_d.start_finish(),
    )
    idx, down_sum, result = sums_l.step(idx, down_sum, result)
    for _ in range(3, steps):
        (idx,) = sums_u.step(idx)
    output = from_windows(result, per_dev, tokens.shape)
    (grad_rows, in_sums), output, down_parts = stage(
        [sums_l, sums_u],
        input_back(idx, grads, x, grad_middle, mod, triple_w),
        output,
        sums_d.finish(down_sum),
    )

    rows_of = lambda v: v.reshape(-1, LANES)
    grad_mod = jnp.concatenate(
        [in_sums, grad_gate_one[None], mid_sums[0:2], grad_gate_two], axis=0
    )
    here = jnp.arange(n)[:, None, None] == ring.rank
    spans = position_table.shape[1]
    wide = -(-spans // LANES) * LANES
    pieces = [
        rows_of(jnp.pad(table_grad, ((0, 0), (0, wide - spans)))),
        rows_of(last_sums[0, :width]),
        rows_of(last_sums[0, 2 * width : 3 * width]),
        rows_of(project_bias_grad),
        rows_of(up_bias_grad[0]),
        rows_of(down_bias_grad),
        jnp.where(here, rows_of(grad_mod)[None], 0.0).reshape(-1, LANES),
    ]
    ends = np.cumsum([0] + [p.shape[0] for p in pieces])
    pad = -int(ends[-1]) % (n * groups * 8)
    packed = jnp.concatenate(pieces + [jnp.zeros((pad, LANES), F32)])
    packed, idx = sums_l.step(packed, idx)
    packed, down_half, idx, down_other, input_grad = stage(
        [sums_l],
        ring.sum_part(packed),
        turn_half(idx, down_parts[0], True),
        idx,
        down_parts[1],
        from_windows_apart(grad_rows, per_dev, tokens.shape),
    )
    for _ in range(3, steps):
        packed, idx, sums_u.a, sums_u.b = sums_l.step(packed, idx, sums_u.a, sums_u.b)
    packed, down_weight_grad, up_sum, idx = stage(
        [sums_l],
        ring.share_parts(packed),
        turn_half(idx, down_other, False, down_half),
        sums_u.start_finish(),
        idx,
    )
    last_sum = sums_l.start_finish()
    (up_weight_grad,) = join_halves(idx, *sums_u.finish(up_sum), [inner])
    table_grad, *bias_grads, grad_mod = (packed[ends[i] : ends[i + 1]] for i in range(len(pieces)))
    table_grad = table_grad.reshape(-1, wide)[:, :spans]
    bias_grads = [jnp.concatenate(bias_grads[:2]), *bias_grads[2:]]
    bias_grads = [
        lax.dynamic_slice_in_dim(g.reshape(-1), ring.rank * (g.size // n), g.size // n)
        for g in bias_grads
    ]
    grad_mod = grad_mod.reshape(n, -1).astype(BF16)
    modulate_weight_grad = mm(cond_rows, grad_mod, TN)
    modulate_bias_grad = lax.dynamic_slice_in_dim(
        jnp.sum(grad_mod.astype(F32), axis=0), ring.rank * (6 * rows), 6 * rows
    )
    back = lax.all_to_all(mm(grad_mod, modulate_weight, NT), "clip", 0, 0, tiled=True)
    condition_grad = back.reshape(1, width) * (sigma * (1.0 + condition * (1.0 - sigma)))
    last_sum, condition_grad, up_weight_grad, table_grad, bias_grads = together(
        last_sum, condition_grad, up_weight_grad, table_grad, bias_grads
    )
    triple_weight_grad, project_weight_grad = join_halves(
        idx, *sums_l.finish(last_sum), [3 * width, width]
    )
    triple_bias_grad, project_bias_grad, up_bias_grad, down_bias_grad = bias_grads
    return (
        output,
        input_grad,
        condition_grad,
        triple_weight_grad,
        triple_bias_grad,
        project_weight_grad,
        project_bias_grad,
        up_weight_grad,
        up_bias_grad,
        down_weight_grad,
        down_bias_grad,
        modulate_weight_grad,
        modulate_bias_grad,
        table_grad,
    )


def solution(mesh):
    grid = P("clip", None, None, "win", None, None)
    matrix, vector = P("clip", None), P("clip")
    placed = (
        grid,
        matrix,
        vector,
        matrix,
        vector,
        matrix,
        vector,
        matrix,
        vector,
        matrix,
        vector,
        matrix,
        vector,
        P(),
        grid,
    )
    return jax.shard_map(
        body,
        mesh=mesh,
        in_specs=placed,
        out_specs=(grid, grid, *placed[1:2], *placed[3:14]),
        check_vma=False,
    )
```
